32 devices in a mesh: load: 2 (over core), brick: 16 (over z, y, x).
Axes of the slice: x: 2, y: 2, z: 4, core: 2. Of those that a mesh axis runs over, the one named last changes fastest.
Arguments:
- density: float32 [192, 64, 128], P('brick'), may hold values from 0.1 to 0.95
- passive: int32 [192, 64, 128], P('brick'), may hold values from 0 to 2, as said below
- support: int32 [192, 64, 128], P('brick'), may hold values 0 or 1
- load_nodes: int32 [4, 64], P('load'), may hold values from 0 to 1572863
- load_force: float32 [4, 64], P('load'), may hold values from -6 to 6
- self_weight: float32 [4], P('load'), may hold values from 0.3 to 3
- body_force: float32 [4, 192, 64, 128], P('load', 'brick'), may hold values from -3 to 3
Outputs:
- new_density: float32 [192, 64, 128], P('brick', 'load')
- momentum: float32 [192, 64, 128], P('brick', 'load')
- displacement: float32 [4, 192, 64, 128], P('load', 'brick')
The draws below stay inside these ranges and needn't reach their ends.
Inputs may be any that keep to these rules, and one draw needn't show every extreme that they name: 0 marks a design voxel, 1 a passive void voxel, 2 a passive solid voxel.
All inputs are finite; a program needn't handle non-finite values. No bound on the sum of `support` on one device may be relied on, other than what follows from the above.
Results may differ from the reference program's by a relative error of at most 0.0001.
Values sent between devices are 32-bit elements; how exact they have to be, the bound alone decides.
No kernel may reach another device: no remote copies, remote signals or barrier semaphores. Data moves between devices by JAX's collectives and lax.ppermute only.
A program may use at most 64 MiB of HBM per device.

```python
import math
import jax
import jax.numpy as jnp
from jax import lax

NY = 64
NZ = 128
POINTS = 64
SWEEPS = 5
DESIGN_ITERS = 2
NX = 192
LOADS = 4


def draw_passive(key, part):
    picked = jax.random.randint(key, (NX, NY, NZ), 0, 16)
    return jnp.where(picked == 0, 1, jnp.where(picked == 1, 2, 0)).astype(jnp.int32)


def touch_ends(result, key, smallest, largest):
    longest = result.shape.index(max(result.shape))
    spots = []
    for shift in (0, 1):
        where = [jax.random.randint(jax.random.fold_in(key, axis), (), 0, length) for axis, length in enumerate(result.shape)]
        where[longest] = (where[longest] + shift) % result.shape[longest]
        spots.append(tuple(where))
    return result.at[spots[0]].set(smallest).at[spots[1]].set(largest)


def steps_of(stream_key, extent, split, least, high):
    factor_of = 1.0
    for position, shards_of in split:
        draws = jax.random.uniform(jax.random.fold_in(jax.random.fold_in(stream_key, 6), position), (shards_of,), jnp.float32, least / len(split), high / len(split))
        factor_of = factor_of * jnp.repeat(jnp.exp(draws), extent[position] // shards_of).reshape((-1,) + (1,) * (len(extent) - 1 - position))
    return factor_of


def noise(stream_key, extent, spread, limit, split=(), dtype=jnp.bfloat16):
    factor_of = steps_of(stream_key, extent, split, -0.22, 0.18) if split else 1.0
    result = jax.random.normal(stream_key, extent, jnp.float32) * spread * factor_of
    return jnp.minimum(jnp.maximum(result, -limit), limit).astype(dtype)


def setup_inputs(seed: int = 0) -> dict:
    keys = jax.random.split(jax.random.key(seed), 8)
    density = jnp.clip(0.1 + 0.84999999 * jax.random.uniform(keys[0], (NX, NY, NZ), jnp.float32) ** steps_of(keys[0], (NX, NY, NZ), ((0, 16),), -0.2, 0.2), 0.1, 0.95)
    passive = draw_passive(jax.random.fold_in(keys[7], 71), 0)
    support = touch_ends((jax.random.randint(keys[2], (NX, NY, NZ), 0, 8) < 1).astype(jnp.int32), jax.random.fold_in(keys[2], 1), 0, 1)
    load_nodes = touch_ends(jax.random.randint(keys[3], (LOADS, POINTS), 0, NX * NY * NZ), jax.random.fold_in(keys[3], 1), 0, (NX * NY * NZ) - 1).astype(jnp.int32)
    load_force = noise(keys[4], (LOADS, POINTS), 1.0, 6.0, ((0, 2),), jnp.float32)
    self_weight = jnp.clip(jnp.exp(math.log(3.0) - 2.3025851 * jax.random.uniform(keys[5], (LOADS,), jnp.float32) ** steps_of(keys[5], (LOADS,), ((0, 2),), -0.2, 0.2)), 0.3, 3.0)
    body_force = noise(keys[6], (LOADS, NX, NY, NZ), 0.5, 3.0, ((0, 2), (1, 16)), jnp.float32)
    return {"density": density, "passive": passive, "support": support, "load_nodes": load_nodes, "load_force": load_force, "self_weight": self_weight, "body_force": body_force}


stiff_floor = 0.01
mass_shift = 0.1
spectrum_low = 0.05
spectrum_high = 2.0
moment_decay = 0.8
step_size = 0.1
volume_pull = 0.5
volume_target = 0.4
density_floor = 0.001


def neighbours(padded):
    return (padded[..., 2:, 1:-1, 1:-1], padded[..., :-2, 1:-1, 1:-1],
            padded[..., 1:-1, 2:, 1:-1], padded[..., 1:-1, :-2, 1:-1],
            padded[..., 1:-1, 1:-1, 2:], padded[..., 1:-1, 1:-1, :-2])


def pad_all(vector):
    return jnp.pad(vector, 1)


def passive_apply(design, passive):
    return jnp.where(passive == 1, density_floor, jnp.where(passive == 2, 1.0, design)).astype(jnp.float32)


def operate(vector, free_mask, stiffness, face_list, padded_free):
    freed = padded_free[..., 1:-1, 1:-1, 1:-1]
    accumulated = mass_shift * stiffness * freed
    for face_weight, beside in zip(face_list, neighbours(padded_free)):
        accumulated = accumulated + face_weight * (freed - beside)
    return free_mask * accumulated + (1.0 - free_mask) * vector


def chebyshev(source, free_mask, stiffness, face_list, diagonal, pad_fn):
    centre = 0.5 * (spectrum_high + spectrum_low)
    half_width = 0.5 * (spectrum_high - spectrum_low)
    ratio_one = centre / half_width
    previous = 1.0 / ratio_one
    solution = jnp.zeros_like(source)
    residual = source
    direction = residual / diagonal / centre
    for sweep_index in range(SWEEPS):
        solution = solution + direction
        if sweep_index < SWEEPS - 1:
            applied = operate(direction, free_mask, stiffness, face_list, pad_fn(free_mask * direction))
            residual = residual - applied
            current = 1.0 / (2.0 * ratio_one - previous)
            direction = (current * previous) * direction + (2.0 * current / half_width) * (residual / diagonal)
            previous = current
    return solution


def load_energy(freed, padded):
    energy = mass_shift * freed * freed
    for beside in neighbours(padded):
        energy = energy + 0.25 * (freed - beside) ** 2
    return energy


def inside_count(start_x, start_y, grid_shape, total_shape):
    along_x = start_x + lax.broadcasted_iota(jnp.int32, grid_shape, 0)
    along_y = start_y + lax.broadcasted_iota(jnp.int32, grid_shape, 1)
    along_z = lax.broadcasted_iota(jnp.int32, grid_shape, 2)
    edges = ((along_x == 0).astype(jnp.float32) + (along_x == total_shape[0] - 1).astype(jnp.float32)
             + (along_y == 0).astype(jnp.float32) + (along_y == total_shape[1] - 1).astype(jnp.float32)
             + (along_z == 0).astype(jnp.float32) + (along_z == total_shape[2] - 1).astype(jnp.float32))
    return 6.0 - edges


def filter_field(sensitivity, padded, neighbour_count):
    accumulated = 2.0 * sensitivity
    for beside in neighbours(padded):
        accumulated = accumulated + beside
    return accumulated / (2.0 + neighbour_count)


def design_step(design, momentum, passive, abs_total, density_total, total_cells):
    mean_step = abs_total / total_cells + 1e-6
    mean_density = density_total / total_cells
    moved = design - step_size * momentum / mean_step - volume_pull * (mean_density - volume_target)
    return passive_apply(jnp.clip(moved, density_floor, 1.0), passive)


def reference(density, passive, support, load_nodes, load_force, self_weight, body_force):
    free_mask = (1 - support).astype(jnp.float32)
    design = passive_apply(density, passive)
    momentum = jnp.zeros_like(design)
    total_cells = NX * NY * NZ
    neighbour_count = inside_count(0, 0, (NX, NY, NZ), (NX, NY, NZ))
    displacement = None
    for iteration in range(DESIGN_ITERS):
        stiffness = stiff_floor + (1.0 - stiff_floor) * design ** 3
        face_list = tuple(0.5 * (stiffness + beside) for beside in neighbours(pad_all(stiffness)))
        face_total = face_list[0]
        for face_weight in face_list[1:]:
            face_total = face_total + face_weight
        diagonal = free_mask * (face_total + mass_shift * stiffness) + (1.0 - free_mask)

        def one_load(carried, inputs):
            node_ids, forces, weight, spread_force = inputs
            points = jnp.zeros((NX * NY * NZ,), jnp.float32).at[node_ids].add(forces).reshape(NX, NY, NZ)
            source = free_mask * (points + weight * design + spread_force)
            solution = chebyshev(source, free_mask, stiffness, face_list, diagonal, pad_all)
            freed = free_mask * solution
            return carried + load_energy(freed, pad_all(freed)), solution

        energy, displacement = lax.scan(one_load, jnp.zeros((NX, NY, NZ), jnp.float32),
                                        (load_nodes, load_force, self_weight, body_force))
        sensitivity = -3.0 * (1.0 - stiff_floor) * design * design * energy
        filtered = filter_field(sensitivity, pad_all(sensitivity), neighbour_count)
        momentum = moment_decay * momentum + filtered
        design = design_step(design, momentum, passive, jnp.sum(jnp.abs(momentum)), jnp.sum(design), total_cells)
    return design, momentum, displacement
```

```python
import functools

import jax
import jax.numpy as jnp
from jax import lax
from jax.experimental import pallas as pl
from jax.experimental.pallas import tpu as pltpu
from jax.sharding import PartitionSpec as P

SWEEPS = 5

stiff_floor = 0.01
mass_shift = 0.1
spectrum_low = 0.05
spectrum_high = 2.0
moment_decay = 0.8
step_size = 0.1
volume_pull = 0.5
volume_target = 0.4
density_floor = 0.001

SOURCE = SWEEPS
DESIGN = SWEEPS + 1
SENSE = SWEEPS + 2


def chebyshev_factors():
    centre = 0.5 * (spectrum_high + spectrum_low)
    half_width = 0.5 * (spectrum_high - spectrum_low)
    ratio_one = centre / half_width
    previous = 1.0 / ratio_one
    factors = []
    for _ in range(SWEEPS - 1):
        current = 1.0 / (2.0 * ratio_one - previous)
        factors.append((current * previous, 2.0 * current / half_width))
        previous = current
    return 1.0 / centre, factors


def shifted(plane):
    size_y, size_z = plane.shape
    return (
        pltpu.roll(plane, 1, 0),
        pltpu.roll(plane, size_y - 1, 0),
        pltpu.roll(plane, 1, 1),
        pltpu.roll(plane, size_z - 1, 1),
    )


def inner_masks(shape):
    along_y = lax.broadcasted_iota(jnp.int32, shape, 0)
    along_z = lax.broadcasted_iota(jnp.int32, shape, 1)
    return (along_y > 0, along_y < shape[0] - 1, along_z > 0, along_z < shape[1] - 1)


def beside_planes(plane, masks):
    return tuple(jnp.where(mask, moved, 0.0) for mask, moved in zip(masks, shifted(plane)))


def edge_planes(masks):
    edges = sum((1.0 - mask.astype(jnp.float32)) for mask in masks)
    return 1.0 / (8.0 - edges), 1.0 / (7.0 - edges)


def stiffness_of(design):
    return stiff_floor + (1.0 - stiff_floor) * (design * design * design)


def weights_stage(rows, free_of, stiff, weight, inverse, masks):
    def one_row(q, carry):
        here, below, above = stiff[q + 1], stiff[q], stiff[q + 2]
        around = (below, above) + beside_planes(here, masks)
        total = around[0]
        for plane in around[1:]:
            total = total + plane
        diagonal = (3.0 + mass_shift) * here + 0.5 * total
        scale = jnp.where(free_of(q), 1.0 / diagonal, 0.0)
        inverse[q] = scale
        half = 0.5 * scale
        weight[0, q] = half * (here + below)
        weight[1, q] = half * (here + above)
        for j in range(4):
            weight[2 + j, q] = jnp.where(masks[j], half * (here + around[2 + j]), 0.0)
        return carry

    lax.fori_loop(0, rows, one_row, 0)


def sweep_stage(rows, loads, weight, resid, steps, shown):
    _, factors = chebyshev_factors()
    for k, (keep, gain) in enumerate(factors):
        last = k == len(factors) - 1

        def one_row(q, carry, k=k, keep=keep, gain=gain, last=last):
            faces = [weight[j, q] for j in range(6)]
            for l in range(loads):
                here = steps[k, l, q]
                total = faces[0] * steps[k, l, q - 1] + faces[1] * steps[k, l, q + 1]
                for face, moved in zip(faces[2:], shifted(here)):
                    total = total + face * moved
                left = resid[l, q] - here + total
                step = keep * here + gain * left
                if last:
                    for earlier in range(k + 1):
                        step = step + steps[earlier, l, q]
                    shown[l, q - (SWEEPS - 1)] = step
                else:
                    resid[l, q] = left
                    steps[k + 1, l, q] = step
            return carry

        lax.fori_loop(k + 1, rows - k - 1, one_row, 0)


def energy_stage(cells, loads, design_of, shown, sense, masks):
    def one_row(i, carry):
        energy = None
        for l in range(loads):
            here = shown[l, i + 1]
            around = (shown[l, i], shown[l, i + 2]) + beside_planes(here, masks)
            spread = None
            for plane in around:
                gap = here - plane
                spread = gap * gap if spread is None else spread + gap * gap
            part = mass_shift * (here * here) + 0.25 * spread
            energy = part if energy is None else energy + part
        design = design_of(i)
        sense[i] = (-3.0 * (1.0 - stiff_floor)) * (design * design) * energy
        return carry

    lax.fori_loop(0, cells, one_row, 0)


def fold(plane):
    return jnp.sum(plane.reshape(plane.shape[0] // 8, 8, plane.shape[1]), axis=0)


def filter_total(cells, sense, is_first, is_last, masks):
    inside, outer = edge_planes(masks)
    beside_inside = sum(beside_planes(inside, masks))
    beside_outer = sum(beside_planes(outer, masks))
    usual = 4.0 * inside + beside_inside
    at_end = 2.0 * outer + inside + beside_outer
    zero = jnp.zeros_like(inside)
    total = lax.fori_loop(0, cells, lambda i, acc: acc + sense[i], zero)
    ends = jnp.where(is_first, sense[0], zero) + jnp.where(is_last, sense[cells - 1], zero)
    nexts = jnp.where(is_first, sense[1], zero) + jnp.where(is_last, sense[cells - 2], zero)
    return -fold(total * usual + ends * (at_end - usual) + nexts * (outer - inside))


def first_kernel(cells, loads, place, self_weight, design_ref, free_ref, force_ref, force_lo, force_hi, points_ref,
                 pair_a, pair_b, sense_ref, tile_ref, design_wide, free_wide, base_wide,
                 stiff, weight, inverse, resid, steps, shown):
    even, is_first, is_last = place[0] == 1, place[1] == 1, place[2] == 1
    shape = design_ref.shape[1:]
    masks = inner_masks(shape)
    wide = cells + 2 * DESIGN
    rows = cells + 2 * SOURCE
    zero = jnp.zeros(shape, jnp.float32)

    for i in range(DESIGN):
        low = jnp.where(even, pair_a[i], pair_b[i])
        high = jnp.where(even, pair_b[i], pair_a[i])
        design_wide[i] = low
        design_wide[DESIGN + cells + i] = high
        stiff[i] = jnp.where(is_first, zero, stiffness_of(low))
        stiff[DESIGN + cells + i] = jnp.where(is_last, zero, stiffness_of(high))
    for i in range(SOURCE):
        low = jnp.where(even, pair_a[DESIGN + i], pair_b[DESIGN + i])
        high = jnp.where(even, pair_b[DESIGN + i], pair_a[DESIGN + i])
        free_wide[i] = jnp.where(is_first, zero, low)
        free_wide[SOURCE + cells + i] = jnp.where(is_last, zero, high)

    def own(i, carry):
        design = design_ref[i]
        design_wide[DESIGN + i] = design
        stiff[DESIGN + i] = stiffness_of(design)
        free_wide[SOURCE + i] = free_ref[i]
        return carry

    lax.fori_loop(0, cells, own, 0)

    weights_stage(rows, lambda q: free_wide[q] > 0.5, stiff, weight, inverse, masks)

    first_scale, _ = chebyshev_factors()
    for l in range(loads):
        for start, count, force in ((0, SOURCE, force_lo), (SOURCE, cells, force_ref), (SOURCE + cells, SOURCE, force_hi)):

            def one_row(i, carry, l=l, start=start, force=force):
                q = start + i
                base = points_ref[l, q] + force[l, i]
                base_wide[l, q] = base
                left = inverse[q] * (base + self_weight[l] * design_wide[q + 1])
                resid[l, q] = left
                steps[0, l, q] = first_scale * left
                return carry

            lax.fori_loop(0, count, one_row, 0)

    sweep_stage(rows, loads, weight, resid, steps, shown)
    energy_stage(cells, loads, lambda i: design_ref[i], shown, sense_ref, masks)
    tile_ref[0] = filter_total(cells, sense_ref, is_first, is_last, masks)
    tile_ref[1] = fold(lax.fori_loop(0, cells, lambda i, acc: acc + design_ref[i], zero))


def second_kernel(cells, loads, total_cells, share, place, self_weight, tile_in, sense_a, sense_b, pair_a, pair_b,
                  design_wide, free_wide, base_wide,
                  shown_ref, sense_ref, tile_ref, design_out, momentum_out,
                  sense_wide, stiff, weight, inverse, resid, steps, shown, design_new):
    even, is_first, is_last = place[0] == 1, place[1] == 1, place[2] == 1
    shape = sense_a.shape[1:]
    masks = inner_masks(shape)
    wide = cells + 2 * DESIGN
    rows = cells + 2 * SOURCE
    zero = jnp.zeros(shape, jnp.float32)
    for i in range(SENSE):
        low = jnp.where(even, pair_a[i], pair_b[i])
        high = jnp.where(even, pair_b[i], pair_a[i])
        sense_wide[i] = jnp.where(is_first, zero, low)
        sense_wide[SENSE + cells + i] = jnp.where(is_last, zero, high)

    def own(i, carry):
        sense_wide[SENSE + i] = sense_a[i] + sense_b[i]
        return carry

    lax.fori_loop(0, cells, own, 0)

    abs_total = jnp.sum(tile_in[0], keepdims=True)
    density_total = jnp.sum(tile_in[1], keepdims=True) * share
    mean_step = abs_total / total_cells + 1e-6
    pull = volume_pull * (density_total / total_cells - volume_target)
    rate = step_size / mean_step
    inside, outer = edge_planes(masks)

    def one_row(r, carry):
        here = sense_wide[r + 1]
        total = 2.0 * here + sense_wide[r] + sense_wide[r + 2]
        for plane in beside_planes(here, masks):
            total = total + plane
        at_end = (is_first & (r == DESIGN)) | (is_last & (r == DESIGN + cells - 1))
        momentum = total * jnp.where(at_end, outer, inside)
        before = design_wide[r]
        moved = jnp.clip(before - rate * momentum - pull, density_floor, 1.0)
        fixed = (before == density_floor) | (before == 1.0)
        design = jnp.where(fixed, before, moved)
        design_new[r] = design
        outside = (is_first & (r < DESIGN)) | (is_last & (r >= DESIGN + cells))
        stiff[r] = jnp.where(outside, zero, stiffness_of(design))

        @pl.when((r >= DESIGN) & (r < DESIGN + cells))
        def _():
            momentum_out[r - DESIGN] = momentum
            design_out[r - DESIGN] = design

        return carry

    lax.fori_loop(0, wide, one_row, 0)

    weights_stage(rows, lambda q: free_wide[q] > 0.5, stiff, weight, inverse, masks)
    first_scale, _ = chebyshev_factors()

    def start_row(q, carry):
        scale, design = inverse[q], design_new[q + 1]
        for l in range(loads):
            left = scale * (base_wide[l, q] + self_weight[l] * design)
            resid[l, q] = left
            steps[0, l, q] = first_scale * left
        return carry

    lax.fori_loop(0, rows, start_row, 0)
    sweep_stage(rows, loads, weight, resid, steps, shown)
    for l in range(loads):

        def copy_row(i, carry, l=l):
            shown_ref[l, i] = shown[l, i + 1]
            return carry

        lax.fori_loop(0, cells, copy_row, 0)
    energy_stage(cells, loads, lambda i: design_out[i], shown, sense_ref, masks)
    tile_ref[0] = filter_total(cells, sense_ref, is_first, is_last, masks)
    tile_ref[1] = fold(lax.fori_loop(0, cells, lambda i, acc: acc + design_out[i], zero))


def last_kernel(cells, slab, total_cells, share, place, tile_before, tile_in, sense_a, sense_b, row_lo, row_hi,
                momentum_in, design_in, passive_ref, design_ref, momentum_ref, sense_wide, design_all, momentum_all):
    is_first, is_last, start = place[1] == 1, place[2] == 1, place[3]
    shape = sense_a.shape[1:]
    masks = inner_masks(shape)
    zero = jnp.zeros(shape, jnp.float32)
    sense_wide[0] = jnp.where(is_first, zero, row_lo[0])
    sense_wide[cells + 1] = jnp.where(is_last, zero, row_hi[0])

    def own(i, carry):
        sense_wide[i + 1] = sense_a[i] + sense_b[i]
        return carry

    lax.fori_loop(0, cells, own, 0)
    abs_total = jnp.sum(moment_decay * tile_before[0] + tile_in[0], keepdims=True)
    density_total = jnp.sum(tile_in[1], keepdims=True) * share
    mean_step = abs_total / total_cells + 1e-6
    pull = volume_pull * (density_total / total_cells - volume_target)
    rate = step_size / mean_step
    inside, outer = edge_planes(masks)

    def one_row(i, carry):
        here = sense_wide[i + 1]
        total = 2.0 * here + sense_wide[i] + sense_wide[i + 2]
        for plane in beside_planes(here, masks):
            total = total + plane
        at_end = (is_first & (i == 0)) | (is_last & (i == cells - 1))
        momentum = moment_decay * momentum_in[i] + total * jnp.where(at_end, outer, inside)
        moved = jnp.clip(design_in[i] - rate * momentum - pull, density_floor, 1.0)
        kind = passive_ref[i]
        design_all[i] = jnp.where(kind == 1, density_floor, jnp.where(kind == 2, 1.0, moved))
        momentum_all[i] = momentum
        return carry

    lax.fori_loop(0, cells, one_row, 0)
    window = pl.ds(pl.multiple_of(start, 8), slab)
    design_ref[...] = design_all[:, window, :]
    momentum_ref[...] = momentum_all[:, window, :]


VMEM = pl.BlockSpec(memory_space=pltpu.VMEM)
SMEM = pl.BlockSpec(memory_space=pltpu.SMEM)


def on_core(kernel, operands, scalars, outs, scratch):
    return pl.pallas_call(
        kernel,
        out_shape=[jax.ShapeDtypeStruct(shape, jnp.float32) for shape in outs],
        in_specs=[SMEM] * scalars + [VMEM] * (len(operands) - scalars),
        out_specs=[VMEM] * len(outs),
        scratch_shapes=[pltpu.VMEM(shape, jnp.float32) for shape in scratch],
        compiler_params=pltpu.CompilerParams(vmem_limit_bytes=48 * 1024 * 1024),
    )(*operands)


def swap(value, axis, bit):
    count = lax.axis_size(axis)
    return lax.ppermute(value, axis, [(i, i ^ bit) for i in range(count)])


def along(value, step):
    count = lax.axis_size("brick")
    pairs = [(i, i + step) for i in range(count) if 0 <= i + step < count]
    return lax.ppermute(value, "brick", pairs)


def both_ways(value):
    count, loads = lax.axis_size("brick"), lax.axis_size("load")
    pairs = []
    for l in range(loads):
        step = 1 if l % 2 == 0 else -1
        pairs += [(l * count + i, l * count + i + step) for i in range(count) if 0 <= i + step < count]
    return lax.ppermute(value, ("load", "brick"), pairs)


def bits_of(count):
    return [1 << k for k in range(count.bit_length() - 1)]


def sum_over(value, axis):
    for bit in bits_of(lax.axis_size(axis)):
        value = value + swap(value, axis, bit)
    return value


def load_terms(value):
    bits = bits_of(lax.axis_size("load"))
    for bit in bits[:-1]:
        value = value + swap(value, "load", bit)
    return value, swap(value, "load", bits[-1])


def place_points(load_nodes, load_force, first_x, rows_x, size_y, size_z):
    loads_here = load_nodes.shape[0]
    span_cells = rows_x * size_y * size_z
    local_ids = load_nodes - first_x * size_y * size_z
    inside = (local_ids >= 0) & (local_ids < span_cells)
    slot_ids = jnp.where(inside, local_ids, span_cells)
    row_ids = lax.broadcasted_iota(jnp.int32, load_nodes.shape, 0)
    points = (
        jnp.zeros((loads_here, span_cells + 1), jnp.float32).at[row_ids, slot_ids].add(load_force)
    )
    return points[:, :span_cells].reshape(loads_here, rows_x, size_y, size_z)


def body(density, passive, support, load_nodes, load_force, self_weight, body_force):
    cells, size_y, size_z = density.shape
    loads = body_force.shape[0]
    bricks, brick = lax.axis_size("brick"), lax.axis_index("brick")
    load_count, load_index = lax.axis_size("load"), lax.axis_index("load")
    slab = size_y // load_count
    total_cells = float(cells * bricks * size_y * size_z)
    share = 1.0 / load_count
    even = load_index % 2 == 0
    place = jnp.stack([even, brick == 0, brick == bricks - 1, load_index * slab]).astype(jnp.int32)
    plane = (size_y, size_z)
    wide, rows = cells + 2 * DESIGN, cells + 2 * SOURCE

    free = (1 - support).astype(jnp.float32)
    design = jnp.where(passive == 1, density_floor, jnp.where(passive == 2, 1.0, density))
    upward = jnp.concatenate([design[cells - DESIGN:], free[cells - SOURCE:]])
    downward = jnp.concatenate([design[:DESIGN], free[:SOURCE]])
    pair_a = both_ways(jnp.where(even, upward, downward))
    pair_b = swap(pair_a, "load", 1)
    force_lo = along(body_force[:, cells - SOURCE:], 1)
    force_hi = along(body_force[:, :SOURCE], -1)
    points = place_points(load_nodes, load_force, brick * cells - SOURCE, rows, size_y, size_z)

    solve_scratch = [
        (wide,) + plane,
        (6, rows) + plane,
        (rows,) + plane,
        (loads, rows) + plane,
        (SWEEPS - 1, loads, rows) + plane,
        (loads, cells + 2) + plane,
    ]
    tile = (2, 8, size_z)
    sense, tiles, design_wide, free_wide, base_wide = on_core(
        functools.partial(first_kernel, cells, loads),
        (place, self_weight, design, free, body_force, force_lo, force_hi, points, pair_a, pair_b),
        2,
        [(cells,) + plane, tile, (wide,) + plane, (rows,) + plane, (loads, rows) + plane],
        solve_scratch,
    )
    tiles_first = sum_over(sum_over(tiles, "load"), "brick")
    sense_a, sense_b = load_terms(sense)
    start = jnp.where(even, cells - SENSE, 0)
    edge = lax.dynamic_slice_in_dim(sense_a, start, SENSE, 0) + lax.dynamic_slice_in_dim(sense_b, start, SENSE, 0)
    pair_a = both_ways(edge)
    pair_b = swap(pair_a, "load", 1)

    shown, sense, tiles, design, momentum = on_core(
        functools.partial(second_kernel, cells, loads, total_cells, share),
        (place, self_weight, tiles_first, sense_a, sense_b, pair_a, pair_b, design_wide, free_wide, base_wide),
        2,
        [(loads, cells) + plane, (cells,) + plane, tile, (cells,) + plane, (cells,) + plane],
        [(cells + 2 * SENSE,) + plane] + solve_scratch + [(wide,) + plane],
    )
    tiles_last = sum_over(sum_over(tiles, "load"), "brick")
    sense_a, sense_b = load_terms(sense)
    row_lo = along(sense_a[cells - 1:] + sense_b[cells - 1:], 1)
    row_hi = along(sense_a[:1] + sense_b[:1], -1)
    design, momentum = on_core(
        functools.partial(last_kernel, cells, slab, total_cells, share),
        (place, tiles_first, tiles_last, sense_a, sense_b, row_lo, row_hi, momentum, design, passive),
        1,
        [(cells, slab, size_z)] * 2,
        [(cells + 2,) + plane, (cells,) + plane, (cells,) + plane],
    )
    return design, momentum, shown


def solution(mesh):
    placed = (
        P("brick", None, None),
        P("brick", None, None),
        P("brick", None, None),
        P("load", None),
        P("load", None),
        P("load"),
        P("load", "brick", None, None),
    )
    return jax.shard_map(
        body,
        mesh=mesh,
        in_specs=placed,
        out_specs=(
            P("brick", "load", None),
            P("brick", "load", None),
            P("load", "brick", None, None),
        ),
        check_vma=False,
    )
```

```python
import functools

import jax
import jax.numpy as jnp
from jax import lax
from jax.experimental import pallas as pl
from jax.experimental.pallas import tpu as pltpu
from jax.sharding import PartitionSpec as P

SWEEPS = 5

stiff_floor = 0.01
mass_shift = 0.1
spectrum_low = 0.05
spectrum_high = 2.0
moment_decay = 0.8
step_size = 0.1
volume_pull = 0.5
volume_target = 0.4
density_floor = 0.001

SOURCE = SWEEPS
DESIGN = SWEEPS + 1
SENSE = SWEEPS + 2


def chebyshev_factors():
    centre = 0.5 * (spectrum_high + spectrum_low)
    half_width = 0.5 * (spectrum_high - spectrum_low)
    ratio_one = centre / half_width
    previous = 1.0 / ratio_one
    factors = []
    for _ in range(SWEEPS - 1):
        current = 1.0 / (2.0 * ratio_one - previous)
        factors.append((current * previous, 2.0 * current / half_width))
        previous = current
    return 1.0 / centre, factors


def shifted(plane):
    size_y, size_z = plane.shape
    return (
        pltpu.roll(plane, 1, 0),
        pltpu.roll(plane, size_y - 1, 0),
        pltpu.roll(plane, 1, 1),
        pltpu.roll(plane, size_z - 1, 1),
    )


def inner_masks(shape):
    along_y = lax.broadcasted_iota(jnp.int32, shape, 0)
    along_z = lax.broadcasted_iota(jnp.int32, shape, 1)
    return (along_y > 0, along_y < shape[0] - 1, along_z > 0, along_z < shape[1] - 1)


def beside_planes(plane, masks):
    return tuple(jnp.where(mask, moved, 0.0) for mask, moved in zip(masks, shifted(plane)))


def edge_planes(masks):
    edges = sum((1.0 - mask.astype(jnp.float32)) for mask in masks)
    return 1.0 / (8.0 - edges), 1.0 / (7.0 - edges)


def stiffness_of(design):
    return stiff_floor + (1.0 - stiff_floor) * (design * design * design)


def weight_row(q, is_free, stiff, weight, inverse, masks):
    here, below, above = stiff[q + 1], stiff[q], stiff[q + 2]
    around = (below, above) + beside_planes(here, masks)
    total = around[0]
    for plane in around[1:]:
        total = total + plane
    diagonal = (3.0 + mass_shift) * here + 0.5 * total
    scale = jnp.where(is_free, 1.0 / diagonal, 0.0)
    inverse[q] = scale
    half = 0.5 * scale
    weight[0, q] = half * (here + below)
    weight[1, q] = half * (here + above)
    for j in range(4):
        weight[2 + j, q] = jnp.where(masks[j], half * (here + around[2 + j]), 0.0)


class Kept:
    def __init__(self):
        self.places = {}

    def put(self, key, ref, index, value):
        ref[index] = value
        self.places[key] = (ref, index)

    def get(self, key):
        ref, index = self.places[key]
        return ref[index]


def sweep_row(k, q, loads, weight, resid, steps, resid_to, steps_to, shown_to, shown):
    _, factors = chebyshev_factors()
    keep, gain = factors[k]
    last = k == len(factors) - 1
    faces = [weight[j, q] for j in range(6)]
    for l in range(loads):
        here = steps.get((k, l, q))
        total = faces[0] * steps.get((k, l, q - 1)) + faces[1] * steps.get((k, l, q + 1))
        for face, moved in zip(faces[2:], shifted(here)):
            total = total + face * moved
        left = resid.get((l, q)) - here + total
        step = keep * here + gain * left
        if last:
            for earlier in range(k + 1):
                step = step + steps.get((earlier, l, q))
            shown.put((l, q), shown_to, (l, q - (SWEEPS - 1)), step)
        else:
            resid.put((l, q), resid_to, (l, q), left)
            steps.put((k + 1, l, q), steps_to, (k + 1, l, q), step)


def energy_row(i, loads, design, shown, masks):
    q = i + SOURCE
    energy = None
    for l in range(loads):
        here = shown.get((l, q))
        around = (shown.get((l, q - 1)), shown.get((l, q + 1))) + beside_planes(here, masks)
        spread = None
        for plane in around:
            gap = here - plane
            spread = gap * gap if spread is None else spread + gap * gap
        part = mass_shift * (here * here) + 0.25 * spread
        energy = part if energy is None else energy + part
    return (-3.0 * (1.0 - stiff_floor)) * (design * design) * energy


def fold(plane):
    return jnp.sum(plane.reshape(plane.shape[0] // 8, 8, plane.shape[1]), axis=0)


def filter_total(cells, sense, is_first, is_last, masks):
    inside, outer = edge_planes(masks)
    usual = 4.0 * inside + sum(beside_planes(inside, masks))
    at_end = 2.0 * outer + inside + sum(beside_planes(outer, masks))
    zero = jnp.zeros_like(inside)
    total = sense[0]
    for i in range(1, cells):
        total = total + sense[i]
    ends = jnp.where(is_first, sense[0], zero) + jnp.where(is_last, sense[cells - 1], zero)
    nexts = jnp.where(is_first, sense[1], zero) + jnp.where(is_last, sense[cells - 2], zero)
    return -fold(total * usual + ends * (at_end - usual) + nexts * (outer - inside))


def fold_rows(cells, ref):
    total = ref[0]
    for i in range(1, cells):
        total = total + ref[i]
    return fold(total)


def points_kernel(cells, loads, place, nodes, forces, force_ref, base_ref):
    rows = cells + 2 * SOURCE
    size_y, size_z = base_ref.shape[2:]
    zero = jnp.zeros((size_y, size_z), jnp.float32)
    for l in range(loads):
        for q in range(rows):
            own = SOURCE <= q < SOURCE + cells
            base_ref[l, q] = force_ref[l, q - SOURCE] if own else zero
    first = place[4]
    along_z = lax.broadcasted_iota(jnp.int32, (1, size_z), 1)
    for l in range(loads):

        def one_point(p, carry, l=l):
            cell = nodes[l, p] - first

            @pl.when((cell >= 0) & (cell < rows * size_y * size_z))
            def _():
                line, z = cell // size_z, cell % size_z
                q, y = line // size_y, line % size_y
                spot = (l, q, pl.ds(y, 1), slice(None))
                base_ref[spot] = base_ref[spot] + jnp.where(along_z == z, forces[l, p], 0.0)

            return carry

        lax.fori_loop(0, nodes.shape[1], one_point, 0)


def inner_steps(cells, rows):
    return [range(SOURCE + k, SOURCE + cells - k) for k in range(SWEEPS)]


def early_kernel(cells, loads, place, self_weight, design_ref, free_ref, base_ref, pair_a, pair_b,
                 design_wide, free_wide, weight, inverse, resid_ref, steps_ref, shown_ref, stiff):
    even, is_first, is_last = place[0] == 1, place[1] == 1, place[2] == 1
    shape = design_ref.shape[1:]
    masks = inner_masks(shape)
    rows = cells + 2 * SOURCE
    zero = jnp.zeros(shape, jnp.float32)
    for i in range(DESIGN):
        low = jnp.where(even, pair_a[i], pair_b[i])
        high = jnp.where(even, pair_b[i], pair_a[i])
        design_wide[i] = low
        design_wide[DESIGN + cells + i] = high
        stiff[i] = jnp.where(is_first, zero, stiffness_of(low))
        stiff[DESIGN + cells + i] = jnp.where(is_last, zero, stiffness_of(high))
    for i in range(SOURCE):
        low = jnp.where(even, pair_a[DESIGN + i], pair_b[DESIGN + i])
        high = jnp.where(even, pair_b[DESIGN + i], pair_a[DESIGN + i])
        free_wide[i] = jnp.where(is_first, zero, low)
        free_wide[SOURCE + cells + i] = jnp.where(is_last, zero, high)
    for i in range(cells):
        design_wide[DESIGN + i] = design_ref[i]
        stiff[DESIGN + i] = stiffness_of(design_ref[i])
        free_wide[SOURCE + i] = free_ref[i]
    for q in range(rows):
        weight_row(q, free_wide[q] > 0.5, stiff, weight, inverse, masks)
    first_scale, _ = chebyshev_factors()
    resid, steps, shown = Kept(), Kept(), Kept()
    inner = inner_steps(cells, rows)
    for q in inner[0]:
        for l in range(loads):
            left = inverse[q] * (base_ref[l, q] + self_weight[l] * design_wide[q + 1])
            resid.put((l, q), resid_ref, (l, q), left)
            steps.put((0, l, q), steps_ref, (0, l, q), first_scale * left)
    for k in range(SWEEPS - 1):
        for q in inner[k + 1]:
            sweep_row(k, q, loads, weight, resid, steps, resid_ref, steps_ref, shown_ref, shown)


def first_kernel(cells, loads, place, self_weight, force_lo, force_hi, base_in, design_wide, weight, inverse,
                 resid_in, steps_in, shown_in, sense_ref, tile_ref, base_ref, resid_ref, steps_ref, shown_ref):
    is_first, is_last = place[1] == 1, place[2] == 1
    shape = design_wide.shape[1:]
    masks = inner_masks(shape)
    rows = cells + 2 * SOURCE
    first_scale, _ = chebyshev_factors()
    resid, steps, shown = Kept(), Kept(), Kept()
    inner = inner_steps(cells, rows)
    for l in range(loads):
        for k in range(SWEEPS - 1):
            for q in inner[k]:
                steps.places[(k, l, q)] = (steps_in, (k, l, q))
        for q in inner[0]:
            resid.places[(l, q)] = (resid_in, (l, q))
        for q in inner[SWEEPS - 1]:
            shown.places[(l, q)] = (shown_in, (l, q - (SWEEPS - 1)))
    for l in range(loads):
        for q in range(rows):
            base = base_in[l, q]
            if q in inner[0]:
                base_ref[l, q] = base
                continue
            base = base + (force_lo[l, q] if q < SOURCE else force_hi[l, q - SOURCE - cells])
            base_ref[l, q] = base
            left = inverse[q] * (base + self_weight[l] * design_wide[q + 1])
            resid.put((l, q), resid_ref, (l, q), left)
            steps.put((0, l, q), steps_ref, (0, l, q), first_scale * left)
    for k in range(SWEEPS - 1):
        for q in range(k + 1, rows - k - 1):
            if q not in inner[k + 1]:
                sweep_row(k, q, loads, weight, resid, steps, resid_ref, steps_ref, shown_ref, shown)
    for i in range(cells):
        sense_ref[i] = energy_row(i, loads, design_wide[DESIGN + i], shown, masks)
    tile_ref[0] = filter_total(cells, sense_ref, is_first, is_last, masks)
    tile_ref[1] = fold_rows(cells, design_wide.at[pl.ds(DESIGN, cells)])


def moment_kernel(cells, place, sense_a, sense_b, pair_a, pair_b, moment_ref, sense_wide):
    even, is_first, is_last = place[0] == 1, place[1] == 1, place[2] == 1
    shape = sense_a.shape[1:]
    masks = inner_masks(shape)
    zero = jnp.zeros(shape, jnp.float32)
    for i in range(SENSE):
        low = jnp.where(even, pair_a[i], pair_b[i])
        high = jnp.where(even, pair_b[i], pair_a[i])
        sense_wide[i] = jnp.where(is_first, zero, low)
        sense_wide[SENSE + cells + i] = jnp.where(is_last, zero, high)
    for i in range(cells):
        sense_wide[SENSE + i] = sense_a[i] + sense_b[i]
    inside, outer = edge_planes(masks)
    for r in range(cells + 2 * DESIGN):
        at_end = (is_first & (r == DESIGN)) | (is_last & (r == DESIGN + cells - 1))
        moment_ref[r] = filtered_row(r, sense_wide, masks) * jnp.where(at_end, outer, inside)


def filtered_row(r, sense_wide, masks):
    here = sense_wide[r + 1]
    total = 2.0 * here + sense_wide[r] + sense_wide[r + 2]
    for plane in beside_planes(here, masks):
        total = total + plane
    return total


def rate_and_pull(abs_tile, density_tile, total_cells, share):
    abs_total = jnp.sum(abs_tile, keepdims=True)
    density_total = jnp.sum(density_tile, keepdims=True) * share
    mean_step = abs_total / total_cells + 1e-6
    return step_size / mean_step, volume_pull * (density_total / total_cells - volume_target)


def second_kernel(cells, loads, total_cells, share, place, self_weight, tile_in, moment_wide,
                  design_wide, free_wide, base_wide,
                  shown_ref, sense_ref, tile_ref, design_out,
                  stiff, weight, inverse, resid_ref, steps_ref, shown_to, design_new):
    is_first, is_last = place[1] == 1, place[2] == 1
    shape = moment_wide.shape[1:]
    masks = inner_masks(shape)
    wide = cells + 2 * DESIGN
    rows = cells + 2 * SOURCE
    zero = jnp.zeros(shape, jnp.float32)
    rate, pull = rate_and_pull(tile_in[0], tile_in[1], total_cells, share)
    for r in range(wide):
        before = design_wide[r]
        moved = jnp.clip(before - rate * moment_wide[r] - pull, density_floor, 1.0)
        fixed = (before == density_floor) | (before == 1.0)
        design = jnp.where(fixed, before, moved)
        design_new[r] = design
        stiffness = stiffness_of(design)
        if r < DESIGN:
            stiff[r] = jnp.where(is_first, zero, stiffness)
        elif r >= DESIGN + cells:
            stiff[r] = jnp.where(is_last, zero, stiffness)
        else:
            stiff[r] = stiffness
            design_out[r - DESIGN] = design
    resid, steps, shown = Kept(), Kept(), Kept()
    first_scale, _ = chebyshev_factors()
    for q in range(rows):
        weight_row(q, free_wide[q] > 0.5, stiff, weight, inverse, masks)
        scale, design = inverse[q], design_new[q + 1]
        for l in range(loads):
            left = scale * (base_wide[l, q] + self_weight[l] * design)
            resid.put((l, q), resid_ref, (l, q), left)
            steps.put((0, l, q), steps_ref, (0, l, q), first_scale * left)
    for k in range(SWEEPS - 1):
        for q in range(k + 1, rows - k - 1):
            sweep_row(k, q, loads, weight, resid, steps, resid_ref, steps_ref, shown_to, shown)
    for i in range(cells):
        for l in range(loads):
            shown_ref[l, i] = shown.get((l, i + SOURCE))
        sense_ref[i] = energy_row(i, loads, design_out[i], shown, masks)
    tile_ref[0] = filter_total(cells, sense_ref, is_first, is_last, masks)
    tile_ref[1] = fold_rows(cells, design_out)


def last_moment_kernel(cells, slab, place, sense_a, sense_b, pair_a, pair_b, moment_wide,
                       momentum_ref, sense_wide, momentum_all):
    even, is_first, is_last, start = place[0] == 1, place[1] == 1, place[2] == 1, place[3]
    shape = sense_a.shape[1:]
    masks = inner_masks(shape)
    zero = jnp.zeros(shape, jnp.float32)
    sense_wide[0] = jnp.where(is_first, zero, jnp.where(even, pair_a[0], pair_b[0]))
    sense_wide[cells + 1] = jnp.where(is_last, zero, jnp.where(even, pair_b[0], pair_a[0]))
    for i in range(cells):
        sense_wide[i + 1] = sense_a[i] + sense_b[i]
    inside, outer = edge_planes(masks)
    for i in range(cells):
        scale = inside
        if i == 0:
            scale = jnp.where(is_first, outer, inside)
        elif i == cells - 1:
            scale = jnp.where(is_last, outer, inside)
        momentum_all[i] = moment_decay * moment_wide[DESIGN + i] + filtered_row(i, sense_wide, masks) * scale
    momentum_ref[...] = momentum_all[:, pl.ds(pl.multiple_of(start, 8), slab), :]


def last_kernel(cells, slab, total_cells, share, place, tile_before, tile_in, momentum_ref, design_in, passive_ref,
                design_ref):
    window = pl.ds(pl.multiple_of(place[3], 8), slab)
    rate, pull = rate_and_pull(moment_decay * tile_before[0] + tile_in[0], tile_in[1], total_cells, share)
    for i in range(cells):
        moved = jnp.clip(design_in[i, window, :] - rate * momentum_ref[i] - pull, density_floor, 1.0)
        kind = passive_ref[i, window, :]
        design_ref[i] = jnp.where(kind == 1, density_floor, jnp.where(kind == 2, 1.0, moved))


VMEM = pl.BlockSpec(memory_space=pltpu.VMEM)
SMEM = pl.BlockSpec(memory_space=pltpu.SMEM)


def on_core(kernel, operands, scalars, outs, scratch, limit=24):
    return pl.pallas_call(
        kernel,
        out_shape=[jax.ShapeDtypeStruct(shape, jnp.float32) for shape in outs],
        in_specs=[SMEM] * scalars + [VMEM] * (len(operands) - scalars),
        out_specs=[VMEM] * len(outs),
        scratch_shapes=[pltpu.VMEM(shape, jnp.float32) for shape in scratch],
        compiler_params=pltpu.CompilerParams(vmem_limit_bytes=limit * 1024 * 1024),
    )(*operands)


def swap(value, axis, bit):
    count = lax.axis_size(axis)
    return lax.ppermute(value, axis, [(i, i ^ bit) for i in range(count)])


def along(value, step):
    count = lax.axis_size("brick")
    pairs = [(i, i + step) for i in range(count) if 0 <= i + step < count]
    return lax.ppermute(value, "brick", pairs)


def both_ways(value):
    count, loads = lax.axis_size("brick"), lax.axis_size("load")
    pairs = []
    for l in range(loads):
        step = 1 if l % 2 == 0 else -1
        pairs += [(l * count + i, l * count + i + step) for i in range(count) if 0 <= i + step < count]
    return lax.ppermute(value, ("load", "brick"), pairs)


def bits_of(count):
    return [1 << k for k in range(count.bit_length() - 1)]


def sum_over(value, axis):
    for bit in bits_of(lax.axis_size(axis)):
        value = value + swap(value, axis, bit)
    return value


def load_terms(value):
    bits = bits_of(lax.axis_size("load"))
    for bit in bits[:-1]:
        value = value + swap(value, "load", bit)
    return value, swap(value, "load", bits[-1])


def after(value, other):
    return lax.optimization_barrier((value, other))[0]


def meet(sense, tiles, width, even):
    cells = sense.shape[0]
    tiles = sum_over(tiles, "load")
    sense_a, sense_b = load_terms(after(sense, tiles))
    bits = bits_of(lax.axis_size("brick"))
    tiles = tiles + swap(tiles, "brick", bits[0])
    start = jnp.where(even, cells - width, 0)
    sense_a, sense_b = after((sense_a, sense_b), tiles)
    edge = lax.dynamic_slice_in_dim(sense_a, start, width, 0) + lax.dynamic_slice_in_dim(sense_b, start, width, 0)
    pair_a = both_ways(edge)
    for bit in bits[1:-1]:
        tiles = tiles + swap(tiles, "brick", bit)
    pair_b = swap(after(pair_a, tiles), "load", 1)
    tiles = tiles + swap(tiles, "brick", bits[-1])
    return sense_a, sense_b, pair_a, pair_b, tiles


def body(density, passive, support, load_nodes, load_force, self_weight, body_force):
    cells, size_y, size_z = density.shape
    loads = body_force.shape[0]
    bricks, brick = lax.axis_size("brick"), lax.axis_index("brick")
    load_count, load_index = lax.axis_size("load"), lax.axis_index("load")
    slab = size_y // load_count
    total_cells = float(cells * bricks * size_y * size_z)
    share = 1.0 / load_count
    even = load_index % 2 == 0
    first_cell = (brick * cells - SOURCE) * size_y * size_z
    place = jnp.stack([even, brick == 0, brick == bricks - 1, load_index * slab, first_cell]).astype(jnp.int32)
    plane = (size_y, size_z)
    wide, rows = cells + 2 * DESIGN, cells + 2 * SOURCE
    tile = (2, 8, size_z)
    shown_shape = (loads, cells + 2) + plane
    resid_shape = (loads, rows) + plane
    steps_shape = (SWEEPS - 1, loads, rows) + plane

    free = (1 - support).astype(jnp.float32)
    design = jnp.where(passive == 1, density_floor, jnp.where(passive == 2, 1.0, density))
    upward = jnp.concatenate([design[cells - DESIGN:], free[cells - SOURCE:]])
    downward = jnp.concatenate([design[:DESIGN], free[:SOURCE]])
    pair_a = both_ways(jnp.where(even, upward, downward))
    pair_b = swap(pair_a, "load", 1)
    force_lo = along(body_force[:, cells - SOURCE:], 1)
    force_hi = along(body_force[:, :SOURCE], -1)
    (base,) = on_core(
        functools.partial(points_kernel, cells, loads),
        (place, load_nodes, load_force, body_force),
        3,
        [resid_shape],
        [],
    )
    design_wide, free_wide, weight, inverse, resid, steps, shown = on_core(
        functools.partial(early_kernel, cells, loads),
        (place, self_weight, design, free, base, pair_a, pair_b),
        2,
        [(wide,) + plane, (rows,) + plane, (6, rows) + plane, (rows,) + plane, resid_shape, steps_shape, shown_shape],
        [(wide,) + plane],
    )
    sense, tiles, base_wide = on_core(
        functools.partial(first_kernel, cells, loads),
        (place, self_weight, force_lo, force_hi, base, design_wide, weight, inverse, resid, steps, shown),
        2,
        [(cells,) + plane, tile, resid_shape],
        [resid_shape, steps_shape, shown_shape],
    )
    sense_a, sense_b, pair_a, pair_b, tiles_first = meet(sense, tiles, SENSE, even)
    (moment_wide,) = on_core(
        functools.partial(moment_kernel, cells),
        (place, sense_a, sense_b, pair_a, pair_b),
        1,
        [(wide,) + plane],
        [(cells + 2 * SENSE,) + plane],
    )
    shown, sense, tiles, design = on_core(
        functools.partial(second_kernel, cells, loads, total_cells, share),
        (place, self_weight, tiles_first, moment_wide, design_wide, free_wide, base_wide),
        2,
        [(loads, cells) + plane, (cells,) + plane, tile, (cells,) + plane],
        [(wide,) + plane, (6, rows) + plane, (rows,) + plane, resid_shape, steps_shape, shown_shape, (wide,) + plane],
    )
    sense_a, sense_b, pair_a, pair_b, tiles_last = meet(sense, tiles, 1, even)
    (momentum,) = on_core(
        functools.partial(last_moment_kernel, cells, slab),
        (place, sense_a, sense_b, pair_a, pair_b, moment_wide),
        1,
        [(cells, slab, size_z)],
        [(cells + 2,) + plane, (cells,) + plane],
    )
    (design,) = on_core(
        functools.partial(last_kernel, cells, slab, total_cells, share),
        (place, tiles_first, tiles_last, momentum, design, passive),
        1,
        [(cells, slab, size_z)],
        [],
    )
    return design, momentum, shown


def solution(mesh):
    placed = (
        P("brick", None, None),
        P("brick", None, None),
        P("brick", None, None),
        P("load", None),
        P("load", None),
        P("load"),
        P("load", "brick", None, None),
    )
    return jax.shard_map(
        body,
        mesh=mesh,
        in_specs=placed,
        out_specs=(
            P("brick", "load", None),
            P("brick", "load", None),
            P("load", "brick", None, None),
        ),
        check_vma=False,
    )
```

```python
import functools

import jax
import jax.numpy as jnp
from jax import lax
from jax.experimental import pallas as pl
from jax.experimental.pallas import tpu as pltpu
from jax.sharding import PartitionSpec as P

SWEEPS = 5

stiff_floor = 0.01
mass_shift = 0.1
spectrum_low = 0.05
spectrum_high = 2.0
moment_decay = 0.8
step_size = 0.1
volume_pull = 0.5
volume_target = 0.4
density_floor = 0.001

SOURCE = SWEEPS
DESIGN = SWEEPS + 1
SENSE = SWEEPS + 2


def chebyshev_factors():
    centre = 0.5 * (spectrum_high + spectrum_low)
    half_width = 0.5 * (spectrum_high - spectrum_low)
    ratio_one = centre / half_width
    previous = 1.0 / ratio_one
    factors = []
    for _ in range(SWEEPS - 1):
        current = 1.0 / (2.0 * ratio_one - previous)
        factors.append((current * previous, 2.0 * current / half_width))
        previous = current
    return 1.0 / centre, factors


def shifted(plane):
    size_y, size_z = plane.shape
    return (
        pltpu.roll(plane, 1, 0),
        pltpu.roll(plane, size_y - 1, 0),
        pltpu.roll(plane, 1, 1),
        pltpu.roll(plane, size_z - 1, 1),
    )


def inner_masks(shape):
    along_y = lax.broadcasted_iota(jnp.int32, shape, 0)
    along_z = lax.broadcasted_iota(jnp.int32, shape, 1)
    return (along_y > 0, along_y < shape[0] - 1, along_z > 0, along_z < shape[1] - 1)


def beside_planes(plane, masks):
    return tuple(jnp.where(mask, moved, 0.0) for mask, moved in zip(masks, shifted(plane)))


def edge_planes(masks):
    edges = sum((1.0 - mask.astype(jnp.float32)) for mask in masks)
    return 1.0 / (8.0 - edges), 1.0 / (7.0 - edges)


def stiffness_of(design):
    return stiff_floor + (1.0 - stiff_floor) * (design * design * design)


def weight_row(q, is_free, stiff, weight, inverse, masks):
    here, below, above = stiff[q + 1], stiff[q], stiff[q + 2]
    around = (below, above) + beside_planes(here, masks)
    total = around[0]
    for plane in around[1:]:
        total = total + plane
    diagonal = (3.0 + mass_shift) * here + 0.5 * total
    scale = jnp.where(is_free, 1.0 / diagonal, 0.0)
    inverse[q] = scale
    half = 0.5 * scale
    weight[0, q] = half * (here + below)
    weight[1, q] = half * (here + above)
    for j in range(4):
        weight[2 + j, q] = jnp.where(masks[j], half * (here + around[2 + j]), 0.0)


class Kept:
    def __init__(self):
        self.places = {}

    def put(self, key, ref, index, value):
        ref[index] = value
        self.places[key] = (ref, index)

    def get(self, key):
        ref, index = self.places[key]
        return ref[index]


def sweep_row(k, q, loads, weight, resid, steps, resid_to, steps_to, shown_to, shown, first=0, first_shown=SWEEPS - 1):
    _, factors = chebyshev_factors()
    keep, gain = factors[k]
    last = k == len(factors) - 1
    faces = [weight[j, q] for j in range(6)]
    for l in range(loads):
        here = steps.get((k, l, q))
        total = faces[0] * steps.get((k, l, q - 1)) + faces[1] * steps.get((k, l, q + 1))
        for face, moved in zip(faces[2:], shifted(here)):
            total = total + face * moved
        left = resid.get((l, q)) - here + total
        step = keep * here + gain * left
        if last:
            for earlier in range(k + 1):
                step = step + steps.get((earlier, l, q))
            shown.put((l, q), shown_to, (l, q - first_shown), step)
        else:
            resid.put((l, q), resid_to, (l, q - first), left)
            steps.put((k + 1, l, q), steps_to, (k + 1, l, q - first), step)


def energy_row(i, loads, design, shown, masks):
    q = i + SOURCE
    energy = None
    for l in range(loads):
        here = shown.get((l, q))
        around = (shown.get((l, q - 1)), shown.get((l, q + 1))) + beside_planes(here, masks)
        spread = None
        for plane in around:
            gap = here - plane
            spread = gap * gap if spread is None else spread + gap * gap
        part = mass_shift * (here * here) + 0.25 * spread
        energy = part if energy is None else energy + part
    return (-3.0 * (1.0 - stiff_floor)) * (design * design) * energy


def fold(plane):
    return jnp.sum(plane.reshape(plane.shape[0] // 8, 8, plane.shape[1]), axis=0)


def filter_total(cells, sense, is_first, is_last, masks):
    inside, outer = edge_planes(masks)
    usual = 4.0 * inside + sum(beside_planes(inside, masks))
    at_end = 2.0 * outer + inside + sum(beside_planes(outer, masks))
    zero = jnp.zeros_like(inside)
    total = sense[0]
    for i in range(1, cells):
        total = total + sense[i]
    ends = jnp.where(is_first, sense[0], zero) + jnp.where(is_last, sense[cells - 1], zero)
    nexts = jnp.where(is_first, sense[1], zero) + jnp.where(is_last, sense[cells - 2], zero)
    return -fold(total * usual + ends * (at_end - usual) + nexts * (outer - inside))


def fold_rows(cells, ref):
    total = jnp.abs(ref[0])
    for i in range(1, cells):
        total = total + jnp.abs(ref[i])
    return fold(total)


def place_of():
    brick = lax.axis_index("brick")
    return lax.axis_index("load") % 2 == 0, brick == 0, brick == lax.axis_size("brick") - 1


def prepare_kernel(cells, density, passive, support, force, payload_ref, upper_ref, lower_ref,
                   design_rows, kind_rows, hold_rows, sems):
    even, _, _ = place_of()
    start = jnp.where(even, cells - DESIGN, 0)
    start_mask = jnp.where(even, cells - SOURCE, 0)
    copies = [
        pltpu.make_async_copy(source, target, sems.at[i])
        for i, (source, target) in enumerate((
            (density.at[pl.ds(start, DESIGN)], design_rows),
            (passive.at[pl.ds(start, DESIGN)], kind_rows),
            (support.at[pl.ds(start_mask, SOURCE)], hold_rows),
            (force.at[:, pl.ds(cells - SOURCE, SOURCE)], upper_ref),
            (force.at[:, pl.ds(0, SOURCE)], lower_ref),
        ))
    ]
    for copy in copies:
        copy.start()
    for copy in copies[:3]:
        copy.wait()
    for i in range(DESIGN):
        payload_ref[i] = passive_apply(design_rows[i], kind_rows[i])
    for i in range(SOURCE):
        payload_ref[DESIGN + i] = (1 - hold_rows[i]).astype(jnp.float32)
    for copy in copies[3:]:
        copy.wait()


def points_kernel(cells, loads, nodes, forces, force_ref, base_ref):
    rows = cells + 2 * SOURCE
    size_y, size_z = base_ref.shape[2:]
    zero = jnp.zeros((size_y, size_z), jnp.float32)
    for l in range(loads):
        for q in range(rows):
            own = SOURCE <= q < SOURCE + cells
            base_ref[l, q] = force_ref[l, q - SOURCE] if own else zero
    first = (lax.axis_index("brick") * cells - SOURCE) * size_y * size_z
    along_z = lax.broadcasted_iota(jnp.int32, (1, size_z), 1)
    for l in range(loads):

        def one_point(p, carry, l=l):
            cell = nodes[l, p] - first

            @pl.when((cell >= 0) & (cell < rows * size_y * size_z))
            def _():
                line, z = cell // size_z, cell % size_z
                q, y = line // size_y, line % size_y
                spot = (l, q, pl.ds(y, 1), slice(None))
                base_ref[spot] = base_ref[spot] + jnp.where(along_z == z, forces[l, p], 0.0)

            return carry

        lax.fori_loop(0, nodes.shape[1], one_point, 0)


def base_row(l, q, cells, base_in, force_lo, force_hi):
    if q < SOURCE:
        return base_in[l, q] + force_lo[l, q]
    if q >= SOURCE + cells:
        return base_in[l, q] + force_hi[l, q - SOURCE - cells]
    return base_in[l, q]


def inner_steps(cells):
    return [range(SOURCE + k, SOURCE + cells - k) for k in range(SWEEPS)]


def early_kernel(cells, loads, self_weight, density, passive, support, base_ref, pair_a, pair_b,
                 design_wide, weight, inverse, resid_ref, steps_ref, shown_ref, stiff,
                 free_wide, design_low, design_high):
    even, is_first, is_last = place_of()
    shape = density.shape[1:]
    masks = inner_masks(shape)
    rows = cells + 2 * SOURCE
    zero = jnp.zeros(shape, jnp.float32)
    for i in range(DESIGN):
        low = jnp.where(even, pair_a[i], pair_b[i])
        high = jnp.where(even, pair_b[i], pair_a[i])
        design_low[i] = low
        design_high[i] = high
        stiff[i] = jnp.where(is_first, zero, stiffness_of(low))
        stiff[DESIGN + cells + i] = jnp.where(is_last, zero, stiffness_of(high))
    for i in range(SOURCE):
        low = jnp.where(even, pair_a[DESIGN + i], pair_b[DESIGN + i])
        high = jnp.where(even, pair_b[DESIGN + i], pair_a[DESIGN + i])
        free_wide[i] = jnp.where(is_first, zero, low)
        free_wide[SOURCE + cells + i] = jnp.where(is_last, zero, high)
    for i in range(cells):
        design = passive_apply(density[i], passive[i])
        stiff[DESIGN + i] = stiffness_of(design)
        free_wide[SOURCE + i] = (1 - support[i]).astype(jnp.float32)
        design_wide[DESIGN + i] = jnp.where(support[i] == 0, design, -design)
    for r in range(DESIGN):
        free = free_wide[r - 1] > 0.5 if r > 0 else zero > 0.5
        design_wide[r] = jnp.where(free, design_low[r], -design_low[r])
        q = SOURCE + cells + r
        free = free_wide[q] > 0.5 if q < rows else zero > 0.5
        design_wide[DESIGN + cells + r] = jnp.where(free, design_high[r], -design_high[r])
    for q in range(rows):
        weight_row(q, free_wide[q] > 0.5, stiff, weight, inverse, masks)
    first_scale, _ = chebyshev_factors()
    resid, steps, shown = Kept(), Kept(), Kept()
    inner = inner_steps(cells)
    for q in inner[0]:
        for l in range(loads):
            left = inverse[q] * (base_ref[l, q] + self_weight[l] * jnp.abs(design_wide[q + 1]))
            resid.put((l, q), resid_ref, (l, q - SOURCE), left)
            steps.put((0, l, q), steps_ref, (0, l, q - SOURCE), first_scale * left)
    for k in range(SWEEPS - 1):
        for q in inner[k + 1]:
            sweep_row(
                k, q, loads, weight, resid, steps, resid_ref, steps_ref, shown_ref, shown,
                SOURCE, SOURCE + SWEEPS - 1,
            )


def first_kernel(cells, loads, self_weight, force_lo, force_hi, base_in, design_wide, weight, inverse,
                 resid_in, steps_in, shown_in, sense_ref, tile_ref, resid_ref, steps_ref, shown_ref):
    _, is_first, is_last = place_of()
    shape = design_wide.shape[1:]
    masks = inner_masks(shape)
    rows = cells + 2 * SOURCE
    first_scale, _ = chebyshev_factors()
    resid, steps, shown = Kept(), Kept(), Kept()
    inner = inner_steps(cells)
    for l in range(loads):
        for k in range(SWEEPS - 1):
            for q in inner[k]:
                steps.places[(k, l, q)] = (steps_in, (k, l, q - SOURCE))
        for q in inner[0]:
            resid.places[(l, q)] = (resid_in, (l, q - SOURCE))
        for q in inner[SWEEPS - 1]:
            shown.places[(l, q)] = (shown_in, (l, q - SOURCE - (SWEEPS - 1)))
    for l in range(loads):
        for q in range(rows):
            if q in inner[0]:
                continue
            base = base_row(l, q, cells, base_in, force_lo, force_hi)
            left = inverse[q] * (base + self_weight[l] * jnp.abs(design_wide[q + 1]))
            resid.put((l, q), resid_ref, (l, q), left)
            steps.put((0, l, q), steps_ref, (0, l, q), first_scale * left)
    for k in range(SWEEPS - 1):
        for q in range(k + 1, rows - k - 1):
            if q not in inner[k + 1]:
                sweep_row(k, q, loads, weight, resid, steps, resid_ref, steps_ref, shown_ref, shown)
    for i in range(cells):
        sense_ref[i] = energy_row(i, loads, design_wide[DESIGN + i], shown, masks)
    own = design_wide.at[pl.ds(DESIGN, cells)]
    spread_totals(tile_ref, filter_total(cells, sense_ref, is_first, is_last, masks), fold_rows(cells, own))


def moment_kernel(cells, sense, pair_a, pair_b, moment_ref, sense_wide):
    even, is_first, is_last = place_of()
    shape = sense.shape[1:]
    masks = inner_masks(shape)
    zero = jnp.zeros(shape, jnp.float32)
    for i in range(SENSE):
        low = jnp.where(even, pair_a[i], pair_b[i])
        high = jnp.where(even, pair_b[i], pair_a[i])
        sense_wide[i] = jnp.where(is_first, zero, low)
        sense_wide[SENSE + cells + i] = jnp.where(is_last, zero, high)
    for i in range(cells):
        sense_wide[SENSE + i] = sense[i]
    inside, outer = edge_planes(masks)
    for r in range(cells + 2 * DESIGN):
        at_end = (is_first & (r == DESIGN)) | (is_last & (r == DESIGN + cells - 1))
        moment_ref[r] = filtered_row(r, sense_wide, masks) * jnp.where(at_end, outer, inside)


def filtered_row(r, sense_wide, masks):
    here = sense_wide[r + 1]
    total = 2.0 * here + sense_wide[r] + sense_wide[r + 2]
    for plane in beside_planes(here, masks):
        total = total + plane
    return total


def spread_totals(tile_ref, abs_tile, density_tile):
    count, width = tile_ref.shape
    row = jnp.concatenate([jnp.sum(tile, axis=0, keepdims=True) for tile in (abs_tile, density_tile)], axis=1)
    tile_ref[...] = jnp.broadcast_to(row, (count, width))


def rate_and_pull(totals, total_cells, share):
    half = totals.shape[1] // 2
    abs_total = jnp.sum(totals[:, :half], keepdims=True)
    density_total = jnp.sum(totals[:, half:], keepdims=True) * share
    mean_step = abs_total / total_cells + 1e-6
    return step_size / mean_step, volume_pull * (density_total / total_cells - volume_target)


def second_kernel(cells, loads, total_cells, share, self_weight, tile_in, moment_wide,
                  design_wide, base_far, lo_far, hi_far,
                  shown_ref, design_out, sense_ref, tile_ref,
                  stiff, weight, inverse, resid_ref, steps_ref, shown_to, design_new,
                  base_in, force_lo, force_hi, sems):
    copies = [
        pltpu.make_async_copy(source, target, sems.at[i])
        for i, (source, target) in enumerate(
            ((base_far, base_in), (lo_far, force_lo), (hi_far, force_hi)))
    ]
    for copy in copies:
        copy.start()
    _, is_first, is_last = place_of()
    shape = moment_wide.shape[1:]
    masks = inner_masks(shape)
    wide = cells + 2 * DESIGN
    rows = cells + 2 * SOURCE
    zero = jnp.zeros(shape, jnp.float32)
    rate, pull = rate_and_pull(tile_in[...], total_cells, share)
    for r in range(wide):
        signed = design_wide[r]
        before = jnp.abs(signed)
        moved = jnp.clip(before - rate * moment_wide[r] - pull, density_floor, 1.0)
        fixed = (before == density_floor) | (before == 1.0)
        design = jnp.where(fixed, before, moved)
        design_new[r] = design
        stiffness = stiffness_of(design)
        if r < DESIGN:
            stiff[r] = jnp.where(is_first, zero, stiffness)
        elif r >= DESIGN + cells:
            stiff[r] = jnp.where(is_last, zero, stiffness)
        else:
            stiff[r] = stiffness
    own_rows = pltpu.make_async_copy(design_new.at[pl.ds(DESIGN, cells)], design_out, sems.at[len(copies) + loads])
    own_rows.start()
    resid, steps, shown = Kept(), Kept(), Kept()
    first_scale, _ = chebyshev_factors()
    for q in range(rows):
        weight_row(q, design_wide[q + 1] > 0.0, stiff, weight, inverse, masks)
    for copy in copies:
        copy.wait()
    for q in range(rows):
        scale, design = inverse[q], design_new[q + 1]
        for l in range(loads):
            left = scale * (base_row(l, q, cells, base_in, force_lo, force_hi) + self_weight[l] * design)
            resid.put((l, q), resid_ref, (l, q), left)
            steps.put((0, l, q), steps_ref, (0, l, q), first_scale * left)
    for k in range(SWEEPS - 1):
        for q in range(k + 1, rows - k - 1):
            sweep_row(k, q, loads, weight, resid, steps, resid_ref, steps_ref, shown_to, shown)
    results = [
        pltpu.make_async_copy(shown_to.at[l, pl.ds(1, cells)], shown_ref.at[l], sems.at[len(copies) + l])
        for l in range(loads)
    ]
    for copy in results:
        copy.start()
    for i in range(cells):
        sense_ref[i] = energy_row(i, loads, design_new[DESIGN + i], shown, masks)
    own = design_new.at[pl.ds(DESIGN, cells)]
    spread_totals(tile_ref, filter_total(cells, sense_ref, is_first, is_last, masks), fold_rows(cells, own))
    for copy in results + [own_rows]:
        copy.wait()


def last_moment_kernel(cells, slab, sense, pair_a, pair_b, moment_wide, design_far, passive_far,
                       momentum_ref, kept_ref, before_ref, least_ref, most_ref, sense_wide, momentum_all,
                       kinds, sems):
    even, is_first, is_last = place_of()
    window = pl.ds(pl.multiple_of(lax.axis_index("load") * slab, 8), slab)
    copies = [
        pltpu.make_async_copy(design_far.at[:, window, :], before_ref, sems.at[1]),
        pltpu.make_async_copy(passive_far.at[:, window, :], kinds, sems.at[2]),
    ]
    for copy in copies:
        copy.start()
    shape = sense.shape[1:]
    masks = inner_masks(shape)
    zero = jnp.zeros(shape, jnp.float32)
    sense_wide[0] = jnp.where(is_first, zero, jnp.where(even, pair_a[0], pair_b[0]))
    sense_wide[cells + 1] = jnp.where(is_last, zero, jnp.where(even, pair_b[0], pair_a[0]))
    for i in range(cells):
        sense_wide[i + 1] = sense[i]
    inside, outer = edge_planes(masks)
    for i in range(cells):
        scale = inside
        if i == 0:
            scale = jnp.where(is_first, outer, inside)
        elif i == cells - 1:
            scale = jnp.where(is_last, outer, inside)
        momentum_all[i] = moment_decay * moment_wide[DESIGN + i] + filtered_row(i, sense_wide, masks) * scale
        momentum = momentum_all[i, window, :]
        kept_ref[i] = momentum
    copy = pltpu.make_async_copy(kept_ref, momentum_ref, sems.at[0])
    copy.start()
    for other in copies:
        other.wait()
    for i in range(cells):
        kind = kinds[i]
        least_ref[i] = jnp.where(kind == 2, 1.0, density_floor)
        most_ref[i] = jnp.where(kind == 1, density_floor, 1.0)
    copy.wait()


def last_kernel(cells, total_cells, share, tile_before, tile_in, momentum_ref, before_ref, least_ref, most_ref,
                design_ref, design_near, sems):
    half = tile_in.shape[1] // 2
    along = lax.broadcasted_iota(jnp.int32, tile_in.shape, 1)
    totals = tile_in[...] + jnp.where(along < half, moment_decay * tile_before[...], 0.0)
    rate, pull = rate_and_pull(totals, total_cells, share)
    for i in range(cells):
        moved = before_ref[i] - rate * momentum_ref[i] - pull
        design_near[i] = jnp.minimum(jnp.maximum(moved, least_ref[i]), most_ref[i])
    copy = pltpu.make_async_copy(design_near, design_ref, sems.at[0])
    copy.start()
    copy.wait()


VMEM = pl.BlockSpec(memory_space=pltpu.VMEM)
SMEM = pl.BlockSpec(memory_space=pltpu.SMEM)


def on_core(kernel, operands, scalars, outs, scratch, cost=0, limit=4, far=0, far_outs=0, keep=False):
    anywhere = pl.BlockSpec(memory_space=pl.ANY)
    operands = [
        pltpu.with_memory_space_constraint(operand, pltpu.VMEM)
        if scalars <= i and (i < len(operands) - far or keep) else pltpu.with_memory_space_constraint(operand, pltpu.HBM) if i >= len(operands) - far else operand
        for i, operand in enumerate(operands)
    ]
    return pl.pallas_call(
        kernel,
        out_shape=[
            jax.ShapeDtypeStruct(shape, jnp.float32) if i < far_outs else pltpu.VMEM(shape, jnp.float32)
            for i, shape in enumerate(outs)
        ],
        in_specs=[SMEM] * scalars + [VMEM] * (len(operands) - scalars - far) + [anywhere] * far,
        out_specs=[anywhere] * far_outs + [VMEM] * (len(outs) - far_outs),
        scratch_shapes=[pltpu.VMEM(item, jnp.float32) if isinstance(item, tuple) else item for item in scratch],
        cost_estimate=pl.CostEstimate(flops=cost, bytes_accessed=cost, transcendentals=0) if cost else None,
        compiler_params=pltpu.CompilerParams(vmem_limit_bytes=limit * 1024 * 1024),
    )(*operands)


def passive_apply(design, passive):
    return jnp.where(passive == 1, density_floor, jnp.where(passive == 2, 1.0, design))


def swap(value, axis, bit):
    count = lax.axis_size(axis)
    return lax.ppermute(value, axis, [(i, i ^ bit) for i in range(count)])


def swap_parts(value, count, bit=1):
    return jnp.concatenate([swap(value[i:i + count], "load", bit) for i in range(0, value.shape[0], count)])


def along(value, step):
    count = lax.axis_size("brick")
    pairs = [(i, i + step) for i in range(count) if 0 <= i + step < count]
    return lax.ppermute(value, "brick", pairs)


def both_ways(value):
    count, loads = lax.axis_size("brick"), lax.axis_size("load")
    pairs = []
    for l in range(loads):
        step = 1 if l % 2 == 0 else -1
        pairs += [(l * count + i, l * count + i + step) for i in range(count) if 0 <= i + step < count]
    return lax.ppermute(value, ("load", "brick"), pairs)


def bits_of(count):
    return [1 << k for k in range(count.bit_length() - 1)]


def sum_over(value, axis):
    for bit in bits_of(lax.axis_size(axis)):
        value = value + swap(value, axis, bit)
    return value


def load_terms(value):
    bits = bits_of(lax.axis_size("load"))
    for bit in bits[:-1]:
        value = value + swap(value, "load", bit)
    return value, swap_parts(value, 6, bits[-1])


def after(value, other):
    return lax.optimization_barrier((value, other))[0]


def meet(sense, tiles, width, even, filtered):
    cells = sense.shape[0]
    sense_a, sense_b = load_terms(sense)
    sense = sense_a + sense_b
    edge = lax.dynamic_slice_in_dim(sense, jnp.where(even, cells - width, 0), width, 0)
    pair_a = both_ways(edge)
    tiles = lax.all_to_all(after(tiles, edge), ("load", "brick"), 0, 0, tiled=True)
    pair_b = swap(after(pair_a, tiles), "load", 1)
    return filtered(sense, pair_a, pair_b), tiles


def body(density, passive, support, load_nodes, load_force, self_weight, body_force):
    cells, size_y, size_z = density.shape
    loads = body_force.shape[0]
    load_count, bricks = lax.axis_size("load"), lax.axis_size("brick")
    slab = size_y // load_count
    total_cells = float(cells * bricks * size_y * size_z)
    share = 1.0 / load_count
    even = lax.axis_index("load") % 2 == 0
    plane = (size_y, size_z)
    wide, rows = cells + 2 * DESIGN, cells + 2 * SOURCE
    tile = (load_count * bricks, 2 * size_z)
    shown_shape = (loads, cells + 2) + plane
    resid_shape = (loads, rows) + plane
    steps_shape = (SWEEPS - 1, loads, rows) + plane

    payload, upper, lower = on_core(
        functools.partial(prepare_kernel, cells),
        (density, passive, support, body_force),
        0,
        [(DESIGN + SOURCE,) + plane, (loads, SOURCE) + plane, (loads, SOURCE) + plane],
        [pltpu.VMEM((DESIGN,) + plane, jnp.float32), pltpu.VMEM((DESIGN,) + plane, jnp.int32),
         pltpu.VMEM((SOURCE,) + plane, jnp.int32), pltpu.SemaphoreType.DMA((5,))],
        far=4,
    )
    pair_a = both_ways(payload)
    force_lo = along(upper, 1)
    force_hi = along(lower, -1)
    (base,) = on_core(
        functools.partial(points_kernel, cells, loads),
        (load_nodes, load_force, after(body_force, (upper, lower))),
        2,
        [resid_shape],
        [],
        cost=1,
    )
    pair_b = swap_parts(after(pair_a, base), 3)
    design_wide, weight, inverse, resid, steps, shown = on_core(
        functools.partial(early_kernel, cells, loads),
        (self_weight, density, passive, support, base, pair_a, pair_b),
        1,
        [(wide,) + plane, (6, rows) + plane, (rows,) + plane,
         (loads, cells) + plane, (SWEEPS - 1, loads, cells) + plane, (loads, cells - 2 * (SWEEPS - 1)) + plane],
        [(wide,) + plane, (rows,) + plane, (DESIGN,) + plane, (DESIGN,) + plane],
        cost=1,
    )
    sense, tiles = on_core(
        functools.partial(first_kernel, cells, loads),
        (self_weight, force_lo, force_hi, base, design_wide, weight, inverse, resid, steps, shown),
        1,
        [(cells,) + plane, tile],
        [resid_shape, steps_shape, shown_shape],
    )
    (moment_wide,), tiles_first = meet(
        sense, tiles, SENSE, even,
        lambda *sensed: on_core(
            functools.partial(moment_kernel, cells),
            sensed,
            0,
            [(wide,) + plane],
            [(cells + 2 * SENSE,) + plane],
        ),
    )
    shown, design, sense, tiles = on_core(
        functools.partial(second_kernel, cells, loads, total_cells, share),
        (self_weight, tiles_first, moment_wide, design_wide, base, force_lo, force_hi),
        1,
        [(loads, cells) + plane, (cells,) + plane, (cells,) + plane, tile],
        [(wide,) + plane, (6, rows) + plane, (rows,) + plane, resid_shape, steps_shape, shown_shape, (wide,) + plane,
         resid_shape, (loads, SOURCE) + plane, (loads, SOURCE) + plane,
         pltpu.SemaphoreType.DMA((4 + loads,))],
        limit=14,
        far=3,
        far_outs=2,
        keep=True,
    )
    last_ones, tiles_last = meet(
        sense, tiles, 1, even,
        lambda *sensed: on_core(
            functools.partial(last_moment_kernel, cells, slab),
            sensed + (moment_wide, design, passive),
            0,
            [(cells, slab, size_z)] * 5,
            [(cells + 2,) + plane, (cells,) + plane,
             pltpu.VMEM((cells, slab, size_z), jnp.int32), pltpu.SemaphoreType.DMA((3,))],
            far=2,
            far_outs=1,
        ),
    )
    (design,) = on_core(
        functools.partial(last_kernel, cells, total_cells, share),
        (tiles_first, tiles_last) + tuple(last_ones[1:]),
        0,
        [(cells, slab, size_z)],
        [(cells, slab, size_z), pltpu.SemaphoreType.DMA((1,))],
        far_outs=1,
    )
    return design, last_ones[0], shown


def solution(mesh):
    placed = (
        P("brick", None, None),
        P("brick", None, None),
        P("brick", None, None),
        P("load", None),
        P("load", None),
        P("load"),
        P("load", "brick", None, None),
    )
    return jax.shard_map(
        body,
        mesh=mesh,
        in_specs=placed,
        out_specs=(
            P("brick", "load", None),
            P("brick", "load", None),
            P("load", "brick", None, None),
        ),
        check_vma=False,
    )
```

```python
import functools

import jax
import jax.numpy as jnp
from jax import lax
from jax.experimental import pallas as pl
from jax.experimental.pallas import tpu as pltpu
from jax.sharding import PartitionSpec as P

SWEEPS = 5

stiff_floor = 0.01
mass_shift = 0.1
spectrum_low = 0.05
spectrum_high = 2.0
moment_decay = 0.8
step_size = 0.1
volume_pull = 0.5
volume_target = 0.4
density_floor = 0.001

SOURCE = SWEEPS
DESIGN = SWEEPS + 1
SENSE = SWEEPS + 2


def chebyshev_factors():
    centre = 0.5 * (spectrum_high + spectrum_low)
    half_width = 0.5 * (spectrum_high - spectrum_low)
    ratio_one = centre / half_width
    previous = 1.0 / ratio_one
    factors = []
    for _ in range(SWEEPS - 1):
        current = 1.0 / (2.0 * ratio_one - previous)
        factors.append((current * previous, 2.0 * current / half_width))
        previous = current
    return 1.0 / centre, factors


def shifted(plane):
    size_y, size_z = plane.shape
    return (
        pltpu.roll(plane, 1, 0),
        pltpu.roll(plane, size_y - 1, 0),
        pltpu.roll(plane, 1, 1),
        pltpu.roll(plane, size_z - 1, 1),
    )


def inner_masks(shape):
    along_y = lax.broadcasted_iota(jnp.int32, shape, 0)
    along_z = lax.broadcasted_iota(jnp.int32, shape, 1)
    return (along_y > 0, along_y < shape[0] - 1, along_z > 0, along_z < shape[1] - 1)


def beside_planes(plane, masks):
    return tuple(jnp.where(mask, moved, 0.0) for mask, moved in zip(masks, shifted(plane)))


def edge_planes(masks):
    edges = sum((1.0 - mask.astype(jnp.float32)) for mask in masks)
    return 1.0 / (8.0 - edges), 1.0 / (7.0 - edges)


def stiffness_of(design):
    return stiff_floor + (1.0 - stiff_floor) * (design * design * design)


def weight_row(q, is_free, stiff, weight, inverse, masks):
    here, below, above = stiff[q + 1], stiff[q], stiff[q + 2]
    around = (below, above) + beside_planes(here, masks)
    total = around[0]
    for plane in around[1:]:
        total = total + plane
    diagonal = (3.0 + mass_shift) * here + 0.5 * total
    scale = jnp.where(is_free, 1.0 / diagonal, 0.0)
    inverse[q] = scale
    half = 0.5 * scale
    weight[0, q] = half * (here + below)
    weight[1, q] = half * (here + above)
    for j in range(4):
        weight[2 + j, q] = jnp.where(masks[j], half * (here + around[2 + j]), 0.0)


class Kept:
    def __init__(self):
        self.places = {}

    def put(self, key, ref, index, value):
        ref[index] = value
        self.places[key] = (ref, index)

    def get(self, key):
        ref, index = self.places[key]
        return ref[index]


def sweep_row(k, q, loads, weight, resid, steps, resid_to, steps_to, shown_to, shown, first=0, first_shown=SWEEPS - 1):
    _, factors = chebyshev_factors()
    keep, gain = factors[k]
    last = k == len(factors) - 1
    faces = [weight[j, q] for j in range(6)]
    for l in range(loads):
        here = steps.get((k, l, q))
        total = faces[0] * steps.get((k, l, q - 1)) + faces[1] * steps.get((k, l, q + 1))
        for face, moved in zip(faces[2:], shifted(here)):
            total = total + face * moved
        left = resid.get((l, q)) - here + total
        step = keep * here + gain * left
        if last:
            for earlier in range(k + 1):
                step = step + steps.get((earlier, l, q))
            shown.put((l, q), shown_to, (l, q - first_shown), step)
        else:
            resid.put((l, q), resid_to, (l, q - first), left)
            steps.put((k + 1, l, q), steps_to, (k + 1, l, q - first), step)


def energy_row(i, loads, design, shown, masks):
    q = i + SOURCE
    energy = None
    for l in range(loads):
        here = shown.get((l, q))
        around = (shown.get((l, q - 1)), shown.get((l, q + 1))) + beside_planes(here, masks)
        spread = None
        for plane in around:
            gap = here - plane
            spread = gap * gap if spread is None else spread + gap * gap
        part = mass_shift * (here * here) + 0.25 * spread
        energy = part if energy is None else energy + part
    return (-3.0 * (1.0 - stiff_floor)) * (design * design) * energy


def fold(plane):
    return jnp.sum(plane.reshape(plane.shape[0] // 8, 8, plane.shape[1]), axis=0)


def filter_total(cells, sense, is_first, is_last, masks):
    inside, outer = edge_planes(masks)
    usual = 4.0 * inside + sum(beside_planes(inside, masks))
    at_end = 2.0 * outer + inside + sum(beside_planes(outer, masks))
    zero = jnp.zeros_like(inside)
    total = sense[0]
    for i in range(1, cells):
        total = total + sense[i]
    ends = jnp.where(is_first, sense[0], zero) + jnp.where(is_last, sense[cells - 1], zero)
    nexts = jnp.where(is_first, sense[1], zero) + jnp.where(is_last, sense[cells - 2], zero)
    return -fold(total * usual + ends * (at_end - usual) + nexts * (outer - inside))


def fold_rows(cells, ref):
    total = jnp.abs(ref[0])
    for i in range(1, cells):
        total = total + jnp.abs(ref[i])
    return fold(total)


def place_of():
    brick = lax.axis_index("brick")
    return lax.axis_index("load") % 2 == 0, brick == 0, brick == lax.axis_size("brick") - 1


def prepare_kernel(cells, density, passive, support, force, payload_ref, upper_ref, lower_ref,
                   design_rows, kind_rows, hold_rows, sems):
    even, _, _ = place_of()
    start = jnp.where(even, cells - DESIGN, 0)
    start_mask = jnp.where(even, cells - SOURCE, 0)
    copies = [
        pltpu.make_async_copy(source, target, sems.at[i])
        for i, (source, target) in enumerate((
            (density.at[pl.ds(start, DESIGN)], design_rows),
            (passive.at[pl.ds(start, DESIGN)], kind_rows),
            (support.at[pl.ds(start_mask, SOURCE)], hold_rows),
            (force.at[:, pl.ds(cells - SOURCE, SOURCE)], upper_ref),
            (force.at[:, pl.ds(0, SOURCE)], lower_ref),
        ))
    ]
    for copy in copies:
        copy.start()
    for copy in copies[:3]:
        copy.wait()
    for i in range(DESIGN):
        payload_ref[i] = passive_apply(design_rows[i], kind_rows[i])
    for i in range(SOURCE):
        payload_ref[DESIGN + i] = (1 - hold_rows[i]).astype(jnp.float32)
    for copy in copies[3:]:
        copy.wait()


def points_kernel(cells, loads, nodes, forces, force_ref, base_far, base_ref, sems):
    rows = cells + 2 * SOURCE
    size_y, size_z = base_ref.shape[2:]
    zero = jnp.zeros((size_y, size_z), jnp.float32)
    for l in range(loads):
        for q in range(rows):
            own = SOURCE <= q < SOURCE + cells
            base_ref[l, q] = force_ref[l, q - SOURCE] if own else zero
    first = (lax.axis_index("brick") * cells - SOURCE) * size_y * size_z
    along_z = lax.broadcasted_iota(jnp.int32, (1, size_z), 1)
    for l in range(loads):

        def one_point(p, carry, l=l):
            cell = nodes[l, p] - first

            @pl.when((cell >= 0) & (cell < rows * size_y * size_z))
            def _():
                line, z = cell // size_z, cell % size_z
                q, y = line // size_y, line % size_y
                spot = (l, q, pl.ds(y, 1), slice(None))
                base_ref[spot] = base_ref[spot] + jnp.where(along_z == z, forces[l, p], 0.0)

            return carry

        lax.fori_loop(0, nodes.shape[1], one_point, 0)
    copy = pltpu.make_async_copy(base_ref, base_far, sems.at[0])
    copy.start()
    copy.wait()


def base_row(l, q, cells, base_in, force_lo, force_hi):
    if q < SOURCE:
        return base_in[l, q] + force_lo[l, q]
    if q >= SOURCE + cells:
        return base_in[l, q] + force_hi[l, q - SOURCE - cells]
    return base_in[l, q]


def inner_steps(cells):
    return [range(SOURCE + k, SOURCE + cells - k) for k in range(SWEEPS)]


def early_kernel(cells, loads, self_weight, density, passive, support, base_ref, pair_a, pair_b, pair_c,
                 design_wide, weight, inverse, resid_ref, steps_ref, shown_ref, stiff,
                 free_wide, design_low, design_high):
    even, is_first, is_last = place_of()
    shape = density.shape[1:]
    masks = inner_masks(shape)
    rows = cells + 2 * SOURCE
    zero = jnp.zeros(shape, jnp.float32)
    for i in range(DESIGN):
        low = jnp.where(even, pair_a[i], pair_b[i])
        high = jnp.where(even, pair_b[i], pair_a[i])
        design_low[i] = low
        design_high[i] = high
        stiff[i] = jnp.where(is_first, zero, stiffness_of(low))
        stiff[DESIGN + cells + i] = jnp.where(is_last, zero, stiffness_of(high))
    for i in range(SOURCE):
        low = jnp.where(even, pair_a[DESIGN + i], pair_c[i])
        high = jnp.where(even, pair_c[i], pair_a[DESIGN + i])
        free_wide[i] = jnp.where(is_first, zero, low)
        free_wide[SOURCE + cells + i] = jnp.where(is_last, zero, high)
    for i in range(cells):
        design = passive_apply(density[i], passive[i])
        stiff[DESIGN + i] = stiffness_of(design)
        free_wide[SOURCE + i] = (1 - support[i]).astype(jnp.float32)
        design_wide[DESIGN + i] = jnp.where(support[i] == 0, design, -design)
    for r in range(DESIGN):
        free = free_wide[r - 1] > 0.5 if r > 0 else zero > 0.5
        design_wide[r] = jnp.where(free, design_low[r], -design_low[r])
        q = SOURCE + cells + r
        free = free_wide[q] > 0.5 if q < rows else zero > 0.5
        design_wide[DESIGN + cells + r] = jnp.where(free, design_high[r], -design_high[r])
    for q in range(rows):
        weight_row(q, free_wide[q] > 0.5, stiff, weight, inverse, masks)
    first_scale, _ = chebyshev_factors()
    resid, steps, shown = Kept(), Kept(), Kept()
    inner = inner_steps(cells)
    for q in inner[0]:
        for l in range(loads):
            left = inverse[q] * (base_ref[l, q] + self_weight[l] * jnp.abs(design_wide[q + 1]))
            resid.put((l, q), resid_ref, (l, q - SOURCE), left)
            steps.put((0, l, q), steps_ref, (0, l, q - SOURCE), first_scale * left)
    for k in range(SWEEPS - 1):
        for q in inner[k + 1]:
            sweep_row(
                k, q, loads, weight, resid, steps, resid_ref, steps_ref, shown_ref, shown,
                SOURCE, SOURCE + SWEEPS - 1,
            )


def first_kernel(cells, loads, self_weight, force_lo, force_hi, base_in, design_wide, weight, inverse,
                 resid_in, steps_in, shown_in, lo_far, hi_far, keep, spare, outer, rest, tile_ref,
                 resid_ref, steps_ref, shown_ref, sense_ref, sems):
    copies = [
        pltpu.make_async_copy(source, target, sems.at[i])
        for i, (source, target) in enumerate(((force_lo, lo_far), (force_hi, hi_far)))
    ]
    for copy in copies:
        copy.start()
    even, is_first, is_last = place_of()
    shape = design_wide.shape[1:]
    masks = inner_masks(shape)
    rows = cells + 2 * SOURCE
    first_scale, _ = chebyshev_factors()
    resid, steps, shown = Kept(), Kept(), Kept()
    inner = inner_steps(cells)
    for l in range(loads):
        for k in range(SWEEPS - 1):
            for q in inner[k]:
                steps.places[(k, l, q)] = (steps_in, (k, l, q - SOURCE))
        for q in inner[0]:
            resid.places[(l, q)] = (resid_in, (l, q - SOURCE))
        for q in inner[SWEEPS - 1]:
            shown.places[(l, q)] = (shown_in, (l, q - SOURCE - (SWEEPS - 1)))
    for l in range(loads):
        for q in range(rows):
            if q in inner[0]:
                continue
            base = base_row(l, q, cells, base_in, force_lo, force_hi)
            left = inverse[q] * (base + self_weight[l] * jnp.abs(design_wide[q + 1]))
            resid.put((l, q), resid_ref, (l, q), left)
            steps.put((0, l, q), steps_ref, (0, l, q), first_scale * left)
    for k in range(SWEEPS - 1):
        for q in range(k + 1, rows - k - 1):
            if q not in inner[k + 1]:
                sweep_row(k, q, loads, weight, resid, steps, resid_ref, steps_ref, shown_ref, shown)
    for i in range(cells):
        sense_ref[i] = energy_row(i, loads, design_wide[DESIGN + i], shown, masks)
    cut_rows(cells, even, sense_ref, keep, spare, outer, rest)
    own = design_wide.at[pl.ds(DESIGN, cells)]
    spread_totals(tile_ref, filter_total(cells, sense_ref, is_first, is_last, masks), fold_rows(cells, own))
    for copy in copies:
        copy.wait()


def cut_rows(cells, even, sense, keep, spare, outer, rest):
    width = keep.shape[0]
    for i in range(width):
        first, last = sense[i], sense[cells - width + i]
        keep[i] = jnp.where(even, last, first)
        outer[i] = jnp.where(even, first, last)
    for i in range(cells - width):
        first, last = sense[i], sense[width + i]
        spare[i] = jnp.where(even, first, last)
        rest[i] = jnp.where(even, last, first)


def whole_row(i, cells, even, edge, spare, rest):
    width = edge.shape[0]
    if_even = spare[i] + rest[i] if i < cells - width else edge[i - (cells - width)]
    if_odd = edge[i] if i < width else spare[i - width] + rest[i - width]
    return jnp.where(even, if_even, if_odd)


def moment_kernel(cells, edge, spare, rest, pair_a, pair_b, moment_ref, sense_wide):
    even, is_first, is_last = place_of()
    shape = edge.shape[1:]
    masks = inner_masks(shape)
    zero = jnp.zeros(shape, jnp.float32)
    for i in range(SENSE):
        low = jnp.where(even, pair_a[i], pair_b[i])
        high = jnp.where(even, pair_b[i], pair_a[i])
        sense_wide[i] = jnp.where(is_first, zero, low)
        sense_wide[SENSE + cells + i] = jnp.where(is_last, zero, high)
    for i in range(cells):
        sense_wide[SENSE + i] = whole_row(i, cells, even, edge, spare, rest)
    inside, at_ends = edge_planes(masks)
    for r in range(cells + 2 * DESIGN):
        at_end = (is_first & (r == DESIGN)) | (is_last & (r == DESIGN + cells - 1))
        moment_ref[r] = filtered_row(r, sense_wide, masks) * jnp.where(at_end, at_ends, inside)


def filtered_row(r, sense_wide, masks):
    here = sense_wide[r + 1]
    total = 2.0 * here + sense_wide[r] + sense_wide[r + 2]
    for plane in beside_planes(here, masks):
        total = total + plane
    return total


def spread_totals(tile_ref, abs_tile, density_tile):
    row = jnp.concatenate([jnp.sum(tile, axis=0, keepdims=True) for tile in (abs_tile, density_tile)], axis=1)
    tile_ref[...] = jnp.broadcast_to(row[None], tile_ref.shape)


def totals_kernel(total_cells, share, decay, tile_in, before, total_ref):
    half = tile_in.shape[2] // 2
    totals = jnp.sum(tile_in[...], axis=0)
    abs_total = jnp.sum(totals[:, :half], keepdims=True)
    if decay:
        abs_total = abs_total + decay * before[2:3, :1]
    density_total = jnp.sum(totals[:, half:], keepdims=True) * share
    rate = step_size / (abs_total / total_cells + 1e-6)
    pull = volume_pull * (density_total / total_cells - volume_target)
    row = lax.broadcasted_iota(jnp.int32, total_ref.shape, 0)
    total_ref[...] = jnp.where(row == 0, rate, jnp.where(row == 1, pull, abs_total))


def second_kernel(cells, loads, self_weight, step_ref, moment_wide,
                  design_wide, base_far, lo_far, hi_far,
                  shown_ref, design_out, keep, spare, outer, rest, tile_ref,
                  stiff, weight, inverse, resid_ref, steps_ref, shown_to, design_new,
                  base_in, force_lo, force_hi, sense_ref, sems):
    copies = [
        pltpu.make_async_copy(source, target, sems.at[i])
        for i, (source, target) in enumerate(((base_far, base_in), (lo_far, force_lo), (hi_far, force_hi)))
    ]
    for copy in copies:
        copy.start()
    even, is_first, is_last = place_of()
    shape = moment_wide.shape[1:]
    masks = inner_masks(shape)
    wide = cells + 2 * DESIGN
    rows = cells + 2 * SOURCE
    zero = jnp.zeros(shape, jnp.float32)
    rate, pull = step_ref[0:1, :], step_ref[1:2, :]
    for r in range(wide):
        signed = design_wide[r]
        before = jnp.abs(signed)
        moved = jnp.clip(before - rate * moment_wide[r] - pull, density_floor, 1.0)
        fixed = (before == density_floor) | (before == 1.0)
        design = jnp.where(fixed, before, moved)
        design_new[r] = design
        stiffness = stiffness_of(design)
        if r < DESIGN:
            stiff[r] = jnp.where(is_first, zero, stiffness)
        elif r >= DESIGN + cells:
            stiff[r] = jnp.where(is_last, zero, stiffness)
        else:
            stiff[r] = stiffness
    own_rows = pltpu.make_async_copy(design_new.at[pl.ds(DESIGN, cells)], design_out, sems.at[len(copies) + loads])
    own_rows.start()
    resid, steps, shown = Kept(), Kept(), Kept()
    first_scale, _ = chebyshev_factors()
    for q in range(rows):
        weight_row(q, design_wide[q + 1] > 0.0, stiff, weight, inverse, masks)
    for copy in copies:
        copy.wait()
    for q in range(rows):
        scale, design = inverse[q], design_new[q + 1]
        for l in range(loads):
            left = scale * (base_row(l, q, cells, base_in, force_lo, force_hi) + self_weight[l] * design)
            resid.put((l, q), resid_ref, (l, q), left)
            steps.put((0, l, q), steps_ref, (0, l, q), first_scale * left)
    for k in range(SWEEPS - 1):
        for q in range(k + 1, rows - k - 1):
            sweep_row(k, q, loads, weight, resid, steps, resid_ref, steps_ref, shown_to, shown)
    results = [
        pltpu.make_async_copy(shown_to.at[l, pl.ds(1, cells)], shown_ref.at[l], sems.at[len(copies) + l])
        for l in range(loads)
    ]
    for copy in results:
        copy.start()
    for i in range(cells):
        sense_ref[i] = energy_row(i, loads, design_new[DESIGN + i], shown, masks)
    cut_rows(cells, even, sense_ref, keep, spare, outer, rest)
    own = design_new.at[pl.ds(DESIGN, cells)]
    spread_totals(tile_ref, filter_total(cells, sense_ref, is_first, is_last, masks), fold_rows(cells, own))
    for copy in results + [own_rows]:
        copy.wait()


def last_moment_kernel(cells, slab, edge, spare, rest, pair_a, pair_b, moment_wide, design_far, passive_far,
                       momentum_ref, kept_ref, before_ref, least_ref, most_ref, sense_wide, momentum_all,
                       kinds, sems):
    even, is_first, is_last = place_of()
    window = pl.ds(pl.multiple_of(lax.axis_index("load") * slab, 8), slab)
    copies = [
        pltpu.make_async_copy(design_far.at[:, window, :], before_ref, sems.at[1]),
        pltpu.make_async_copy(passive_far.at[:, window, :], kinds, sems.at[2]),
    ]
    for copy in copies:
        copy.start()
    shape = edge.shape[1:]
    masks = inner_masks(shape)
    zero = jnp.zeros(shape, jnp.float32)
    sense_wide[0] = jnp.where(is_first, zero, jnp.where(even, pair_a[0], pair_b[0]))
    sense_wide[cells + 1] = jnp.where(is_last, zero, jnp.where(even, pair_b[0], pair_a[0]))
    for i in range(cells):
        sense_wide[i + 1] = whole_row(i, cells, even, edge, spare, rest)
    inside, at_ends = edge_planes(masks)
    for i in range(cells):
        scale = inside
        if i == 0:
            scale = jnp.where(is_first, at_ends, inside)
        elif i == cells - 1:
            scale = jnp.where(is_last, at_ends, inside)
        momentum_all[i] = moment_decay * moment_wide[DESIGN + i] + filtered_row(i, sense_wide, masks) * scale
        momentum = momentum_all[i, window, :]
        kept_ref[i] = momentum
    copy = pltpu.make_async_copy(kept_ref, momentum_ref, sems.at[0])
    copy.start()
    for other in copies:
        other.wait()
    for i in range(cells):
        kind = kinds[i]
        least_ref[i] = jnp.where(kind == 2, 1.0, density_floor)
        most_ref[i] = jnp.where(kind == 1, density_floor, 1.0)
    copy.wait()


def last_kernel(cells, step_ref, momentum_ref, before_ref, least_ref, most_ref, design_ref, design_near, sems):
    rate, pull = step_ref[0:1, :], step_ref[1:2, :]
    for i in range(cells):
        moved = before_ref[i] - rate * momentum_ref[i] - pull
        design_near[i] = jnp.minimum(jnp.maximum(moved, least_ref[i]), most_ref[i])
    copy = pltpu.make_async_copy(design_near, design_ref, sems.at[0])
    copy.start()
    copy.wait()


VMEM = pl.BlockSpec(memory_space=pltpu.VMEM)
SMEM = pl.BlockSpec(memory_space=pltpu.SMEM)


def on_core(kernel, operands, scalars, outs, scratch, cost=0, limit=4, far=0, far_outs=0):
    anywhere = pl.BlockSpec(memory_space=pl.ANY)
    operands = [
        pltpu.with_memory_space_constraint(operand, pltpu.VMEM)
        if scalars <= i < len(operands) - far else pltpu.with_memory_space_constraint(operand, pltpu.HBM) if i >= len(operands) - far else operand
        for i, operand in enumerate(operands)
    ]
    return pl.pallas_call(
        kernel,
        out_shape=[
            pltpu.HBM(shape, jnp.float32) if i < far_outs else pltpu.VMEM(shape, jnp.float32)
            for i, shape in enumerate(outs)
        ],
        in_specs=[SMEM] * scalars + [VMEM] * (len(operands) - scalars - far) + [anywhere] * far,
        out_specs=[anywhere] * far_outs + [VMEM] * (len(outs) - far_outs),
        scratch_shapes=[pltpu.VMEM(item, jnp.float32) if isinstance(item, tuple) else item for item in scratch],
        cost_estimate=pl.CostEstimate(flops=cost, bytes_accessed=cost, transcendentals=0) if cost else None,
        compiler_params=pltpu.CompilerParams(vmem_limit_bytes=limit * 1024 * 1024),
    )(*operands)


def passive_apply(design, passive):
    return jnp.where(passive == 1, density_floor, jnp.where(passive == 2, 1.0, design))


def swap(value, axis, bit):
    count = lax.axis_size(axis)
    return lax.ppermute(value, axis, [(i, i ^ bit) for i in range(count)])


def along(value, step):
    count = lax.axis_size("brick")
    pairs = [(i, i + step) for i in range(count) if 0 <= i + step < count]
    return lax.ppermute(value, "brick", pairs)


def both_ways(value):
    count, loads = lax.axis_size("brick"), lax.axis_size("load")
    pairs = []
    for l in range(loads):
        step = 1 if l % 2 == 0 else -1
        pairs += [(l * count + i, l * count + i + step) for i in range(count) if 0 <= i + step < count]
    return lax.ppermute(value, ("load", "brick"), pairs)


def bits_of(count):
    return [1 << k for k in range(count.bit_length() - 1)]


def sum_over(value, axis):
    for bit in bits_of(lax.axis_size(axis)):
        value = value + swap(value, axis, bit)
    return value


def after(value, other):
    return lax.optimization_barrier((value, other))[0]


def add_kernel(first, second, sum_ref):
    sum_ref[...] = first[...] + second[...]


def meet(parts, tiles, filtered, totals):
    total = totals(lax.all_to_all(tiles, ("load", "brick"), 0, 0, tiled=True))
    for bit in bits_of(lax.axis_size("load"))[1:]:
        parts = [part + swap(part, "load", bit) for part in parts]
    keep, spare, outer, rest = parts
    (edge,) = on_core(add_kernel, (keep, swap(outer, "load", 1)), 0, [keep.shape], [])
    pair_a = both_ways(edge)
    rest = swap(rest, "load", 1)
    pair_b = swap(pair_a, "load", 1)
    return filtered(edge, spare, rest, pair_a, pair_b), total


def body(density, passive, support, load_nodes, load_force, self_weight, body_force):
    cells, size_y, size_z = density.shape
    loads = body_force.shape[0]
    load_count, bricks = lax.axis_size("load"), lax.axis_size("brick")
    slab = size_y // load_count
    total_cells = float(cells * bricks * size_y * size_z)
    share = 1.0 / load_count
    plane = (size_y, size_z)
    wide, rows = cells + 2 * DESIGN, cells + 2 * SOURCE
    tile = (load_count * bricks, 1, 2 * size_z)
    shown_shape = (loads, cells + 2) + plane
    resid_shape = (loads, rows) + plane
    steps_shape = (SWEEPS - 1, loads, rows) + plane

    def parts_of(width):
        return [(count,) + plane for count in (width, cells - width, width, cells - width)]

    payload, upper, lower = on_core(
        functools.partial(prepare_kernel, cells),
        (density, passive, support, body_force),
        0,
        [(DESIGN + SOURCE,) + plane, (loads, SOURCE) + plane, (loads, SOURCE) + plane],
        [pltpu.VMEM((DESIGN,) + plane, jnp.float32), pltpu.VMEM((DESIGN,) + plane, jnp.int32),
         pltpu.VMEM((SOURCE,) + plane, jnp.int32), pltpu.SemaphoreType.DMA((5,))],
        far=4,
    )
    pair_a = both_ways(payload)
    force_lo = along(upper, 1)
    force_hi = along(lower, -1)
    base_far, base = on_core(
        functools.partial(points_kernel, cells, loads),
        (load_nodes, load_force, after(body_force, (upper, lower))),
        2,
        [resid_shape, resid_shape],
        [pltpu.SemaphoreType.DMA((1,))],
        cost=1,
        far_outs=1,
    )
    pair_a = after(pair_a, base)
    pair_b = swap(pair_a[:DESIGN], "load", 1)
    pair_c = swap(pair_a[DESIGN:], "load", 1)
    design_wide, weight, inverse, resid, steps, shown = on_core(
        functools.partial(early_kernel, cells, loads),
        (self_weight, density, passive, support, base, pair_a, pair_b, pair_c),
        1,
        [(wide,) + plane, (6, rows) + plane, (rows,) + plane,
         (loads, cells) + plane, (SWEEPS - 1, loads, cells) + plane, (loads, cells - 2 * (SWEEPS - 1)) + plane],
        [(wide,) + plane, (rows,) + plane, (DESIGN,) + plane, (DESIGN,) + plane],
        cost=1,
    )
    lo_far, hi_far, *parts, tiles = on_core(
        functools.partial(first_kernel, cells, loads),
        (self_weight, force_lo, force_hi, base, design_wide, weight, inverse, resid, steps, shown),
        1,
        [(loads, SOURCE) + plane] * 2 + parts_of(SENSE) + [tile],
        [resid_shape, steps_shape, shown_shape, (cells,) + plane, pltpu.SemaphoreType.DMA((2,))],
        far_outs=2,
    )
    def totals(decay, before):
        return lambda tiles: on_core(
            functools.partial(totals_kernel, total_cells, share, decay),
            (tiles, before),
            0,
            [(8, size_z)],
            [],
            cost=2000000000,
        )[0]

    (moment_wide,), step_first = meet(
        parts, tiles,
        lambda *sensed: on_core(
            functools.partial(moment_kernel, cells),
            sensed,
            0,
            [(wide,) + plane],
            [(cells + 2 * SENSE,) + plane],
        ),
        totals(0.0, tiles),
    )
    shown, design, *parts, tiles = on_core(
        functools.partial(second_kernel, cells, loads),
        (self_weight, step_first, moment_wide, design_wide, base_far, lo_far, hi_far),
        1,
        [(loads, cells) + plane, (cells,) + plane] + parts_of(1) + [tile],
        [(wide,) + plane, (6, rows) + plane, (rows,) + plane, resid_shape, steps_shape, shown_shape, (wide,) + plane,
         resid_shape, (loads, SOURCE) + plane, (loads, SOURCE) + plane, (cells,) + plane,
         pltpu.SemaphoreType.DMA((4 + loads,))],
        limit=14,
        far=3,
        far_outs=2,
    )
    last_ones, step_last = meet(
        parts, tiles,
        lambda *sensed: on_core(
            functools.partial(last_moment_kernel, cells, slab),
            sensed + (moment_wide, design, passive),
            0,
            [(cells, slab, size_z)] * 5,
            [(cells + 2,) + plane, (cells,) + plane,
             pltpu.VMEM((cells, slab, size_z), jnp.int32), pltpu.SemaphoreType.DMA((3,))],
            far=2,
            far_outs=1,
        ),
        totals(moment_decay, step_first),
    )
    (design,) = on_core(
        functools.partial(last_kernel, cells),
        (step_last,) + tuple(last_ones[1:]),
        0,
        [(cells, slab, size_z)],
        [(cells, slab, size_z), pltpu.SemaphoreType.DMA((1,))],
        far_outs=1,
    )
    return design, last_ones[0], shown


def solution(mesh):
    placed = (
        P("brick", None, None),
        P("brick", None, None),
        P("brick", None, None),
        P("load", None),
        P("load", None),
        P("load"),
        P("load", "brick", None, None),
    )
    return jax.shard_map(
        body,
        mesh=mesh,
        in_specs=placed,
        out_specs=(
            P("brick", "load", None),
            P("brick", "load", None),
            P("load", "brick", None, None),
        ),
        check_vma=False,
    )
```

```python
import functools

import jax
import jax.numpy as jnp
from jax import lax
from jax.experimental import pallas as pl
from jax.experimental.pallas import tpu as pltpu
from jax.sharding import PartitionSpec as P

SWEEPS = 5

stiff_floor = 0.01
mass_shift = 0.1
spectrum_low = 0.05
spectrum_high = 2.0
moment_decay = 0.8
step_size = 0.1
volume_pull = 0.5
volume_target = 0.4
density_floor = 0.001

SOURCE = SWEEPS
DESIGN = SWEEPS + 1
SENSE = SWEEPS + 2


def chebyshev_factors():
    centre = 0.5 * (spectrum_high + spectrum_low)
    half_width = 0.5 * (spectrum_high - spectrum_low)
    ratio_one = centre / half_width
    previous = 1.0 / ratio_one
    factors = []
    for _ in range(SWEEPS - 1):
        current = 1.0 / (2.0 * ratio_one - previous)
        factors.append((current * previous, 2.0 * current / half_width))
        previous = current
    return 1.0 / centre, factors


def shifted(plane):
    size_y, size_z = plane.shape
    return (
        pltpu.roll(plane, 1, 0),
        pltpu.roll(plane, size_y - 1, 0),
        pltpu.roll(plane, 1, 1),
        pltpu.roll(plane, size_z - 1, 1),
    )


def inner_masks(shape):
    along_y = lax.broadcasted_iota(jnp.int32, shape, 0)
    along_z = lax.broadcasted_iota(jnp.int32, shape, 1)
    return (along_y > 0, along_y < shape[0] - 1, along_z > 0, along_z < shape[1] - 1)


def beside_planes(plane, masks):
    return tuple(jnp.where(mask, moved, 0.0) for mask, moved in zip(masks, shifted(plane)))


def edge_planes(masks):
    edges = sum((1.0 - mask.astype(jnp.float32)) for mask in masks)
    return 1.0 / (8.0 - edges), 1.0 / (7.0 - edges)


def stiffness_of(design):
    return stiff_floor + (1.0 - stiff_floor) * (design * design * design)


class Kept:
    def __init__(self):
        self.places = {}

    def put(self, key, ref, index, value):
        ref[index] = value
        self.places[key] = (ref, index)

    def get(self, key):
        ref, index = self.places[key]
        return ref[index]


def weight_row(q, is_free, stiff, weight, inverse, weight_to, inverse_to, place, masks):
    here, below, above = stiff[q + 1], stiff[q], stiff[q + 2]
    around = (below, above) + beside_planes(here, masks)
    total = around[0]
    for plane in around[1:]:
        total = total + plane
    diagonal = (3.0 + mass_shift) * here + 0.5 * total
    scale = jnp.where(is_free, 1.0 / diagonal, 0.0)
    inverse.put(q, inverse_to, place, scale)
    half = 0.5 * scale
    weight.put((0, q), weight_to, (0, place), half * (here + below))
    weight.put((1, q), weight_to, (1, place), half * (here + above))
    for j in range(4):
        weight.put((2 + j, q), weight_to, (2 + j, place), jnp.where(masks[j], half * (here + around[2 + j]), 0.0))


def sweep_row(k, q, loads, weight, resid, steps, resid_to, steps_to, shown_to, shown, first=0, first_shown=SWEEPS - 1):
    _, factors = chebyshev_factors()
    keep, gain = factors[k]
    last = k == len(factors) - 1
    faces = [weight.get((j, q)) for j in range(6)]
    for l in range(loads):
        here = steps.get((k, l, q))
        total = faces[0] * steps.get((k, l, q - 1)) + faces[1] * steps.get((k, l, q + 1))
        for face, moved in zip(faces[2:], shifted(here)):
            total = total + face * moved
        left = resid.get((l, q)) - here + total
        step = keep * here + gain * left
        if last:
            for earlier in range(k + 1):
                step = step + steps.get((earlier, l, q))
            shown.put((l, q), shown_to, (l, q - first_shown), step)
        else:
            resid.put((l, q), resid_to, (l, q - first), left)
            steps.put((k + 1, l, q), steps_to, (k + 1, l, q - first), step)


def energy_row(i, loads, design, shown, masks):
    q = i + SOURCE
    energy = None
    for l in range(loads):
        here = shown.get((l, q))
        around = (shown.get((l, q - 1)), shown.get((l, q + 1))) + beside_planes(here, masks)
        spread = None
        for plane in around:
            gap = here - plane
            spread = gap * gap if spread is None else spread + gap * gap
        part = mass_shift * (here * here) + 0.25 * spread
        energy = part if energy is None else energy + part
    return (-3.0 * (1.0 - stiff_floor)) * (design * design) * energy


def fold(plane):
    return jnp.sum(plane.reshape(plane.shape[0] // 8, 8, plane.shape[1]), axis=0)


def filter_total(cells, sense, is_first, is_last, masks):
    inside, outer = edge_planes(masks)
    usual = 4.0 * inside + sum(beside_planes(inside, masks))
    at_end = 2.0 * outer + inside + sum(beside_planes(outer, masks))
    zero = jnp.zeros_like(inside)
    total = sense[0]
    for i in range(1, cells):
        total = total + sense[i]
    ends = jnp.where(is_first, sense[0], zero) + jnp.where(is_last, sense[cells - 1], zero)
    nexts = jnp.where(is_first, sense[1], zero) + jnp.where(is_last, sense[cells - 2], zero)
    return -fold(total * usual + ends * (at_end - usual) + nexts * (outer - inside))


def fold_rows(cells, ref):
    total = jnp.abs(ref[0])
    for i in range(1, cells):
        total = total + jnp.abs(ref[i])
    return fold(total)


def place_of():
    brick = lax.axis_index("brick")
    return lax.axis_index("load") % 2 == 0, brick == 0, brick == lax.axis_size("brick") - 1


def prepare_kernel(cells, density, passive, support, force, payload_ref, upper_ref, lower_ref,
                   design_rows, kind_rows, hold_rows, sems):
    even, _, _ = place_of()
    start = jnp.where(even, cells - DESIGN, 0)
    start_mask = jnp.where(even, cells - SOURCE, 0)
    copies = [
        pltpu.make_async_copy(source, target, sems.at[i])
        for i, (source, target) in enumerate((
            (density.at[pl.ds(start, DESIGN)], design_rows),
            (passive.at[pl.ds(start, DESIGN)], kind_rows),
            (support.at[pl.ds(start_mask, SOURCE)], hold_rows),
            (force.at[:, pl.ds(cells - SOURCE, SOURCE)], upper_ref),
            (force.at[:, pl.ds(0, SOURCE)], lower_ref),
        ))
    ]
    for copy in copies:
        copy.start()
    for copy in copies[:3]:
        copy.wait()
    for i in range(DESIGN):
        payload_ref[i] = passive_apply(design_rows[i], kind_rows[i])
    for i in range(SOURCE):
        payload_ref[DESIGN + i] = (1 - hold_rows[i]).astype(jnp.float32)
    for copy in copies[3:]:
        copy.wait()


def points_kernel(cells, loads, nodes, forces, force_ref, base_far, base_ref, sems):
    rows = cells + 2 * SOURCE
    size_y, size_z = base_ref.shape[2:]
    zero = jnp.zeros((size_y, size_z), jnp.float32)
    for l in range(loads):
        for q in range(rows):
            own = SOURCE <= q < SOURCE + cells
            base_ref[l, q] = force_ref[l, q - SOURCE] if own else zero
    first = (lax.axis_index("brick") * cells - SOURCE) * size_y * size_z
    along_z = lax.broadcasted_iota(jnp.int32, (1, size_z), 1)
    for l in range(loads):

        def one_point(p, carry, l=l):
            cell = nodes[l, p] - first

            @pl.when((cell >= 0) & (cell < rows * size_y * size_z))
            def _():
                line, z = cell // size_z, cell % size_z
                q, y = line // size_y, line % size_y
                spot = (l, q, pl.ds(y, 1), slice(None))
                base_ref[spot] = base_ref[spot] + jnp.where(along_z == z, forces[l, p], 0.0)

            return carry

        lax.fori_loop(0, nodes.shape[1], one_point, 0)
    copy = pltpu.make_async_copy(base_ref, base_far, sems.at[0])
    copy.start()
    copy.wait()


def base_row(l, q, cells, base_in, force_lo, force_hi):
    if q < SOURCE:
        return base_in[l, q] + force_lo[l, q]
    if q >= SOURCE + cells:
        return base_in[l, q] + force_hi[l, q - SOURCE - cells]
    return base_in[l, q]


def inner_steps(cells, margin):
    return [range(SOURCE + margin + k, SOURCE + cells - margin - k) for k in range(SWEEPS)]


def outer_place(q, cells):
    return q if q <= SOURCE else q - (cells - 2)


def start_row(q, base, design, self_weight, inverse, resid, steps, resid_to, steps_to, first):
    first_scale, _ = chebyshev_factors()
    for l, one in enumerate(base):
        left = inverse.get(q) * (one + self_weight[l] * design)
        resid.put((l, q), resid_to, (l, q - first), left)
        steps.put((0, l, q), steps_to, (0, l, q - first), first_scale * left)


def inner_places(cells, loads, near, early):
    weight, inverse, resid, steps, shown = Kept(), Kept(), Kept(), Kept(), Kept()
    rows = cells + 2 * SOURCE
    near_rows, early_rows = inner_steps(cells, 1), inner_steps(cells, 0)
    for q in range(rows):
        inside = q in near_rows[0]
        if not inside and early is None:
            continue
        place = q - SOURCE if inside else outer_place(q, cells)
        weights, inverses = (near if inside else early)[:2]
        inverse.places[q] = (inverses, place)
        for j in range(6):
            weight.places[(j, q)] = (weights, (j, place))
    for refs, ranges in ((early, early_rows), (near, near_rows)):
        if refs is None:
            continue
        for l in range(loads):
            for k in range(SWEEPS - 1):
                for q in ranges[k]:
                    steps.places[(k, l, q)] = (refs[3], (k, l, q - SOURCE))
            for q in ranges[SWEEPS - 1]:
                shown.places[(l, q)] = (refs[4], (l, q - SOURCE - (SWEEPS - 1)))
    for l in range(loads):
        for q in early_rows[0]:
            depth = min(q - SOURCE, SOURCE + cells - 1 - q)
            at_early = early is not None and depth < SWEEPS - 1
            if at_early or q in near_rows[0]:
                resid.places[(l, q)] = ((early if at_early else near)[2], (l, q - SOURCE))
    return weight, inverse, resid, steps, shown


def own_kernel(cells, loads, self_weight, density, passive, support, base_ref,
               design_own, stiff, weight_ref, inverse_ref, resid_ref, steps_ref, shown_ref, stiff_wide):
    masks = inner_masks(density.shape[1:])
    weight, inverse, resid, steps, shown = Kept(), Kept(), Kept(), Kept(), Kept()
    for i in range(cells):
        design = passive_apply(density[i], passive[i])
        stiffness = stiffness_of(design)
        stiff[i] = stiffness
        stiff_wide[DESIGN + i] = stiffness
        design_own[i] = jnp.where(support[i] == 0, design, -design)
    inner = inner_steps(cells, 1)
    for q in inner[0]:
        i = q - SOURCE
        weight_row(q, support[i] == 0, stiff_wide, weight, inverse, weight_ref, inverse_ref, i, masks)
        base = [base_ref[l, q] for l in range(loads)]
        start_row(q, base, jnp.abs(design_own[i]), self_weight, inverse, resid, steps, resid_ref, steps_ref, SOURCE)
    for k in range(SWEEPS - 1):
        for q in inner[k + 1]:
            sweep_row(
                k, q, loads, weight, resid, steps, resid_ref, steps_ref, shown_ref, shown,
                SOURCE, SOURCE + SWEEPS - 1,
            )


def early_kernel(cells, loads, self_weight, base_ref, pair_a, pair_b, pair_c, design_own, stiff_own,
                 near_weight, near_inverse, near_resid, near_steps, near_shown,
                 design_wide, weight_ref, inverse_ref, resid_ref, steps_ref, shown_ref, stiff):
    even, is_first, is_last = place_of()
    shape = design_own.shape[1:]
    masks = inner_masks(shape)
    zero = jnp.zeros(shape, jnp.float32)
    weight, inverse, resid, steps, shown = inner_places(
        cells, loads, (near_weight, near_inverse, near_resid, near_steps, near_shown), None
    )
    for i in range(DESIGN):
        low = jnp.where(even, pair_a[i], pair_b[i])
        high = jnp.where(even, pair_b[i], pair_a[i])
        stiff[i] = jnp.where(is_first, zero, stiffness_of(low))
        stiff[DESIGN + cells + i] = jnp.where(is_last, zero, stiffness_of(high))
        below, above = i - 1, i
        if below >= 0:
            free = jnp.where(even, pair_a[DESIGN + below], pair_c[below])
            low = jnp.where((free > 0.5) & jnp.logical_not(is_first), low, -low)
        else:
            low = -low
        if above < SOURCE:
            free = jnp.where(even, pair_c[above], pair_a[DESIGN + above])
            high = jnp.where((free > 0.5) & jnp.logical_not(is_last), high, -high)
        else:
            high = -high
        design_wide[i] = low
        design_wide[DESIGN + cells + i] = high
    for i in range(cells):
        design_wide[DESIGN + i] = design_own[i]
        stiff[DESIGN + i] = stiff_own[i]
    near, inner = inner_steps(cells, 1), inner_steps(cells, 0)
    for q in range(cells + 2 * SOURCE):
        if q not in near[0]:
            weight_row(
                q, design_wide[q + 1] > 0.0, stiff, weight, inverse, weight_ref, inverse_ref, outer_place(q, cells), masks
            )
    for q in inner[0]:
        if q not in near[0]:
            base = [base_ref[l, q] for l in range(loads)]
            design = jnp.abs(design_wide[q + 1])
            start_row(q, base, design, self_weight, inverse, resid, steps, resid_ref, steps_ref, SOURCE)
    for k in range(SWEEPS - 1):
        for q in inner[k + 1]:
            if q not in near[k + 1]:
                sweep_row(
                    k, q, loads, weight, resid, steps, resid_ref, steps_ref, shown_ref, shown,
                    SOURCE, SOURCE + SWEEPS - 1,
                )


def first_kernel(cells, loads, self_weight, force_lo, force_hi, base_in, design_wide,
                 near_weight, near_inverse, near_resid, near_steps, near_shown,
                 early_weight, early_inverse, early_resid, early_steps, early_shown,
                 lo_far, hi_far, keep, spare, outer, rest, tile_ref,
                 resid_ref, steps_ref, shown_ref, sense_ref, sems):
    copies = [
        pltpu.make_async_copy(source, target, sems.at[i])
        for i, (source, target) in enumerate(((force_lo, lo_far), (force_hi, hi_far)))
    ]
    for copy in copies:
        copy.start()
    even, is_first, is_last = place_of()
    shape = design_wide.shape[1:]
    masks = inner_masks(shape)
    rows = cells + 2 * SOURCE
    weight, inverse, resid, steps, shown = inner_places(
        cells, loads, (near_weight, near_inverse, near_resid, near_steps, near_shown),
        (early_weight, early_inverse, early_resid, early_steps, early_shown),
    )
    inner = inner_steps(cells, 0)
    for q in range(rows):
        if q not in inner[0]:
            base = [base_row(l, q, cells, base_in, force_lo, force_hi) for l in range(loads)]
            design = jnp.abs(design_wide[q + 1])
            start_row(q, base, design, self_weight, inverse, resid, steps, resid_ref, steps_ref, 0)
    for k in range(SWEEPS - 1):
        for q in range(k + 1, rows - k - 1):
            if q not in inner[k + 1]:
                sweep_row(k, q, loads, weight, resid, steps, resid_ref, steps_ref, shown_ref, shown)
    for i in range(cells):
        sense_ref[i] = energy_row(i, loads, design_wide[DESIGN + i], shown, masks)
    cut_rows(cells, even, sense_ref, keep, spare, outer, rest)
    own = design_wide.at[pl.ds(DESIGN, cells)]
    spread_totals(tile_ref, filter_total(cells, sense_ref, is_first, is_last, masks), fold_rows(cells, own))
    for copy in copies:
        copy.wait()


def cut_rows(cells, even, sense, keep, spare, outer, rest):
    width = keep.shape[0]
    for i in range(width):
        first, last = sense[i], sense[cells - width + i]
        keep[i] = jnp.where(even, last, first)
        outer[i] = jnp.where(even, first, last)
    for i in range(cells - width):
        first, last = sense[i], sense[width + i]
        spare[i] = jnp.where(even, first, last)
        rest[i] = jnp.where(even, last, first)


def whole_row(i, cells, even, edge, spare, rest):
    width = edge.shape[0]
    if_even = spare[i] + rest[i] if i < cells - width else edge[i - (cells - width)]
    if_odd = edge[i] if i < width else spare[i - width] + rest[i - width]
    return jnp.where(even, if_even, if_odd)


def moment_kernel(cells, edge, spare, rest, pair_a, pair_b, moment_ref, sense_wide):
    even, is_first, is_last = place_of()
    shape = edge.shape[1:]
    masks = inner_masks(shape)
    zero = jnp.zeros(shape, jnp.float32)
    for i in range(SENSE):
        low = jnp.where(even, pair_a[i], pair_b[i])
        high = jnp.where(even, pair_b[i], pair_a[i])
        sense_wide[i] = jnp.where(is_first, zero, low)
        sense_wide[SENSE + cells + i] = jnp.where(is_last, zero, high)
    for i in range(cells):
        sense_wide[SENSE + i] = whole_row(i, cells, even, edge, spare, rest)
    inside, at_ends = edge_planes(masks)
    for r in range(cells + 2 * DESIGN):
        at_end = (is_first & (r == DESIGN)) | (is_last & (r == DESIGN + cells - 1))
        moment_ref[r] = filtered_row(r, sense_wide, masks) * jnp.where(at_end, at_ends, inside)


def filtered_row(r, sense_wide, masks):
    here = sense_wide[r + 1]
    total = 2.0 * here + sense_wide[r] + sense_wide[r + 2]
    for plane in beside_planes(here, masks):
        total = total + plane
    return total


def spread_totals(tile_ref, abs_tile, density_tile):
    row = jnp.concatenate([jnp.sum(tile, axis=0, keepdims=True) for tile in (abs_tile, density_tile)], axis=1)
    tile_ref[...] = jnp.broadcast_to(row[None], tile_ref.shape)


def totals_kernel(total_cells, share, decay, tile_in, before, total_ref):
    half = tile_in.shape[2] // 2
    totals = jnp.sum(tile_in[...], axis=0)
    abs_total = jnp.sum(totals[:, :half], keepdims=True)
    if decay:
        abs_total = abs_total + decay * before[2:3, :1]
    density_total = jnp.sum(totals[:, half:], keepdims=True) * share
    rate = step_size / (abs_total / total_cells + 1e-6)
    pull = volume_pull * (density_total / total_cells - volume_target)
    row = lax.broadcasted_iota(jnp.int32, total_ref.shape, 0)
    total_ref[...] = jnp.where(row == 0, rate, jnp.where(row == 1, pull, abs_total))


def second_kernel(cells, loads, self_weight, step_ref, moment_wide,
                  design_wide, base_far, lo_far, hi_far,
                  shown_ref, design_out, keep, spare, outer, rest, tile_ref,
                  stiff, weight_ref, inverse_ref, resid_ref, steps_ref, shown_to, design_new,
                  base_in, force_lo, force_hi, sense_ref, sems):
    copies = [
        pltpu.make_async_copy(source, target, sems.at[i])
        for i, (source, target) in enumerate(((base_far, base_in), (lo_far, force_lo), (hi_far, force_hi)))
    ]
    for copy in copies:
        copy.start()
    even, is_first, is_last = place_of()
    shape = moment_wide.shape[1:]
    masks = inner_masks(shape)
    wide = cells + 2 * DESIGN
    rows = cells + 2 * SOURCE
    zero = jnp.zeros(shape, jnp.float32)
    rate, pull = step_ref[0:1, :], step_ref[1:2, :]
    for r in range(wide):
        signed = design_wide[r]
        before = jnp.abs(signed)
        moved = jnp.clip(before - rate * moment_wide[r] - pull, density_floor, 1.0)
        fixed = (before == density_floor) | (before == 1.0)
        design = jnp.where(fixed, before, moved)
        design_new[r] = design
        stiffness = stiffness_of(design)
        if r < DESIGN:
            stiff[r] = jnp.where(is_first, zero, stiffness)
        elif r >= DESIGN + cells:
            stiff[r] = jnp.where(is_last, zero, stiffness)
        else:
            stiff[r] = stiffness
    own_rows = pltpu.make_async_copy(design_new.at[pl.ds(DESIGN, cells)], design_out, sems.at[len(copies) + loads])
    own_rows.start()
    weight, inverse, resid, steps, shown = Kept(), Kept(), Kept(), Kept(), Kept()
    for q in range(rows):
        weight_row(q, design_wide[q + 1] > 0.0, stiff, weight, inverse, weight_ref, inverse_ref, q, masks)
    for copy in copies:
        copy.wait()
    for q in range(rows):
        base = [base_row(l, q, cells, base_in, force_lo, force_hi) for l in range(loads)]
        start_row(q, base, design_new[q + 1], self_weight, inverse, resid, steps, resid_ref, steps_ref, 0)
    for k in range(SWEEPS - 1):
        for q in range(k + 1, rows - k - 1):
            sweep_row(k, q, loads, weight, resid, steps, resid_ref, steps_ref, shown_to, shown)
    results = [
        pltpu.make_async_copy(shown_to.at[l, pl.ds(1, cells)], shown_ref.at[l], sems.at[len(copies) + l])
        for l in range(loads)
    ]
    for copy in results:
        copy.start()
    for i in range(cells):
        sense_ref[i] = energy_row(i, loads, design_new[DESIGN + i], shown, masks)
    cut_rows(cells, even, sense_ref, keep, spare, outer, rest)
    own = design_new.at[pl.ds(DESIGN, cells)]
    spread_totals(tile_ref, filter_total(cells, sense_ref, is_first, is_last, masks), fold_rows(cells, own))
    for copy in results + [own_rows]:
        copy.wait()


def last_moment_kernel(cells, slab, edge, spare, rest, pair_a, pair_b, moment_wide, design_far, passive_far,
                       momentum_ref, kept_ref, before_ref, least_ref, most_ref, sense_wide, momentum_all,
                       kinds, sems):
    even, is_first, is_last = place_of()
    window = pl.ds(pl.multiple_of(lax.axis_index("load") * slab, 8), slab)
    copies = [
        pltpu.make_async_copy(design_far.at[:, window, :], before_ref, sems.at[1]),
        pltpu.make_async_copy(passive_far.at[:, window, :], kinds, sems.at[2]),
    ]
    for copy in copies:
        copy.start()
    shape = edge.shape[1:]
    masks = inner_masks(shape)
    zero = jnp.zeros(shape, jnp.float32)
    sense_wide[0] = jnp.where(is_first, zero, jnp.where(even, pair_a[0], pair_b[0]))
    sense_wide[cells + 1] = jnp.where(is_last, zero, jnp.where(even, pair_b[0], pair_a[0]))
    for i in range(cells):
        sense_wide[i + 1] = whole_row(i, cells, even, edge, spare, rest)
    inside, at_ends = edge_planes(masks)
    for i in range(cells):
        scale = inside
        if i == 0:
            scale = jnp.where(is_first, at_ends, inside)
        elif i == cells - 1:
            scale = jnp.where(is_last, at_ends, inside)
        momentum_all[i] = moment_decay * moment_wide[DESIGN + i] + filtered_row(i, sense_wide, masks) * scale
        momentum = momentum_all[i, window, :]
        kept_ref[i] = momentum
    copy = pltpu.make_async_copy(kept_ref, momentum_ref, sems.at[0])
    copy.start()
    for other in copies:
        other.wait()
    for i in range(cells):
        kind = kinds[i]
        least_ref[i] = jnp.where(kind == 2, 1.0, density_floor)
        most_ref[i] = jnp.where(kind == 1, density_floor, 1.0)
    copy.wait()


def last_kernel(cells, step_ref, momentum_ref, before_ref, least_ref, most_ref, design_ref, design_near, sems):
    rate, pull = step_ref[0:1, :], step_ref[1:2, :]
    for i in range(cells):
        moved = before_ref[i] - rate * momentum_ref[i] - pull
        design_near[i] = jnp.minimum(jnp.maximum(moved, least_ref[i]), most_ref[i])
    copy = pltpu.make_async_copy(design_near, design_ref, sems.at[0])
    copy.start()
    copy.wait()


VMEM = pl.BlockSpec(memory_space=pltpu.VMEM)
SMEM = pl.BlockSpec(memory_space=pltpu.SMEM)


def on_core(kernel, operands, scalars, outs, scratch, cost=0, limit=4, far=0, far_outs=0):
    anywhere = pl.BlockSpec(memory_space=pl.ANY)
    operands = [
        pltpu.with_memory_space_constraint(operand, pltpu.VMEM)
        if scalars <= i < len(operands) - far else pltpu.with_memory_space_constraint(operand, pltpu.HBM) if i >= len(operands) - far else operand
        for i, operand in enumerate(operands)
    ]
    return pl.pallas_call(
        kernel,
        out_shape=[
            pltpu.HBM(shape, jnp.float32) if i < far_outs else pltpu.VMEM(shape, jnp.float32)
            for i, shape in enumerate(outs)
        ],
        in_specs=[SMEM] * scalars + [VMEM] * (len(operands) - scalars - far) + [anywhere] * far,
        out_specs=[anywhere] * far_outs + [VMEM] * (len(outs) - far_outs),
        scratch_shapes=[pltpu.VMEM(item, jnp.float32) if isinstance(item, tuple) else item for item in scratch],
        cost_estimate=pl.CostEstimate(flops=cost, bytes_accessed=cost, transcendentals=0) if cost else None,
        compiler_params=pltpu.CompilerParams(vmem_limit_bytes=limit * 1024 * 1024),
    )(*operands)


def passive_apply(design, passive):
    return jnp.where(passive == 1, density_floor, jnp.where(passive == 2, 1.0, design))


def swap(value, axis, bit):
    count = lax.axis_size(axis)
    return lax.ppermute(value, axis, [(i, i ^ bit) for i in range(count)])


def along(value, step):
    count = lax.axis_size("brick")
    pairs = [(i, i + step) for i in range(count) if 0 <= i + step < count]
    return lax.ppermute(value, "brick", pairs)


def both_ways(value):
    count, loads = lax.axis_size("brick"), lax.axis_size("load")
    pairs = []
    for l in range(loads):
        step = 1 if l % 2 == 0 else -1
        pairs += [(l * count + i, l * count + i + step) for i in range(count) if 0 <= i + step < count]
    return lax.ppermute(value, ("load", "brick"), pairs)


def bits_of(count):
    return [1 << k for k in range(count.bit_length() - 1)]


def sum_over(value, axis):
    for bit in bits_of(lax.axis_size(axis)):
        value = value + swap(value, axis, bit)
    return value


def after(value, other):
    return lax.optimization_barrier((value, other))[0]


def add_kernel(first, second, sum_ref):
    sum_ref[...] = first[...] + second[...]


def meet(parts, tiles, filtered, totals):
    total = totals(lax.all_to_all(tiles, ("load", "brick"), 0, 0, tiled=True))
    for bit in bits_of(lax.axis_size("load"))[1:]:
        parts = [part + swap(part, "load", bit) for part in parts]
    keep, spare, outer, rest = parts
    (edge,) = on_core(add_kernel, (keep, swap(outer, "load", 1)), 0, [keep.shape], [])
    pair_a = both_ways(edge)
    rest = swap(rest, "load", 1)
    pair_b = swap(pair_a, "load", 1)
    return filtered(edge, spare, rest, pair_a, pair_b), total


def body(density, passive, support, load_nodes, load_force, self_weight, body_force):
    cells, size_y, size_z = density.shape
    loads = body_force.shape[0]
    load_count, bricks = lax.axis_size("load"), lax.axis_size("brick")
    slab = size_y // load_count
    total_cells = float(cells * bricks * size_y * size_z)
    share = 1.0 / load_count
    plane = (size_y, size_z)
    wide, rows = cells + 2 * DESIGN, cells + 2 * SOURCE
    tile = (load_count * bricks, 1, 2 * size_z)
    shown_shape = (loads, cells + 2) + plane
    resid_shape = (loads, rows) + plane
    steps_shape = (SWEEPS - 1, loads, rows) + plane

    def parts_of(width):
        return [(count,) + plane for count in (width, cells - width, width, cells - width)]

    payload, upper, lower = on_core(
        functools.partial(prepare_kernel, cells),
        (density, passive, support, body_force),
        0,
        [(DESIGN + SOURCE,) + plane, (loads, SOURCE) + plane, (loads, SOURCE) + plane],
        [pltpu.VMEM((DESIGN,) + plane, jnp.float32), pltpu.VMEM((DESIGN,) + plane, jnp.int32),
         pltpu.VMEM((SOURCE,) + plane, jnp.int32), pltpu.SemaphoreType.DMA((5,))],
        far=4,
    )
    pair_a = both_ways(payload)
    force_lo = along(upper, 1)
    force_hi = along(lower, -1)
    base_far, base = on_core(
        functools.partial(points_kernel, cells, loads),
        (load_nodes, load_force, after(body_force, (upper, lower))),
        2,
        [resid_shape, resid_shape],
        [pltpu.SemaphoreType.DMA((1,))],
        cost=1,
        far_outs=1,
    )
    inner_shapes = [(loads, cells) + plane, (SWEEPS - 1, loads, cells) + plane]
    design_own, stiff_own, *near = on_core(
        functools.partial(own_kernel, cells, loads),
        (self_weight, density, passive, support, base),
        1,
        [(cells,) + plane, (cells,) + plane, (6, cells) + plane, (cells,) + plane]
        + inner_shapes + [(loads, cells - 2 * (SWEEPS - 1)) + plane],
        [(wide,) + plane],
        cost=1,
    )
    pair_a = after(pair_a, stiff_own)
    pair_b = swap(pair_a[:DESIGN], "load", 1)
    pair_c = swap(pair_a[DESIGN:], "load", 1)
    design_wide, *early = on_core(
        functools.partial(early_kernel, cells, loads),
        (self_weight, base, pair_a, pair_b, pair_c, design_own, stiff_own, *near),
        1,
        [(wide,) + plane, (6, 2 * SOURCE + 2) + plane, (2 * SOURCE + 2,) + plane]
        + inner_shapes + [(loads, cells - 2 * (SWEEPS - 1)) + plane],
        [(wide,) + plane],
        cost=1,
    )
    lo_far, hi_far, *parts, tiles = on_core(
        functools.partial(first_kernel, cells, loads),
        (self_weight, force_lo, force_hi, base, design_wide, *near, *early),
        1,
        [(loads, SOURCE) + plane] * 2 + parts_of(SENSE) + [tile],
        [resid_shape, steps_shape, shown_shape, (cells,) + plane, pltpu.SemaphoreType.DMA((2,))],
        far_outs=2,
    )
    def totals(decay, before):
        return lambda tiles: on_core(
            functools.partial(totals_kernel, total_cells, share, decay),
            (tiles, before),
            0,
            [(8, size_z)],
            [],
            cost=2000000000,
        )[0]

    (moment_wide,), step_first = meet(
        parts, tiles,
        lambda *sensed: on_core(
            functools.partial(moment_kernel, cells),
            sensed,
            0,
            [(wide,) + plane],
            [(cells + 2 * SENSE,) + plane],
        ),
        totals(0.0, tiles),
    )
    shown, design, *parts, tiles = on_core(
        functools.partial(second_kernel, cells, loads),
        (self_weight, step_first, moment_wide, design_wide, base_far, lo_far, hi_far),
        1,
        [(loads, cells) + plane, (cells,) + plane] + parts_of(1) + [tile],
        [(wide,) + plane, (6, rows) + plane, (rows,) + plane, resid_shape, steps_shape, shown_shape, (wide,) + plane,
         resid_shape, (loads, SOURCE) + plane, (loads, SOURCE) + plane, (cells,) + plane,
         pltpu.SemaphoreType.DMA((4 + loads,))],
        limit=14,
        far=3,
        far_outs=2,
    )
    last_ones, step_last = meet(
        parts, tiles,
        lambda *sensed: on_core(
            functools.partial(last_moment_kernel, cells, slab),
            sensed + (moment_wide, design, passive),
            0,
            [(cells, slab, size_z)] * 5,
            [(cells + 2,) + plane, (cells,) + plane,
             pltpu.VMEM((cells, slab, size_z), jnp.int32), pltpu.SemaphoreType.DMA((3,))],
            far=2,
            far_outs=1,
        ),
        totals(moment_decay, step_first),
    )
    (design,) = on_core(
        functools.partial(last_kernel, cells),
        (step_last,) + tuple(last_ones[1:]),
        0,
        [(cells, slab, size_z)],
        [(cells, slab, size_z), pltpu.SemaphoreType.DMA((1,))],
        far_outs=1,
    )
    return design, last_ones[0], shown


def solution(mesh):
    placed = (
        P("brick", None, None),
        P("brick", None, None),
        P("brick", None, None),
        P("load", None),
        P("load", None),
        P("load"),
        P("load", "brick", None, None),
    )
    return jax.shard_map(
        body,
        mesh=mesh,
        in_specs=placed,
        out_specs=(
            P("brick", "load", None),
            P("brick", "load", None),
            P("load", "brick", None, None),
        ),
        check_vma=False,
    )
```

```python
import functools

import jax
import jax.numpy as jnp
from jax import lax
from jax.experimental import pallas as pl
from jax.experimental.pallas import tpu as pltpu
from jax.sharding import PartitionSpec as P

SWEEPS = 5

stiff_floor = 0.01
mass_shift = 0.1
spectrum_low = 0.05
spectrum_high = 2.0
moment_decay = 0.8
step_size = 0.1
volume_pull = 0.5
volume_target = 0.4
density_floor = 0.001

SOURCE = SWEEPS
DESIGN = SWEEPS + 1
SENSE = SWEEPS + 2


def chebyshev_factors():
    centre = 0.5 * (spectrum_high + spectrum_low)
    half_width = 0.5 * (spectrum_high - spectrum_low)
    ratio_one = centre / half_width
    previous = 1.0 / ratio_one
    factors = []
    for _ in range(SWEEPS - 1):
        current = 1.0 / (2.0 * ratio_one - previous)
        factors.append((current * previous, 2.0 * current / half_width))
        previous = current
    return 1.0 / centre, factors


def shifted(plane):
    size_y, size_z = plane.shape
    return (
        pltpu.roll(plane, 1, 0),
        pltpu.roll(plane, size_y - 1, 0),
        pltpu.roll(plane, 1, 1),
        pltpu.roll(plane, size_z - 1, 1),
    )


def inner_masks(shape):
    along_y = lax.broadcasted_iota(jnp.int32, shape, 0)
    along_z = lax.broadcasted_iota(jnp.int32, shape, 1)
    return (along_y > 0, along_y < shape[0] - 1, along_z > 0, along_z < shape[1] - 1)


def beside_planes(plane, masks):
    return tuple(jnp.where(mask, moved, 0.0) for mask, moved in zip(masks, shifted(plane)))


def edge_planes(masks):
    edges = sum((1.0 - mask.astype(jnp.float32)) for mask in masks)
    return 1.0 / (8.0 - edges), 1.0 / (7.0 - edges)


def stiffness_of(design):
    return stiff_floor + (1.0 - stiff_floor) * (design * design * design)


class Kept:
    def __init__(self):
        self.places = {}

    def put(self, key, ref, index, value):
        ref[index] = value
        self.places[key] = (ref, index)

    def get(self, key):
        ref, index = self.places[key]
        return ref[index]


def weight_row(q, is_free, stiff, weight, inverse, weight_to, inverse_to, place, masks):
    here, below, above = stiff[q + 1], stiff[q], stiff[q + 2]
    around = (below, above) + beside_planes(here, masks)
    total = around[0]
    for plane in around[1:]:
        total = total + plane
    diagonal = (3.0 + mass_shift) * here + 0.5 * total
    scale = jnp.where(is_free, 1.0 / diagonal, 0.0)
    inverse.put(q, inverse_to, place, scale)
    half = 0.5 * scale
    weight.put((0, q), weight_to, (0, place), half * (here + below))
    weight.put((1, q), weight_to, (1, place), half * (here + above))
    for j in range(4):
        weight.put((2 + j, q), weight_to, (2 + j, place), jnp.where(masks[j], half * (here + around[2 + j]), 0.0))


def sweep_row(k, q, loads, weight, resid, steps, resid_to, steps_to, shown_to, shown, first=0, first_shown=SWEEPS - 1):
    _, factors = chebyshev_factors()
    keep, gain = factors[k]
    last = k == len(factors) - 1
    faces = [weight.get((j, q)) for j in range(6)]
    for l in range(loads):
        here = steps.get((k, l, q))
        total = faces[0] * steps.get((k, l, q - 1)) + faces[1] * steps.get((k, l, q + 1))
        for face, moved in zip(faces[2:], shifted(here)):
            total = total + face * moved
        left = resid.get((l, q)) - here + total
        step = keep * here + gain * left
        if last:
            for earlier in range(k + 1):
                step = step + steps.get((earlier, l, q))
            shown.put((l, q), shown_to, (l, q - first_shown), step)
        else:
            resid.put((l, q), resid_to, (l, q - first), left)
            steps.put((k + 1, l, q), steps_to, (k + 1, l, q - first), step)


def energy_row(i, loads, design, shown, masks):
    q = i + SOURCE
    energy = None
    for l in range(loads):
        here = shown.get((l, q))
        around = (shown.get((l, q - 1)), shown.get((l, q + 1))) + beside_planes(here, masks)
        spread = None
        for plane in around:
            gap = here - plane
            spread = gap * gap if spread is None else spread + gap * gap
        part = mass_shift * (here * here) + 0.25 * spread
        energy = part if energy is None else energy + part
    return (-3.0 * (1.0 - stiff_floor)) * (design * design) * energy


def fold(plane):
    return jnp.sum(plane.reshape(plane.shape[0] // 8, 8, plane.shape[1]), axis=0)


def filter_total(cells, sense, is_first, is_last, masks):
    inside, outer = edge_planes(masks)
    usual = 4.0 * inside + sum(beside_planes(inside, masks))
    at_end = 2.0 * outer + inside + sum(beside_planes(outer, masks))
    zero = jnp.zeros_like(inside)
    total = sense[0]
    for i in range(1, cells):
        total = total + sense[i]
    ends = jnp.where(is_first, sense[0], zero) + jnp.where(is_last, sense[cells - 1], zero)
    nexts = jnp.where(is_first, sense[1], zero) + jnp.where(is_last, sense[cells - 2], zero)
    return -fold(total * usual + ends * (at_end - usual) + nexts * (outer - inside))


def fold_rows(cells, ref):
    total = jnp.abs(ref[0])
    for i in range(1, cells):
        total = total + jnp.abs(ref[i])
    return fold(total)


def place_of():
    brick = lax.axis_index("brick")
    return lax.axis_index("load") % 2 == 0, brick == 0, brick == lax.axis_size("brick") - 1


def prepare_kernel(cells, density, passive, support, force, payload_ref, upper_ref, lower_ref,
                   design_rows, kind_rows, hold_rows, sems):
    even, _, _ = place_of()
    start = jnp.where(even, cells - DESIGN, 0)
    start_mask = jnp.where(even, cells - SOURCE, 0)
    copies = [
        pltpu.make_async_copy(source, target, sems.at[i])
        for i, (source, target) in enumerate((
            (density.at[pl.ds(start, DESIGN)], design_rows),
            (passive.at[pl.ds(start, DESIGN)], kind_rows),
            (support.at[pl.ds(start_mask, SOURCE)], hold_rows),
            (force.at[:, pl.ds(cells - SOURCE, SOURCE)], upper_ref),
            (force.at[:, pl.ds(0, SOURCE)], lower_ref),
        ))
    ]
    for copy in copies:
        copy.start()
    for copy in copies[:3]:
        copy.wait()
    for i in range(DESIGN):
        payload_ref[i] = passive_apply(design_rows[i], kind_rows[i])
    for i in range(SOURCE):
        payload_ref[DESIGN + i] = (1 - hold_rows[i]).astype(jnp.float32)
    for copy in copies[3:]:
        copy.wait()


def points_kernel(cells, loads, nodes, forces, force_ref, base_far, base_ref, sems):
    rows = cells + 2 * SOURCE
    size_y, size_z = base_ref.shape[2:]
    zero = jnp.zeros((size_y, size_z), jnp.float32)
    for l in range(loads):
        for q in range(rows):
            own = SOURCE <= q < SOURCE + cells
            base_ref[l, q] = force_ref[l, q - SOURCE] if own else zero
    first = (lax.axis_index("brick") * cells - SOURCE) * size_y * size_z
    along_z = lax.broadcasted_iota(jnp.int32, (1, size_z), 1)
    for l in range(loads):

        def one_point(p, carry, l=l):
            cell = nodes[l, p] - first

            @pl.when((cell >= 0) & (cell < rows * size_y * size_z))
            def _():
                line, z = cell // size_z, cell % size_z
                q, y = line // size_y, line % size_y
                spot = (l, q, pl.ds(y, 1), slice(None))
                base_ref[spot] = base_ref[spot] + jnp.where(along_z == z, forces[l, p], 0.0)

            return carry

        lax.fori_loop(0, nodes.shape[1], one_point, 0)
    copy = pltpu.make_async_copy(base_ref, base_far, sems.at[0])
    copy.start()
    copy.wait()


def base_row(l, q, cells, base_in, force_lo, force_hi):
    if q < SOURCE:
        return base_in[l, q] + force_lo[l, q]
    if q >= SOURCE + cells:
        return base_in[l, q] + force_hi[l, q - SOURCE - cells]
    return base_in[l, q]


def inner_steps(cells, margin):
    return [range(SOURCE + margin + k, SOURCE + cells - margin - k) for k in range(SWEEPS)]


def outer_place(q, cells):
    return q if q <= SOURCE else q - (cells - 2)


def start_row(q, base, design, self_weight, inverse, resid, steps, resid_to, steps_to, first):
    first_scale, _ = chebyshev_factors()
    for l, one in enumerate(base):
        left = inverse.get(q) * (one + self_weight[l] * design)
        resid.put((l, q), resid_to, (l, q - first), left)
        steps.put((0, l, q), steps_to, (0, l, q - first), first_scale * left)


def inner_places(cells, loads, near, early):
    weight, inverse, resid, steps, shown = Kept(), Kept(), Kept(), Kept(), Kept()
    rows = cells + 2 * SOURCE
    near_rows, early_rows = inner_steps(cells, 1), inner_steps(cells, 0)
    for q in range(rows):
        inside = q in near_rows[0]
        if not inside and early is None:
            continue
        place = q - SOURCE if inside else outer_place(q, cells)
        weights, inverses = (near if inside else early)[:2]
        inverse.places[q] = (inverses, place)
        for j in range(6):
            weight.places[(j, q)] = (weights, (j, place))
    for refs, ranges in ((early, early_rows), (near, near_rows)):
        if refs is None:
            continue
        for l in range(loads):
            for k in range(SWEEPS - 1):
                for q in ranges[k]:
                    steps.places[(k, l, q)] = (refs[3], (k, l, q - SOURCE))
            for q in ranges[SWEEPS - 1]:
                shown.places[(l, q)] = (refs[4], (l, q - SOURCE - (SWEEPS - 1)))
    for l in range(loads):
        for q in early_rows[0]:
            depth = min(q - SOURCE, SOURCE + cells - 1 - q)
            at_early = early is not None and depth < SWEEPS - 1
            if at_early or q in near_rows[0]:
                resid.places[(l, q)] = ((early if at_early else near)[2], (l, q - SOURCE))
    return weight, inverse, resid, steps, shown


def own_kernel(cells, loads, self_weight, density, passive, support, base_ref,
               design_own, stiff, weight_ref, inverse_ref, resid_ref, steps_ref, shown_ref, stiff_wide):
    masks = inner_masks(density.shape[1:])
    weight, inverse, resid, steps, shown = Kept(), Kept(), Kept(), Kept(), Kept()
    for i in range(cells):
        design = passive_apply(density[i], passive[i])
        stiffness = stiffness_of(design)
        stiff[i] = stiffness
        stiff_wide[DESIGN + i] = stiffness
        design_own[i] = jnp.where(support[i] == 0, design, -design)
    inner = inner_steps(cells, 1)
    for q in inner[0]:
        i = q - SOURCE
        weight_row(q, support[i] == 0, stiff_wide, weight, inverse, weight_ref, inverse_ref, i, masks)
        base = [base_ref[l, q] for l in range(loads)]
        start_row(q, base, jnp.abs(design_own[i]), self_weight, inverse, resid, steps, resid_ref, steps_ref, SOURCE)
    for k in range(SWEEPS - 1):
        for q in inner[k + 1]:
            sweep_row(
                k, q, loads, weight, resid, steps, resid_ref, steps_ref, shown_ref, shown,
                SOURCE, SOURCE + SWEEPS - 1,
            )


def early_kernel(cells, loads, self_weight, base_ref, pair_a, pair_b, pair_c, design_own, stiff_own,
                 near_weight, near_inverse, near_resid, near_steps, near_shown,
                 design_wide, weight_ref, inverse_ref, resid_ref, steps_ref, shown_ref, stiff):
    even, is_first, is_last = place_of()
    shape = design_own.shape[1:]
    masks = inner_masks(shape)
    zero = jnp.zeros(shape, jnp.float32)
    weight, inverse, resid, steps, shown = inner_places(
        cells, loads, (near_weight, near_inverse, near_resid, near_steps, near_shown), None
    )
    for i in range(DESIGN):
        low = jnp.where(even, pair_a[i], pair_b[i])
        high = jnp.where(even, pair_b[i], pair_a[i])
        stiff[i] = jnp.where(is_first, zero, stiffness_of(low))
        stiff[DESIGN + cells + i] = jnp.where(is_last, zero, stiffness_of(high))
        below, above = i - 1, i
        if below >= 0:
            free = jnp.where(even, pair_a[DESIGN + below], pair_c[below])
            low = jnp.where((free > 0.5) & jnp.logical_not(is_first), low, -low)
        else:
            low = -low
        if above < SOURCE:
            free = jnp.where(even, pair_c[above], pair_a[DESIGN + above])
            high = jnp.where((free > 0.5) & jnp.logical_not(is_last), high, -high)
        else:
            high = -high
        design_wide[i] = low
        design_wide[DESIGN + cells + i] = high
    for i in range(cells):
        design_wide[DESIGN + i] = design_own[i]
        stiff[DESIGN + i] = stiff_own[i]
    near, inner = inner_steps(cells, 1), inner_steps(cells, 0)
    for q in range(cells + 2 * SOURCE):
        if q not in near[0]:
            weight_row(
                q, design_wide[q + 1] > 0.0, stiff, weight, inverse, weight_ref, inverse_ref, outer_place(q, cells), masks
            )
    for q in inner[0]:
        if q not in near[0]:
            base = [base_ref[l, q] for l in range(loads)]
            design = jnp.abs(design_wide[q + 1])
            start_row(q, base, design, self_weight, inverse, resid, steps, resid_ref, steps_ref, SOURCE)
    for k in range(SWEEPS - 1):
        for q in inner[k + 1]:
            if q not in near[k + 1]:
                sweep_row(
                    k, q, loads, weight, resid, steps, resid_ref, steps_ref, shown_ref, shown,
                    SOURCE, SOURCE + SWEEPS - 1,
                )


def first_kernel(cells, loads, self_weight, force_lo, force_hi, base_in, design_wide,
                 near_weight, near_inverse, near_resid, near_steps, near_shown,
                 early_weight, early_inverse, early_resid, early_steps, early_shown,
                 lo_far, hi_far, sense_ref, outer, rest, tile_ref,
                 resid_ref, steps_ref, shown_ref, sems):
    copies = [
        pltpu.make_async_copy(source, target, sems.at[i])
        for i, (source, target) in enumerate(((force_lo, lo_far), (force_hi, hi_far)))
    ]
    for copy in copies:
        copy.start()
    even, is_first, is_last = place_of()
    shape = design_wide.shape[1:]
    masks = inner_masks(shape)
    rows = cells + 2 * SOURCE
    weight, inverse, resid, steps, shown = inner_places(
        cells, loads, (near_weight, near_inverse, near_resid, near_steps, near_shown),
        (early_weight, early_inverse, early_resid, early_steps, early_shown),
    )
    inner = inner_steps(cells, 0)
    for q in range(rows):
        if q not in inner[0]:
            base = [base_row(l, q, cells, base_in, force_lo, force_hi) for l in range(loads)]
            design = jnp.abs(design_wide[q + 1])
            start_row(q, base, design, self_weight, inverse, resid, steps, resid_ref, steps_ref, 0)
    for k in range(SWEEPS - 1):
        for q in range(k + 1, rows - k - 1):
            if q not in inner[k + 1]:
                sweep_row(k, q, loads, weight, resid, steps, resid_ref, steps_ref, shown_ref, shown)
    for i in range(cells):
        sense_ref[i] = energy_row(i, loads, design_wide[DESIGN + i], shown, masks)
    cut_rows(cells, even, sense_ref, outer, rest)
    own = design_wide.at[pl.ds(DESIGN, cells)]
    spread_totals(tile_ref, filter_total(cells, sense_ref, is_first, is_last, masks), fold_rows(cells, own))
    for copy in copies:
        copy.wait()


def cut_rows(cells, even, sense, outer, rest):
    width = outer.shape[0]
    for i in range(width):
        outer[i] = jnp.where(even, sense[i], sense[cells - width + i])
    for i in range(cells - width):
        rest[i] = jnp.where(even, sense[width + i], sense[i])


def edge_kernel(cells, sense, outer, edge):
    even, _, _ = place_of()
    width = outer.shape[0]
    for i in range(width):
        edge[i] = jnp.where(even, sense[cells - width + i], sense[i]) + outer[i]


def whole_row(i, cells, even, sense, edge, rest):
    width = edge.shape[0]
    if_even = sense[i] + rest[i] if i < cells - width else edge[i - (cells - width)]
    if_odd = edge[i] if i < width else sense[i] + rest[i - width]
    return jnp.where(even, if_even, if_odd)


def moment_kernel(cells, sense, edge, rest, pair_a, pair_b, moment_ref, sense_wide):
    even, is_first, is_last = place_of()
    shape = edge.shape[1:]
    masks = inner_masks(shape)
    zero = jnp.zeros(shape, jnp.float32)
    for i in range(SENSE):
        low = jnp.where(even, pair_a[i], pair_b[i])
        high = jnp.where(even, pair_b[i], pair_a[i])
        sense_wide[i] = jnp.where(is_first, zero, low)
        sense_wide[SENSE + cells + i] = jnp.where(is_last, zero, high)
    for i in range(cells):
        sense_wide[SENSE + i] = whole_row(i, cells, even, sense, edge, rest)
    inside, at_ends = edge_planes(masks)
    for r in range(cells + 2 * DESIGN):
        at_end = (is_first & (r == DESIGN)) | (is_last & (r == DESIGN + cells - 1))
        moment_ref[r] = filtered_row(r, sense_wide, masks) * jnp.where(at_end, at_ends, inside)


def filtered_row(r, sense_wide, masks):
    here = sense_wide[r + 1]
    total = 2.0 * here + sense_wide[r] + sense_wide[r + 2]
    for plane in beside_planes(here, masks):
        total = total + plane
    return total


def spread_totals(tile_ref, abs_tile, density_tile):
    row = jnp.concatenate([jnp.sum(tile, axis=0, keepdims=True) for tile in (abs_tile, density_tile)], axis=1)
    tile_ref[...] = jnp.broadcast_to(row[None], tile_ref.shape)


def totals_kernel(total_cells, share, decay, tile_in, before, total_ref):
    half = tile_in.shape[2] // 2
    totals = jnp.sum(tile_in[...], axis=0)
    abs_total = jnp.sum(totals[:, :half], keepdims=True)
    if decay:
        abs_total = abs_total + decay * before[2:3, :1]
    density_total = jnp.sum(totals[:, half:], keepdims=True) * share
    rate = step_size / (abs_total / total_cells + 1e-6)
    pull = volume_pull * (density_total / total_cells - volume_target)
    row = lax.broadcasted_iota(jnp.int32, total_ref.shape, 0)
    total_ref[...] = jnp.where(row == 0, rate, jnp.where(row == 1, pull, abs_total))


def second_kernel(cells, loads, self_weight, step_ref, moment_wide,
                  design_wide, base_far, lo_far, hi_far,
                  shown_ref, design_out, sense_ref, outer, rest, tile_ref,
                  stiff, weight_ref, inverse_ref, resid_ref, steps_ref, shown_to, design_new,
                  base_in, force_lo, force_hi, sems):
    copies = [
        pltpu.make_async_copy(source, target, sems.at[i])
        for i, (source, target) in enumerate(((base_far, base_in), (lo_far, force_lo), (hi_far, force_hi)))
    ]
    for copy in copies:
        copy.start()
    even, is_first, is_last = place_of()
    shape = moment_wide.shape[1:]
    masks = inner_masks(shape)
    wide = cells + 2 * DESIGN
    rows = cells + 2 * SOURCE
    zero = jnp.zeros(shape, jnp.float32)
    rate, pull = step_ref[0:1, :], step_ref[1:2, :]
    for r in range(wide):
        signed = design_wide[r]
        before = jnp.abs(signed)
        moved = jnp.clip(before - rate * moment_wide[r] - pull, density_floor, 1.0)
        fixed = (before == density_floor) | (before == 1.0)
        design = jnp.where(fixed, before, moved)
        design_new[r] = design
        stiffness = stiffness_of(design)
        if r < DESIGN:
            stiff[r] = jnp.where(is_first, zero, stiffness)
        elif r >= DESIGN + cells:
            stiff[r] = jnp.where(is_last, zero, stiffness)
        else:
            stiff[r] = stiffness
    own_rows = pltpu.make_async_copy(design_new.at[pl.ds(DESIGN, cells)], design_out, sems.at[len(copies) + loads])
    own_rows.start()
    weight, inverse, resid, steps, shown = Kept(), Kept(), Kept(), Kept(), Kept()
    for q in range(rows):
        weight_row(q, design_wide[q + 1] > 0.0, stiff, weight, inverse, weight_ref, inverse_ref, q, masks)
    for copy in copies:
        copy.wait()
    for q in range(rows):
        base = [base_row(l, q, cells, base_in, force_lo, force_hi) for l in range(loads)]
        start_row(q, base, design_new[q + 1], self_weight, inverse, resid, steps, resid_ref, steps_ref, 0)
    for k in range(SWEEPS - 1):
        for q in range(k + 1, rows - k - 1):
            sweep_row(k, q, loads, weight, resid, steps, resid_ref, steps_ref, shown_to, shown)
    results = [
        pltpu.make_async_copy(shown_to.at[l, pl.ds(1, cells)], shown_ref.at[l], sems.at[len(copies) + l])
        for l in range(loads)
    ]
    for copy in results:
        copy.start()
    for i in range(cells):
        sense_ref[i] = energy_row(i, loads, design_new[DESIGN + i], shown, masks)
    cut_rows(cells, even, sense_ref, outer, rest)
    own = design_new.at[pl.ds(DESIGN, cells)]
    spread_totals(tile_ref, filter_total(cells, sense_ref, is_first, is_last, masks), fold_rows(cells, own))
    for copy in results + [own_rows]:
        copy.wait()


def last_moment_kernel(cells, slab, sense, edge, rest, pair_a, pair_b, moment_wide, design_far, passive_far,
                       momentum_ref, kept_ref, before_ref, least_ref, most_ref, sense_wide, momentum_all,
                       kinds, sems):
    even, is_first, is_last = place_of()
    window = pl.ds(pl.multiple_of(lax.axis_index("load") * slab, 8), slab)
    copies = [
        pltpu.make_async_copy(design_far.at[:, window, :], before_ref, sems.at[1]),
        pltpu.make_async_copy(passive_far.at[:, window, :], kinds, sems.at[2]),
    ]
    for copy in copies:
        copy.start()
    shape = edge.shape[1:]
    masks = inner_masks(shape)
    zero = jnp.zeros(shape, jnp.float32)
    sense_wide[0] = jnp.where(is_first, zero, jnp.where(even, pair_a[0], pair_b[0]))
    sense_wide[cells + 1] = jnp.where(is_last, zero, jnp.where(even, pair_b[0], pair_a[0]))
    for i in range(cells):
        sense_wide[i + 1] = whole_row(i, cells, even, sense, edge, rest)
    inside, at_ends = edge_planes(masks)
    for i in range(cells):
        scale = inside
        if i == 0:
            scale = jnp.where(is_first, at_ends, inside)
        elif i == cells - 1:
            scale = jnp.where(is_last, at_ends, inside)
        momentum_all[i] = moment_decay * moment_wide[DESIGN + i] + filtered_row(i, sense_wide, masks) * scale
        momentum = momentum_all[i, window, :]
        kept_ref[i] = momentum
    copy = pltpu.make_async_copy(kept_ref, momentum_ref, sems.at[0])
    copy.start()
    for other in copies:
        other.wait()
    for i in range(cells):
        kind = kinds[i]
        least_ref[i] = jnp.where(kind == 2, 1.0, density_floor)
        most_ref[i] = jnp.where(kind == 1, density_floor, 1.0)
    copy.wait()


def last_kernel(cells, step_ref, momentum_ref, before_ref, least_ref, most_ref, design_ref, design_near, sems):
    rate, pull = step_ref[0:1, :], step_ref[1:2, :]
    for i in range(cells):
        moved = before_ref[i] - rate * momentum_ref[i] - pull
        design_near[i] = jnp.minimum(jnp.maximum(moved, least_ref[i]), most_ref[i])
    copy = pltpu.make_async_copy(design_near, design_ref, sems.at[0])
    copy.start()
    copy.wait()


VMEM = pl.BlockSpec(memory_space=pltpu.VMEM)
SMEM = pl.BlockSpec(memory_space=pltpu.SMEM)


def on_core(kernel, operands, scalars, outs, scratch, cost=0, limit=4, far=0, far_outs=0):
    anywhere = pl.BlockSpec(memory_space=pl.ANY)
    operands = [
        pltpu.with_memory_space_constraint(operand, pltpu.VMEM)
        if scalars <= i < len(operands) - far else pltpu.with_memory_space_constraint(operand, pltpu.HBM) if i >= len(operands) - far else operand
        for i, operand in enumerate(operands)
    ]
    return pl.pallas_call(
        kernel,
        out_shape=[
            pltpu.HBM(shape, jnp.float32) if i < far_outs else pltpu.VMEM(shape, jnp.float32)
            for i, shape in enumerate(outs)
        ],
        in_specs=[SMEM] * scalars + [VMEM] * (len(operands) - scalars - far) + [anywhere] * far,
        out_specs=[anywhere] * far_outs + [VMEM] * (len(outs) - far_outs),
        scratch_shapes=[pltpu.VMEM(item, jnp.float32) if isinstance(item, tuple) else item for item in scratch],
        cost_estimate=pl.CostEstimate(flops=cost, bytes_accessed=cost, transcendentals=0) if cost else None,
        compiler_params=pltpu.CompilerParams(vmem_limit_bytes=limit * 1024 * 1024),
    )(*operands)


def passive_apply(design, passive):
    return jnp.where(passive == 1, density_floor, jnp.where(passive == 2, 1.0, design))


def swap(value, axis, bit):
    count = lax.axis_size(axis)
    return lax.ppermute(value, axis, [(i, i ^ bit) for i in range(count)])


def along(value, step):
    count = lax.axis_size("brick")
    pairs = [(i, i + step) for i in range(count) if 0 <= i + step < count]
    return lax.ppermute(value, "brick", pairs)


def both_ways(value):
    count, loads = lax.axis_size("brick"), lax.axis_size("load")
    pairs = []
    for l in range(loads):
        step = 1 if l % 2 == 0 else -1
        pairs += [(l * count + i, l * count + i + step) for i in range(count) if 0 <= i + step < count]
    return lax.ppermute(value, ("load", "brick"), pairs)


def bits_of(count):
    return [1 << k for k in range(count.bit_length() - 1)]


def sum_over(value, axis):
    for bit in bits_of(lax.axis_size(axis)):
        value = value + swap(value, axis, bit)
    return value


def after(value, other):
    return lax.optimization_barrier((value, other))[0]


def meet(parts, tiles, filtered, totals):
    total = totals(lax.all_to_all(tiles, ("load", "brick"), 0, 0, tiled=True))
    for bit in bits_of(lax.axis_size("load"))[1:]:
        parts = [part + swap(part, "load", bit) for part in parts]
    sense, outer, rest = parts
    outer = swap(outer, "load", 1)
    (edge,) = on_core(functools.partial(edge_kernel, sense.shape[0]), (sense, outer), 0, [outer.shape], [])
    pair_a = both_ways(edge)
    rest = swap(rest, "load", 1)
    pair_b = swap(pair_a, "load", 1)
    return filtered(sense, edge, rest, pair_a, pair_b), total


def body(density, passive, support, load_nodes, load_force, self_weight, body_force):
    cells, size_y, size_z = density.shape
    loads = body_force.shape[0]
    load_count, bricks = lax.axis_size("load"), lax.axis_size("brick")
    slab = size_y // load_count
    total_cells = float(cells * bricks * size_y * size_z)
    share = 1.0 / load_count
    plane = (size_y, size_z)
    wide, rows = cells + 2 * DESIGN, cells + 2 * SOURCE
    tile = (load_count * bricks, 1, 2 * size_z)
    shown_shape = (loads, cells + 2) + plane
    resid_shape = (loads, rows) + plane
    steps_shape = (SWEEPS - 1, loads, rows) + plane

    def parts_of(width):
        return [(count,) + plane for count in (cells, width, cells - width)]

    payload, upper, lower = on_core(
        functools.partial(prepare_kernel, cells),
        (density, passive, support, body_force),
        0,
        [(DESIGN + SOURCE,) + plane, (loads, SOURCE) + plane, (loads, SOURCE) + plane],
        [pltpu.VMEM((DESIGN,) + plane, jnp.float32), pltpu.VMEM((DESIGN,) + plane, jnp.int32),
         pltpu.VMEM((SOURCE,) + plane, jnp.int32), pltpu.SemaphoreType.DMA((5,))],
        far=4,
    )
    pair_a = both_ways(payload)
    force_lo = along(upper, 1)
    force_hi = along(lower, -1)
    base_far, base = on_core(
        functools.partial(points_kernel, cells, loads),
        (load_nodes, load_force, after(body_force, (upper, lower))),
        2,
        [resid_shape, resid_shape],
        [pltpu.SemaphoreType.DMA((1,))],
        cost=1,
        far_outs=1,
    )
    inner_shapes = [(loads, cells) + plane, (SWEEPS - 1, loads, cells) + plane]
    design_own, stiff_own, *near = on_core(
        functools.partial(own_kernel, cells, loads),
        (self_weight, density, passive, support, base),
        1,
        [(cells,) + plane, (cells,) + plane, (6, cells) + plane, (cells,) + plane]
        + inner_shapes + [(loads, cells - 2 * (SWEEPS - 1)) + plane],
        [(wide,) + plane],
        cost=1,
    )
    pair_a = after(pair_a, stiff_own)
    pair_b = swap(pair_a[:DESIGN], "load", 1)
    pair_c = swap(pair_a[DESIGN:], "load", 1)
    design_wide, *early = on_core(
        functools.partial(early_kernel, cells, loads),
        (self_weight, base, pair_a, pair_b, pair_c, design_own, stiff_own, *near),
        1,
        [(wide,) + plane, (6, 2 * SOURCE + 2) + plane, (2 * SOURCE + 2,) + plane]
        + inner_shapes + [(loads, cells - 2 * (SWEEPS - 1)) + plane],
        [(wide,) + plane],
        cost=1,
    )
    lo_far, hi_far, *parts, tiles = on_core(
        functools.partial(first_kernel, cells, loads),
        (self_weight, force_lo, force_hi, base, design_wide, *near, *early),
        1,
        [(loads, SOURCE) + plane] * 2 + parts_of(SENSE) + [tile],
        [resid_shape, steps_shape, shown_shape, pltpu.SemaphoreType.DMA((2,))],
        far_outs=2,
    )
    def totals(decay, before):
        return lambda tiles: on_core(
            functools.partial(totals_kernel, total_cells, share, decay),
            (tiles, before),
            0,
            [(8, size_z)],
            [],
            cost=2000000000,
        )[0]

    (moment_wide,), step_first = meet(
        parts, tiles,
        lambda *sensed: on_core(
            functools.partial(moment_kernel, cells),
            sensed,
            0,
            [(wide,) + plane],
            [(cells + 2 * SENSE,) + plane],
        ),
        totals(0.0, tiles),
    )
    shown, design, *parts, tiles = on_core(
        functools.partial(second_kernel, cells, loads),
        (self_weight, step_first, moment_wide, design_wide, base_far, lo_far, hi_far),
        1,
        [(loads, cells) + plane, (cells,) + plane] + parts_of(1) + [tile],
        [(wide,) + plane, (6, rows) + plane, (rows,) + plane, resid_shape, steps_shape, shown_shape, (wide,) + plane,
         resid_shape, (loads, SOURCE) + plane, (loads, SOURCE) + plane,
         pltpu.SemaphoreType.DMA((4 + loads,))],
        limit=14,
        far=3,
        far_outs=2,
    )
    last_ones, step_last = meet(
        parts, tiles,
        lambda *sensed: on_core(
            functools.partial(last_moment_kernel, cells, slab),
            sensed + (moment_wide, design, passive),
            0,
            [(cells, slab, size_z)] * 5,
            [(cells + 2,) + plane, (cells,) + plane,
             pltpu.VMEM((cells, slab, size_z), jnp.int32), pltpu.SemaphoreType.DMA((3,))],
            far=2,
            far_outs=1,
        ),
        totals(moment_decay, step_first),
    )
    (design,) = on_core(
        functools.partial(last_kernel, cells),
        (step_last,) + tuple(last_ones[1:]),
        0,
        [(cells, slab, size_z)],
        [(cells, slab, size_z), pltpu.SemaphoreType.DMA((1,))],
        far_outs=1,
    )
    return design, last_ones[0], shown


def solution(mesh):
    placed = (
        P("brick", None, None),
        P("brick", None, None),
        P("brick", None, None),
        P("load", None),
        P("load", None),
        P("load"),
        P("load", "brick", None, None),
    )
    return jax.shard_map(
        body,
        mesh=mesh,
        in_specs=placed,
        out_specs=(
            P("brick", "load", None),
            P("brick", "load", None),
            P("load", "brick", None, None),
        ),
        check_vma=False,
    )
```

```python
import functools

import jax
import jax.numpy as jnp
from jax import lax
from jax.experimental import pallas as pl
from jax.experimental.pallas import tpu as pltpu
from jax.sharding import PartitionSpec as P

SWEEPS = 5

stiff_floor = 0.01
mass_shift = 0.1
spectrum_low = 0.05
spectrum_high = 2.0
moment_decay = 0.8
step_size = 0.1
volume_pull = 0.5
volume_target = 0.4
density_floor = 0.001

SOURCE = SWEEPS
DESIGN = SWEEPS + 1
SENSE = SWEEPS + 2


def chebyshev_factors():
    centre = 0.5 * (spectrum_high + spectrum_low)
    half_width = 0.5 * (spectrum_high - spectrum_low)
    ratio_one = centre / half_width
    previous = 1.0 / ratio_one
    factors = []
    for _ in range(SWEEPS - 1):
        current = 1.0 / (2.0 * ratio_one - previous)
        factors.append((current * previous, 2.0 * current / half_width))
        previous = current
    return 1.0 / centre, factors


def shifted(plane):
    size_y, size_z = plane.shape
    return (
        pltpu.roll(plane, 1, 0),
        pltpu.roll(plane, size_y - 1, 0),
        pltpu.roll(plane, 1, 1),
        pltpu.roll(plane, size_z - 1, 1),
    )


def inner_masks(shape):
    along_y = lax.broadcasted_iota(jnp.int32, shape, 0)
    along_z = lax.broadcasted_iota(jnp.int32, shape, 1)
    return (along_y > 0, along_y < shape[0] - 1, along_z > 0, along_z < shape[1] - 1)


def beside_planes(plane, masks):
    return tuple(jnp.where(mask, moved, 0.0) for mask, moved in zip(masks, shifted(plane)))


def edge_planes(masks):
    edges = sum((1.0 - mask.astype(jnp.float32)) for mask in masks)
    return 1.0 / (8.0 - edges), 1.0 / (7.0 - edges)


def stiffness_of(design):
    return stiff_floor + (1.0 - stiff_floor) * (design * design * design)


class Kept:
    def __init__(self):
        self.places = {}

    def put(self, key, ref, index, value):
        ref[index] = value
        self.places[key] = (ref, index)

    def get(self, key):
        ref, index = self.places[key]
        return ref[index]


def weight_row(q, is_free, stiff, weight, inverse, weight_to, inverse_to, place, masks):
    here, below, above = stiff[q + 1], stiff[q], stiff[q + 2]
    around = (below, above) + beside_planes(here, masks)
    total = around[0]
    for plane in around[1:]:
        total = total + plane
    diagonal = (3.0 + mass_shift) * here + 0.5 * total
    scale = jnp.where(is_free, pl.reciprocal(diagonal), 0.0)
    inverse.put(q, inverse_to, place, scale)
    half = 0.5 * scale
    weight.put((0, q), weight_to, (0, place), half * (here + below))
    weight.put((1, q), weight_to, (1, place), half * (here + above))
    for j in range(4):
        weight.put((2 + j, q), weight_to, (2 + j, place), jnp.where(masks[j], half * (here + around[2 + j]), 0.0))


def sweep_row(k, q, loads, weight, resid, steps, resid_to, steps_to, shown_to, shown, first=0, first_shown=SWEEPS - 1):
    _, factors = chebyshev_factors()
    keep, gain = factors[k]
    last = k == len(factors) - 1
    faces = [weight.get((j, q)) for j in range(6)]
    for l in range(loads):
        here = steps.get((k, l, q))
        total = faces[0] * steps.get((k, l, q - 1)) + faces[1] * steps.get((k, l, q + 1))
        for face, moved in zip(faces[2:], shifted(here)):
            total = total + face * moved
        left = resid.get((l, q)) - here + total
        step = keep * here + gain * left
        if last:
            for earlier in range(k + 1):
                step = step + steps.get((earlier, l, q))
            shown.put((l, q), shown_to, (l, q - first_shown), step)
        else:
            resid.put((l, q), resid_to, (l, q - first), left)
            steps.put((k + 1, l, q), steps_to, (k + 1, l, q - first), step)


def energy_row(i, loads, design, shown, masks):
    q = i + SOURCE
    energy = None
    for l in range(loads):
        here = shown.get((l, q))
        around = (shown.get((l, q - 1)), shown.get((l, q + 1))) + beside_planes(here, masks)
        spread = None
        for plane in around:
            gap = here - plane
            spread = gap * gap if spread is None else spread + gap * gap
        part = mass_shift * (here * here) + 0.25 * spread
        energy = part if energy is None else energy + part
    return (-3.0 * (1.0 - stiff_floor)) * (design * design) * energy


def fold(plane):
    return jnp.sum(plane.reshape(plane.shape[0] // 8, 8, plane.shape[1]), axis=0)


def filter_total(cells, sense, is_first, is_last, masks):
    inside, outer = edge_planes(masks)
    usual = 4.0 * inside + sum(beside_planes(inside, masks))
    at_end = 2.0 * outer + inside + sum(beside_planes(outer, masks))
    zero = jnp.zeros_like(inside)
    total = sense[0]
    for i in range(1, cells):
        total = total + sense[i]
    ends = jnp.where(is_first, sense[0], zero) + jnp.where(is_last, sense[cells - 1], zero)
    nexts = jnp.where(is_first, sense[1], zero) + jnp.where(is_last, sense[cells - 2], zero)
    return -fold(total * usual + ends * (at_end - usual) + nexts * (outer - inside))


def fold_rows(cells, ref):
    total = jnp.abs(ref[0])
    for i in range(1, cells):
        total = total + jnp.abs(ref[i])
    return fold(total)


def place_of():
    brick = lax.axis_index("brick")
    return lax.axis_index("load") % 2 == 0, brick == 0, brick == lax.axis_size("brick") - 1


def prepare_kernel(cells, density, passive, support, payload_ref, design_rows, kind_rows, hold_rows, sems):
    even, _, _ = place_of()
    start = jnp.where(even, cells - DESIGN, 0)
    start_mask = jnp.where(even, cells - SOURCE, 0)
    copies = [
        pltpu.make_async_copy(source, target, sems.at[i])
        for i, (source, target) in enumerate((
            (density.at[pl.ds(start, DESIGN)], design_rows),
            (passive.at[pl.ds(start, DESIGN)], kind_rows),
            (support.at[pl.ds(start_mask, SOURCE)], hold_rows),
        ))
    ]
    for copy in copies:
        copy.start()
    for copy in copies:
        copy.wait()
    for i in range(DESIGN):
        payload_ref[i] = passive_apply(design_rows[i], kind_rows[i])
    for i in range(SOURCE):
        payload_ref[DESIGN + i] = (1 - hold_rows[i]).astype(jnp.float32)


def edges_kernel(cells, force, upper_ref, lower_ref, sems):
    copies = [
        pltpu.make_async_copy(force.at[:, pl.ds(cells - SOURCE, SOURCE)], upper_ref, sems.at[0]),
        pltpu.make_async_copy(force.at[:, pl.ds(0, SOURCE)], lower_ref, sems.at[1]),
    ]
    for copy in copies:
        copy.start()
    for copy in copies:
        copy.wait()


def points_kernel(cells, loads, nodes, forces, force_ref, base_far, base_ref, sems):
    rows = cells + 2 * SOURCE
    size_y, size_z = base_ref.shape[2:]
    zero = jnp.zeros((size_y, size_z), jnp.float32)
    for l in range(loads):
        for q in range(rows):
            own = SOURCE <= q < SOURCE + cells
            base_ref[l, q] = force_ref[l, q - SOURCE] if own else zero
    first = (lax.axis_index("brick") * cells - SOURCE) * size_y * size_z
    along_z = lax.broadcasted_iota(jnp.int32, (1, size_z), 1)
    for l in range(loads):

        def one_point(p, carry, l=l):
            cell = nodes[l, p] - first

            @pl.when((cell >= 0) & (cell < rows * size_y * size_z))
            def _():
                line, z = cell // size_z, cell % size_z
                q, y = line // size_y, line % size_y
                spot = (l, q, pl.ds(y, 1), slice(None))
                base_ref[spot] = base_ref[spot] + jnp.where(along_z == z, forces[l, p], 0.0)

            return carry

        lax.fori_loop(0, nodes.shape[1], one_point, 0)
    copy = pltpu.make_async_copy(base_ref, base_far, sems.at[0])
    copy.start()
    copy.wait()


def base_row(l, q, cells, base_in, force_lo, force_hi):
    if q < SOURCE:
        return base_in[l, q] + force_lo[l, q]
    if q >= SOURCE + cells:
        return base_in[l, q] + force_hi[l, q - SOURCE - cells]
    return base_in[l, q]


def inner_steps(cells, margin):
    return [range(SOURCE + margin + k, SOURCE + cells - margin - k) for k in range(SWEEPS)]


def outer_place(q, cells):
    return q if q <= SOURCE else q - (cells - 2)


def start_row(q, base, design, self_weight, inverse, resid, steps, resid_to, steps_to, first):
    first_scale, _ = chebyshev_factors()
    for l, one in enumerate(base):
        left = inverse.get(q) * (one + self_weight[l] * design)
        resid.put((l, q), resid_to, (l, q - first), left)
        steps.put((0, l, q), steps_to, (0, l, q - first), first_scale * left)


def inner_places(cells, loads, near, early):
    weight, inverse, resid, steps, shown = Kept(), Kept(), Kept(), Kept(), Kept()
    rows = cells + 2 * SOURCE
    near_rows, early_rows = inner_steps(cells, 1), inner_steps(cells, 0)
    for q in range(rows):
        inside = q in near_rows[0]
        if not inside and early is None:
            continue
        place = q - SOURCE if inside else outer_place(q, cells)
        weights, inverses = (near if inside else early)[:2]
        inverse.places[q] = (inverses, place)
        for j in range(6):
            weight.places[(j, q)] = (weights, (j, place))
    for refs, ranges in ((early, early_rows), (near, near_rows)):
        if refs is None:
            continue
        for l in range(loads):
            for k in range(SWEEPS - 1):
                for q in ranges[k]:
                    steps.places[(k, l, q)] = (refs[3], (k, l, q - SOURCE))
            for q in ranges[SWEEPS - 1]:
                shown.places[(l, q)] = (refs[4], (l, q - SOURCE - (SWEEPS - 1)))
    for l in range(loads):
        for q in early_rows[0]:
            depth = min(q - SOURCE, SOURCE + cells - 1 - q)
            at_early = early is not None and depth < SWEEPS - 1
            if at_early or q in near_rows[0]:
                resid.places[(l, q)] = ((early if at_early else near)[2], (l, q - SOURCE))
    return weight, inverse, resid, steps, shown


def own_kernel(cells, loads, self_weight, density, passive, support, base_ref,
               design_own, stiff, weight_ref, inverse_ref, resid_ref, steps_ref, shown_ref, stiff_wide):
    masks = inner_masks(density.shape[1:])
    weight, inverse, resid, steps, shown = Kept(), Kept(), Kept(), Kept(), Kept()
    for i in range(cells):
        design = passive_apply(density[i], passive[i])
        stiffness = stiffness_of(design)
        stiff[i] = stiffness
        stiff_wide[DESIGN + i] = stiffness
        design_own[i] = jnp.where(support[i] == 0, design, -design)
    inner = inner_steps(cells, 1)
    for q in inner[0]:
        i = q - SOURCE
        weight_row(q, support[i] == 0, stiff_wide, weight, inverse, weight_ref, inverse_ref, i, masks)
        base = [base_ref[l, q] for l in range(loads)]
        start_row(q, base, jnp.abs(design_own[i]), self_weight, inverse, resid, steps, resid_ref, steps_ref, SOURCE)
    for k in range(SWEEPS - 1):
        for q in inner[k + 1]:
            sweep_row(
                k, q, loads, weight, resid, steps, resid_ref, steps_ref, shown_ref, shown,
                SOURCE, SOURCE + SWEEPS - 1,
            )


def early_kernel(cells, loads, self_weight, base_ref, pair_a, pair_b, pair_c, design_own, stiff_own,
                 near_weight, near_inverse, near_resid, near_steps, near_shown,
                 design_wide, weight_ref, inverse_ref, resid_ref, steps_ref, shown_ref, stiff):
    even, is_first, is_last = place_of()
    shape = design_own.shape[1:]
    masks = inner_masks(shape)
    zero = jnp.zeros(shape, jnp.float32)
    weight, inverse, resid, steps, shown = inner_places(
        cells, loads, (near_weight, near_inverse, near_resid, near_steps, near_shown), None
    )
    for i in range(DESIGN):
        low = jnp.where(even, pair_a[i], pair_b[i])
        high = jnp.where(even, pair_b[i], pair_a[i])
        stiff[i] = jnp.where(is_first, zero, stiffness_of(low))
        stiff[DESIGN + cells + i] = jnp.where(is_last, zero, stiffness_of(high))
        below, above = i - 1, i
        if below >= 0:
            free = jnp.where(even, pair_a[DESIGN + below], pair_c[below])
            low = jnp.where((free > 0.5) & jnp.logical_not(is_first), low, -low)
        else:
            low = -low
        if above < SOURCE:
            free = jnp.where(even, pair_c[above], pair_a[DESIGN + above])
            high = jnp.where((free > 0.5) & jnp.logical_not(is_last), high, -high)
        else:
            high = -high
        design_wide[i] = low
        design_wide[DESIGN + cells + i] = high
    for i in range(cells):
        design_wide[DESIGN + i] = design_own[i]
        stiff[DESIGN + i] = stiff_own[i]
    near, inner = inner_steps(cells, 1), inner_steps(cells, 0)
    for q in range(cells + 2 * SOURCE):
        if q not in near[0]:
            weight_row(
                q, design_wide[q + 1] > 0.0, stiff, weight, inverse, weight_ref, inverse_ref, outer_place(q, cells), masks
            )
    for q in inner[0]:
        if q not in near[0]:
            base = [base_ref[l, q] for l in range(loads)]
            design = jnp.abs(design_wide[q + 1])
            start_row(q, base, design, self_weight, inverse, resid, steps, resid_ref, steps_ref, SOURCE)
    for k in range(SWEEPS - 1):
        for q in inner[k + 1]:
            if q not in near[k + 1]:
                sweep_row(
                    k, q, loads, weight, resid, steps, resid_ref, steps_ref, shown_ref, shown,
                    SOURCE, SOURCE + SWEEPS - 1,
                )


def first_kernel(cells, loads, self_weight, force_lo, force_hi, base_in, design_wide,
                 near_weight, near_inverse, near_resid, near_steps, near_shown,
                 early_weight, early_inverse, early_resid, early_steps, early_shown,
                 lo_far, hi_far, sense_ref, outer, rest, tile_ref,
                 resid_ref, steps_ref, shown_ref, sems):
    copies = [
        pltpu.make_async_copy(source, target, sems.at[i])
        for i, (source, target) in enumerate(((force_lo, lo_far), (force_hi, hi_far)))
    ]
    for copy in copies:
        copy.start()
    even, is_first, is_last = place_of()
    shape = design_wide.shape[1:]
    masks = inner_masks(shape)
    rows = cells + 2 * SOURCE
    weight, inverse, resid, steps, shown = inner_places(
        cells, loads, (near_weight, near_inverse, near_resid, near_steps, near_shown),
        (early_weight, early_inverse, early_resid, early_steps, early_shown),
    )
    inner = inner_steps(cells, 0)
    for q in range(rows):
        if q not in inner[0]:
            base = [base_row(l, q, cells, base_in, force_lo, force_hi) for l in range(loads)]
            design = jnp.abs(design_wide[q + 1])
            start_row(q, base, design, self_weight, inverse, resid, steps, resid_ref, steps_ref, 0)
    for k in range(SWEEPS - 1):
        for q in range(k + 1, rows - k - 1):
            if q not in inner[k + 1]:
                sweep_row(k, q, loads, weight, resid, steps, resid_ref, steps_ref, shown_ref, shown)
    for i in range(cells):
        sense_ref[i] = energy_row(i, loads, design_wide[DESIGN + i], shown, masks)
    cut_rows(cells, even, sense_ref, outer, rest)
    own = design_wide.at[pl.ds(DESIGN, cells)]
    spread_totals(tile_ref, filter_total(cells, sense_ref, is_first, is_last, masks), fold_rows(cells, own))
    for copy in copies:
        copy.wait()


def cut_rows(cells, even, sense, outer, rest):
    width = outer.shape[0]
    for i in range(width):
        outer[i] = jnp.where(even, sense[i], sense[cells - width + i])
    for i in range(cells - width):
        rest[i] = jnp.where(even, sense[width + i], sense[i])


def edge_kernel(cells, sense, outer, edge):
    even, _, _ = place_of()
    width = outer.shape[0]
    for i in range(width):
        edge[i] = jnp.where(even, sense[cells - width + i], sense[i]) + outer[i]


def whole_row(i, cells, even, sense, edge, rest):
    width = edge.shape[0]
    if_even = sense[i] + rest[i] if i < cells - width else edge[i - (cells - width)]
    if_odd = edge[i] if i < width else sense[i] + rest[i - width]
    return jnp.where(even, if_even, if_odd)


def moment_kernel(cells, sense, edge, rest, pair_a, pair_b, moment_ref, sense_wide):
    even, is_first, is_last = place_of()
    shape = edge.shape[1:]
    masks = inner_masks(shape)
    zero = jnp.zeros(shape, jnp.float32)
    for i in range(SENSE):
        low = jnp.where(even, pair_a[i], pair_b[i])
        high = jnp.where(even, pair_b[i], pair_a[i])
        sense_wide[i] = jnp.where(is_first, zero, low)
        sense_wide[SENSE + cells + i] = jnp.where(is_last, zero, high)
    for i in range(cells):
        sense_wide[SENSE + i] = whole_row(i, cells, even, sense, edge, rest)
    inside, at_ends = edge_planes(masks)
    for r in range(cells + 2 * DESIGN):
        at_end = (is_first & (r == DESIGN)) | (is_last & (r == DESIGN + cells - 1))
        moment_ref[r] = filtered_row(r, sense_wide, masks) * jnp.where(at_end, at_ends, inside)


def filtered_row(r, sense_wide, masks):
    here = sense_wide[r + 1]
    total = 2.0 * here + sense_wide[r] + sense_wide[r + 2]
    for plane in beside_planes(here, masks):
        total = total + plane
    return total


def spread_totals(tile_ref, abs_tile, density_tile):
    row = jnp.concatenate([jnp.sum(tile, axis=0, keepdims=True) for tile in (abs_tile, density_tile)], axis=1)
    tile_ref[...] = jnp.broadcast_to(row[None], tile_ref.shape)


def totals_kernel(total_cells, share, decay, tile_in, before, total_ref):
    half = tile_in.shape[2] // 2
    totals = jnp.sum(tile_in[...], axis=0)
    abs_total = jnp.sum(totals[:, :half], keepdims=True)
    if decay:
        abs_total = abs_total + decay * before[2:3, :1]
    density_total = jnp.sum(totals[:, half:], keepdims=True) * share
    rate = step_size / (abs_total / total_cells + 1e-6)
    pull = volume_pull * (density_total / total_cells - volume_target)
    row = lax.broadcasted_iota(jnp.int32, total_ref.shape, 0)
    total_ref[...] = jnp.where(row == 0, rate, jnp.where(row == 1, pull, abs_total))


def second_kernel(cells, loads, self_weight, step_ref, moment_wide,
                  design_wide, base_far, lo_far, hi_far,
                  shown_ref, design_out, sense_ref, outer, rest, tile_ref,
                  stiff, weight_ref, inverse_ref, resid_ref, steps_ref, shown_to, design_new,
                  base_in, force_lo, force_hi, sems):
    copies = [
        pltpu.make_async_copy(source, target, sems.at[i])
        for i, (source, target) in enumerate(((base_far, base_in), (lo_far, force_lo), (hi_far, force_hi)))
    ]
    for copy in copies:
        copy.start()
    even, is_first, is_last = place_of()
    shape = moment_wide.shape[1:]
    masks = inner_masks(shape)
    wide = cells + 2 * DESIGN
    rows = cells + 2 * SOURCE
    zero = jnp.zeros(shape, jnp.float32)
    rate, pull = step_ref[0:1, :], step_ref[1:2, :]
    for r in range(wide):
        signed = design_wide[r]
        before = jnp.abs(signed)
        moved = jnp.clip(before - rate * moment_wide[r] - pull, density_floor, 1.0)
        fixed = (before == density_floor) | (before == 1.0)
        design = jnp.where(fixed, before, moved)
        design_new[r] = design
        stiffness = stiffness_of(design)
        if r < DESIGN:
            stiff[r] = jnp.where(is_first, zero, stiffness)
        elif r >= DESIGN + cells:
            stiff[r] = jnp.where(is_last, zero, stiffness)
        else:
            stiff[r] = stiffness
    own_rows = pltpu.make_async_copy(design_new.at[pl.ds(DESIGN, cells)], design_out, sems.at[len(copies) + loads])
    own_rows.start()
    weight, inverse, resid, steps, shown = Kept(), Kept(), Kept(), Kept(), Kept()
    for q in range(rows):
        weight_row(q, design_wide[q + 1] > 0.0, stiff, weight, inverse, weight_ref, inverse_ref, q, masks)
    for copy in copies:
        copy.wait()
    for q in range(rows):
        base = [base_row(l, q, cells, base_in, force_lo, force_hi) for l in range(loads)]
        start_row(q, base, design_new[q + 1], self_weight, inverse, resid, steps, resid_ref, steps_ref, 0)
    for k in range(SWEEPS - 1):
        for q in range(k + 1, rows - k - 1):
            sweep_row(k, q, loads, weight, resid, steps, resid_ref, steps_ref, shown_to, shown)
    results = [
        pltpu.make_async_copy(shown_to.at[l, pl.ds(1, cells)], shown_ref.at[l], sems.at[len(copies) + l])
        for l in range(loads)
    ]
    for copy in results:
        copy.start()
    for i in range(cells):
        sense_ref[i] = energy_row(i, loads, design_new[DESIGN + i], shown, masks)
    cut_rows(cells, even, sense_ref, outer, rest)
    own = design_new.at[pl.ds(DESIGN, cells)]
    spread_totals(tile_ref, filter_total(cells, sense_ref, is_first, is_last, masks), fold_rows(cells, own))
    for copy in results + [own_rows]:
        copy.wait()


def last_moment_kernel(cells, slab, sense, edge, rest, pair_a, pair_b, moment_wide, design_far, passive_far,
                       momentum_ref, kept_ref, before_ref, least_ref, most_ref, sense_wide, momentum_all,
                       kinds, sems):
    even, is_first, is_last = place_of()
    window = pl.ds(pl.multiple_of(lax.axis_index("load") * slab, 8), slab)
    copies = [
        pltpu.make_async_copy(design_far.at[:, window, :], before_ref, sems.at[1]),
        pltpu.make_async_copy(passive_far.at[:, window, :], kinds, sems.at[2]),
    ]
    for copy in copies:
        copy.start()
    shape = edge.shape[1:]
    masks = inner_masks(shape)
    zero = jnp.zeros(shape, jnp.float32)
    sense_wide[0] = jnp.where(is_first, zero, jnp.where(even, pair_a[0], pair_b[0]))
    sense_wide[cells + 1] = jnp.where(is_last, zero, jnp.where(even, pair_b[0], pair_a[0]))
    for i in range(cells):
        sense_wide[i + 1] = whole_row(i, cells, even, sense, edge, rest)
    inside, at_ends = edge_planes(masks)
    for i in range(cells):
        scale = inside
        if i == 0:
            scale = jnp.where(is_first, at_ends, inside)
        elif i == cells - 1:
            scale = jnp.where(is_last, at_ends, inside)
        momentum_all[i] = moment_decay * moment_wide[DESIGN + i] + filtered_row(i, sense_wide, masks) * scale
        momentum = momentum_all[i, window, :]
        kept_ref[i] = momentum
    copy = pltpu.make_async_copy(kept_ref, momentum_ref, sems.at[0])
    copy.start()
    for other in copies:
        other.wait()
    for i in range(cells):
        kind = kinds[i]
        least_ref[i] = jnp.where(kind == 2, 1.0, density_floor)
        most_ref[i] = jnp.where(kind == 1, density_floor, 1.0)
    copy.wait()


def last_kernel(cells, step_ref, momentum_ref, before_ref, least_ref, most_ref, design_ref, design_near, sems):
    rate, pull = step_ref[0:1, :], step_ref[1:2, :]
    for i in range(cells):
        moved = before_ref[i] - rate * momentum_ref[i] - pull
        design_near[i] = jnp.minimum(jnp.maximum(moved, least_ref[i]), most_ref[i])
    copy = pltpu.make_async_copy(design_near, design_ref, sems.at[0])
    copy.start()
    copy.wait()


VMEM = pl.BlockSpec(memory_space=pltpu.VMEM)
SMEM = pl.BlockSpec(memory_space=pltpu.SMEM)


def on_core(kernel, operands, scalars, outs, scratch, cost=0, limit=4, far=0, far_outs=0):
    anywhere = pl.BlockSpec(memory_space=pl.ANY)
    operands = [
        pltpu.with_memory_space_constraint(operand, pltpu.VMEM)
        if scalars <= i < len(operands) - far else pltpu.with_memory_space_constraint(operand, pltpu.HBM) if i >= len(operands) - far else operand
        for i, operand in enumerate(operands)
    ]
    return pl.pallas_call(
        kernel,
        out_shape=[
            pltpu.HBM(shape, jnp.float32) if i < far_outs else pltpu.VMEM(shape, jnp.float32)
            for i, shape in enumerate(outs)
        ],
        in_specs=[SMEM] * scalars + [VMEM] * (len(operands) - scalars - far) + [anywhere] * far,
        out_specs=[anywhere] * far_outs + [VMEM] * (len(outs) - far_outs),
        scratch_shapes=[pltpu.VMEM(item, jnp.float32) if isinstance(item, tuple) else item for item in scratch],
        cost_estimate=pl.CostEstimate(flops=cost, bytes_accessed=cost, transcendentals=0) if cost else None,
        compiler_params=pltpu.CompilerParams(vmem_limit_bytes=limit * 1024 * 1024),
    )(*operands)


def passive_apply(design, passive):
    return jnp.where(passive == 1, density_floor, jnp.where(passive == 2, 1.0, design))


def swap(value, axis, bit):
    count = lax.axis_size(axis)
    return lax.ppermute(value, axis, [(i, i ^ bit) for i in range(count)])


def along(value, step):
    count = lax.axis_size("brick")
    pairs = [(i, i + step) for i in range(count) if 0 <= i + step < count]
    return lax.ppermute(value, "brick", pairs)


def both_ways(value):
    count, loads = lax.axis_size("brick"), lax.axis_size("load")
    pairs = []
    for l in range(loads):
        step = 1 if l % 2 == 0 else -1
        pairs += [(l * count + i, l * count + i + step) for i in range(count) if 0 <= i + step < count]
    return lax.ppermute(value, ("load", "brick"), pairs)


def bits_of(count):
    return [1 << k for k in range(count.bit_length() - 1)]


def sum_over(value, axis):
    for bit in bits_of(lax.axis_size(axis)):
        value = value + swap(value, axis, bit)
    return value


def after(value, other):
    return lax.optimization_barrier((value, other))[0]


def meet(parts, tiles, filtered, totals):
    total = totals(lax.all_to_all(tiles, ("load", "brick"), 0, 0, tiled=True))
    for bit in bits_of(lax.axis_size("load"))[1:]:
        parts = [part + swap(part, "load", bit) for part in parts]
    sense, outer, rest = parts
    outer = swap(outer, "load", 1)
    (edge,) = on_core(functools.partial(edge_kernel, sense.shape[0]), (sense, outer), 0, [outer.shape], [])
    pair_a = both_ways(edge)
    rest = swap(rest, "load", 1)
    pair_b = swap(pair_a, "load", 1)
    return filtered(sense, edge, rest, pair_a, pair_b), total


def body(density, passive, support, load_nodes, load_force, self_weight, body_force):
    cells, size_y, size_z = density.shape
    loads = body_force.shape[0]
    load_count, bricks = lax.axis_size("load"), lax.axis_size("brick")
    slab = size_y // load_count
    total_cells = float(cells * bricks * size_y * size_z)
    share = 1.0 / load_count
    plane = (size_y, size_z)
    wide, rows = cells + 2 * DESIGN, cells + 2 * SOURCE
    tile = (load_count * bricks, 1, 2 * size_z)
    shown_shape = (loads, cells + 2) + plane
    resid_shape = (loads, rows) + plane
    steps_shape = (SWEEPS - 1, loads, rows) + plane

    def parts_of(width):
        return [(count,) + plane for count in (cells, width, cells - width)]

    (payload,) = on_core(
        functools.partial(prepare_kernel, cells),
        (density, passive, support),
        0,
        [(DESIGN + SOURCE,) + plane],
        [pltpu.VMEM((DESIGN,) + plane, jnp.float32), pltpu.VMEM((DESIGN,) + plane, jnp.int32),
         pltpu.VMEM((SOURCE,) + plane, jnp.int32), pltpu.SemaphoreType.DMA((3,))],
        far=3,
    )
    upper, lower = on_core(
        functools.partial(edges_kernel, cells),
        (after(body_force, payload),),
        0,
        [(loads, SOURCE) + plane, (loads, SOURCE) + plane],
        [pltpu.SemaphoreType.DMA((2,))],
        far=1,
    )
    pair_a = both_ways(payload)
    force_lo = along(upper, 1)
    force_hi = along(lower, -1)
    base_far, base = on_core(
        functools.partial(points_kernel, cells, loads),
        (load_nodes, load_force, after(body_force, (upper, lower))),
        2,
        [resid_shape, resid_shape],
        [pltpu.SemaphoreType.DMA((1,))],
        cost=1,
        far_outs=1,
    )
    inner_shapes = [(loads, cells) + plane, (SWEEPS - 1, loads, cells) + plane]
    design_own, stiff_own, *near = on_core(
        functools.partial(own_kernel, cells, loads),
        (self_weight, density, passive, support, base),
        1,
        [(cells,) + plane, (cells,) + plane, (6, cells) + plane, (cells,) + plane]
        + inner_shapes + [(loads, cells - 2 * (SWEEPS - 1)) + plane],
        [(wide,) + plane],
        cost=1,
    )
    pair_a = after(pair_a, stiff_own)
    pair_b = swap(pair_a[:DESIGN], "load", 1)
    pair_c = swap(pair_a[DESIGN:], "load", 1)
    design_wide, *early = on_core(
        functools.partial(early_kernel, cells, loads),
        (self_weight, base, pair_a, pair_b, pair_c, design_own, stiff_own, *near),
        1,
        [(wide,) + plane, (6, 2 * SOURCE + 2) + plane, (2 * SOURCE + 2,) + plane]
        + inner_shapes + [(loads, cells - 2 * (SWEEPS - 1)) + plane],
        [(wide,) + plane],
        cost=1,
    )
    lo_far, hi_far, *parts, tiles = on_core(
        functools.partial(first_kernel, cells, loads),
        (self_weight, force_lo, force_hi, base, design_wide, *near, *early),
        1,
        [(loads, SOURCE) + plane] * 2 + parts_of(SENSE) + [tile],
        [resid_shape, steps_shape, shown_shape, pltpu.SemaphoreType.DMA((2,))],
        far_outs=2,
    )
    def totals(decay, before):
        return lambda tiles: on_core(
            functools.partial(totals_kernel, total_cells, share, decay),
            (tiles, before),
            0,
            [(8, size_z)],
            [],
            cost=2000000000,
        )[0]

    (moment_wide,), step_first = meet(
        parts, tiles,
        lambda *sensed: on_core(
            functools.partial(moment_kernel, cells),
            sensed,
            0,
            [(wide,) + plane],
            [(cells + 2 * SENSE,) + plane],
        ),
        totals(0.0, tiles),
    )
    shown, design, *parts, tiles = on_core(
        functools.partial(second_kernel, cells, loads),
        (self_weight, step_first, moment_wide, design_wide, base_far, lo_far, hi_far),
        1,
        [(loads, cells) + plane, (cells,) + plane] + parts_of(1) + [tile],
        [(wide,) + plane, (6, rows) + plane, (rows,) + plane, resid_shape, steps_shape, shown_shape, (wide,) + plane,
         resid_shape, (loads, SOURCE) + plane, (loads, SOURCE) + plane,
         pltpu.SemaphoreType.DMA((4 + loads,))],
        limit=14,
        far=3,
        far_outs=2,
    )
    last_ones, step_last = meet(
        parts, tiles,
        lambda *sensed: on_core(
            functools.partial(last_moment_kernel, cells, slab),
            sensed + (moment_wide, design, passive),
            0,
            [(cells, slab, size_z)] * 5,
            [(cells + 2,) + plane, (cells,) + plane,
             pltpu.VMEM((cells, slab, size_z), jnp.int32), pltpu.SemaphoreType.DMA((3,))],
            far=2,
            far_outs=1,
        ),
        totals(moment_decay, step_first),
    )
    (design,) = on_core(
        functools.partial(last_kernel, cells),
        (step_last,) + tuple(last_ones[1:]),
        0,
        [(cells, slab, size_z)],
        [(cells, slab, size_z), pltpu.SemaphoreType.DMA((1,))],
        far_outs=1,
    )
    return design, last_ones[0], shown


def solution(mesh):
    placed = (
        P("brick", None, None),
        P("brick", None, None),
        P("brick", None, None),
        P("load", None),
        P("load", None),
        P("load"),
        P("load", "brick", None, None),
    )
    return jax.shard_map(
        body,
        mesh=mesh,
        in_specs=placed,
        out_specs=(
            P("brick", "load", None),
            P("brick", "load", None),
            P("load", "brick", None, None),
        ),
        check_vma=False,
    )
```
